32 devices in a mesh: section: 2 (over x), mp: 2 (over core), dp: 8 (over z, y).
Axes of the slice: x: 2, y: 2, z: 4, core: 2. Of those that a mesh axis runs over, the one named last changes fastest.
Arguments:
- tokens: bfloat16 [16, 1024, 768], P('dp', ('section', 'mp')), may hold values from -6 to 6
- grad_out: bfloat16 [16, 1024, 768], P('dp', ('section', 'mp')), may hold values from -6 to 6
- attention_in: bfloat16 [2, 768, 3, 768], P('section', None, None, 'mp'), may hold values from -0.21875 to 0.21875
- attention_bias: float32 [2, 2, 768], P('section', None, 'mp'), may hold values from -0.75 to 0.75
- attention_out: bfloat16 [2, 768, 768], P('section', 'mp'), may hold values from -3.5 to 3.5
- up_weight: bfloat16 [2, 768, 3072], P('section', None, 'mp'), may hold values from -0.21875 to 0.21875
- up_bias: float32 [2, 3072], P('section', 'mp'), may hold values from -4 to 4
- down_weight: bfloat16 [2, 3072, 768], P('section', 'mp'), may hold values from -0.109375 to 0.109375
- norm_gains: float32 [2, 2, 768], P('section'), may hold values from 0.5 to 1.5
- layer_biases: float32 [2, 4, 768], P('section'), may hold values from -4 to 4
- block_counts: int32 [16], P('dp'), may hold values from 2 to 3
- lengths: int32 [16], P('dp'), may hold values from 512 to 1024
- head_shifts: int32 [2, 12], P('section', 'mp'), may hold values from 0 to 2
Outputs:
- layer_out: bfloat16 [16, 1024, 768], P('dp', ('section', 'mp'))
- grad_tokens: bfloat16 [16, 1024, 768], P('dp', ('section', 'mp'))
- grad_attention_in: float32 [2, 768, 3, 768], P('section', None, None, 'mp')
- grad_attention_bias: float32 [2, 2, 768], P('section', None, 'mp')
- grad_attention_out: float32 [2, 768, 768], P('section', 'mp')
- grad_up_weight: float32 [2, 768, 3072], P('section', None, 'mp')
- grad_up_bias: float32 [2, 3072], P('section', 'mp')
- grad_down_weight: float32 [2, 3072, 768], P('section', 'mp')
- grad_norm_gains: float32 [2, 2, 768], P('section')
- grad_layer_biases: float32 [2, 4, 768], P('section')
The draws below stay inside these ranges and needn't reach their ends.
Inputs may be any that keep to these rules, and one draw needn't show every extreme that they name: The first lengths[s] positions of sequence s are live, the others padding.
All inputs are finite; a program needn't handle non-finite values.
Results may differ from the reference program's by a relative error of at most 0.03.
Values may be sent and summed in bfloat16 or wider, within the bound.
No kernel may reach another device: no remote copies, remote signals or barrier semaphores. Data moves between devices by JAX's collectives and lax.ppermute only.
A program may use at most 320 MiB of HBM per device.

```python
import jax
import jax.numpy as jnp
from jax import lax

D = 768
HEADS = 12
DH = 64
FF = 3072
LEN = 1024
LAYERS = 2
SEQS = 16


def place_ends(drawn, key, smallest, high):
    extent = drawn.shape
    spot = [jax.random.randint(jax.random.fold_in(key, axis), (), 0, extent[axis]) for axis in range(len(extent))]
    drawn = drawn.at[tuple(spot)].set(smallest)
    longest = extent.index(max(extent))
    spot[longest] = (spot[longest] + 1) % extent[longest]
    return drawn.at[tuple(spot)].set(high)


def block_levels(stream_key, shape, cuts, low, largest):
    def one(dim, blocks):
        draws = jax.random.uniform(jax.random.fold_in(jax.random.fold_in(stream_key, 6), dim), (blocks,), jnp.float32, low / len(cuts), largest / len(cuts))
        return jnp.repeat(jnp.exp(draws), shape[dim] // blocks).reshape((-1,) + (1,) * (len(shape) - dim - 1))

    loudness = one(*cuts[0])
    for cut in cuts[1:]:
        loudness = loudness * one(*cut)
    return loudness


def normal_values(key, extent, scale, limit, split=(), kind=jnp.bfloat16):
    loudness = block_levels(key, extent, split, -0.22, 0.18) if split else 1.0
    array = jax.random.normal(key, extent, jnp.float32) * scale * loudness
    return jnp.minimum(jnp.maximum(array, -limit), limit).astype(kind)


def setup_inputs(seed: int = 0) -> dict:
    keys = jax.random.split(jax.random.key(seed), 14)
    return {
        "tokens": normal_values(keys[0], (SEQS, LEN, D), 1.0, 6.0, ((0, 8), (1, 4))),
        "grad_out": normal_values(keys[1], (SEQS, LEN, D), 1.0, 6.0, ((0, 8), (1, 4))),
        "attention_in": normal_values(keys[2], (LAYERS, D, 3, D), D ** -0.5, 0.21875, ((0, 2), (3, 2))),
        "attention_bias": normal_values(keys[3], (LAYERS, 2, D), 0.05, 0.75, ((0, 2), (2, 2)), jnp.float32),
        "attention_out": normal_values(keys[4], (LAYERS, D, D), (max(D // 256, 1)) ** -0.5, 3.5, ((0, 2), (1, 2))),
        "up_weight": normal_values(keys[5], (LAYERS, D, FF), D ** -0.5, 0.21875, ((0, 2), (2, 2))),
        "up_bias": normal_values(keys[6], (LAYERS, FF), 0.3, 4.0, ((0, 2), (1, 2)), jnp.float32),
        "down_weight": normal_values(keys[7], (LAYERS, FF, D), FF ** -0.5, 0.109375, ((0, 2), (1, 2))),
        "norm_gains": jnp.clip(1.0 + 0.1 * jax.random.normal(keys[8], (LAYERS, 2, D), jnp.float32), 0.5, 1.5),
        "layer_biases": normal_values(keys[9], (LAYERS, 4, D), 0.3, 4.0, ((0, 2),), jnp.float32),
        "block_counts": place_ends(jax.random.randint(keys[10], (SEQS,), 2, 4), jax.random.fold_in(keys[10], 1), 2, 3).astype(jnp.int32),
        "lengths": place_ends(jax.random.randint(keys[11], (SEQS,), LEN // 2, LEN + 1), jax.random.fold_in(keys[11], 1), LEN // 2, LEN).astype(jnp.int32),
        "head_shifts": place_ends(jax.random.randint(keys[12], (LAYERS, HEADS), 0, 3), jax.random.fold_in(keys[12], 1), 0, 2).astype(jnp.int32),
    }


HIGH = lax.Precision.HIGHEST
EPS = 1e-05

@jax.custom_vjp
def low(v):
    return lax.optimization_barrier(v.astype(jnp.bfloat16)).astype(jnp.float32)

@jax.custom_vjp
def low_back(v):
    return v

def low_keep(v):
    return (low(v), None)

def low_pass(kept, grad):
    return (grad,)

def back_keep(v):
    return (v, None)

def back_low(kept, grad):
    return (low(grad),)
low.defvjp(low_keep, low_pass)
low_back.defvjp(back_keep, back_low)

def layer_norm(residual, gain_row, offset_row):
    row_mean = lax.optimization_barrier(jnp.mean(residual, axis=-1, keepdims=True))
    centred = residual - row_mean
    row_var = lax.optimization_barrier(jnp.mean(centred * centred, axis=-1, keepdims=True))
    return centred * lax.rsqrt(row_var + EPS) * gain_row + offset_row

def block_mask(block_count, length, shift_row):
    position = jnp.arange(LEN, dtype=jnp.int32)
    block_of = jnp.minimum(position * block_count // length, block_count - 1)
    target = (block_of[None, :] + shift_row[:, None]) % block_count
    return (block_of[None, None, :] == target[:, :, None]) & (position < length)[None, None, :]

def attend(queries, key_heads, values, allowed):
    scores = jnp.einsum('qhd,khd->hqk', queries, key_heads, precision=HIGH) * DH ** (-0.5)
    scores = low_back(jnp.where(allowed, scores, -1000000000.0))
    shifted = scores - lax.optimization_barrier(jnp.max(scores, axis=-1, keepdims=True))
    exponent = jnp.exp(shifted)
    weights = exponent / lax.optimization_barrier(jnp.sum(exponent, axis=-1, keepdims=True))
    return jnp.einsum('hqk,khd->qhd', low(weights), values, precision=HIGH)

def one_layer(hidden, attention_in, attention_bias, attention_out, up_weight, up_bias, down_weight, norm_gains, layer_biases, block_count, length, shift_row):
    bias_rows = jnp.stack([attention_bias[0], jnp.zeros_like(attention_bias[0]), attention_bias[1]])
    projected = jnp.einsum('ld,dcf->lcf', hidden, attention_in, precision=HIGH) + bias_rows
    projected = low(low_back(projected))
    per_head = projected.reshape(LEN, 3, HEADS, DH)
    allowed = block_mask(block_count, length, shift_row)
    mixed_heads = attend(per_head[:, 0], per_head[:, 1], per_head[:, 2], allowed).reshape(LEN, D)
    mixed_heads = low(low_back(mixed_heads))
    attention = low_back(jnp.dot(mixed_heads, attention_out, precision=HIGH))
    resid_one = hidden + attention + layer_biases[0]
    normed_one = layer_norm(resid_one, norm_gains[0], layer_biases[1])
    pre_act = low_back(jnp.dot(low(normed_one), up_weight, precision=HIGH) + up_bias)
    activation = low(jax.nn.gelu(pre_act, approximate=False))
    feed_out = low_back(jnp.dot(activation, down_weight, precision=HIGH))
    resid_two = normed_one + feed_out + layer_biases[2]
    return low(low_back(layer_norm(resid_two, norm_gains[1], layer_biases[3])))

def run_layers(arrays, block_counts, lengths, head_shifts):
    tokens, attention_in, attention_bias, attention_out, up_weight, up_bias, down_weight, norm_gains, layer_biases = arrays

    def one_sequence(sequence_item):
        hidden, block_count, length = sequence_item
        for layer_index in range(LAYERS):
            hidden = one_layer(hidden, attention_in[layer_index], attention_bias[layer_index], attention_out[layer_index], up_weight[layer_index], up_bias[layer_index], down_weight[layer_index], norm_gains[layer_index], layer_biases[layer_index], block_count, length, head_shifts[layer_index])
        return hidden
    return lax.map(jax.checkpoint(one_sequence), (tokens, block_counts, lengths))

def reference(tokens, grad_out, attention_in, attention_bias, attention_out, up_weight, up_bias, down_weight, norm_gains, layer_biases, block_counts, lengths, head_shifts):
    arrays = tuple((item.astype(jnp.float32) for item in (tokens, attention_in, attention_bias, attention_out, up_weight, up_bias, down_weight, norm_gains, layer_biases)))

    def forward(*floats):
        return run_layers(floats, block_counts, lengths, head_shifts)
    layer_out, pullback = jax.vjp(forward, *arrays)
    gradients = pullback(grad_out.astype(jnp.float32))
    return (layer_out.astype(jnp.bfloat16), gradients[0].astype(jnp.bfloat16), gradients[1], gradients[2], gradients[3], gradients[4], gradients[5], gradients[6], gradients[7], gradients[8])
```

```python
import math

import jax
import jax.numpy as jnp
from jax import lax
from jax.experimental import pallas as pl
from jax.experimental.pallas import tpu as pltpu
from jax.sharding import PartitionSpec as P

EPS = 1e-05
BF=jnp.bfloat16; F32=jnp.float32
NEG=-1e30
TQ=256
WINDOWS=(384,528)
UNROLL_F=3
UNROLL_B=2

def dotf(a,b):
    return lax.dot_general(a,b,(((1,),(0,)),((),())),preferred_element_type=F32)

def key_ext(th1,th2,n,rows):
    u=lax.broadcasted_iota(jnp.int32,(rows,128),0)
    col=lax.broadcasted_iota(jnp.int32,(rows,128),1)
    blk=(u>=th1).astype(jnp.int32)+(u>=th2).astype(jnp.int32)
    open_=(blk==col)&(u<n)
    one=jnp.where(col<8,1.0,0.0)
    return jnp.where(col<3,jnp.where(open_,0.0,NEG),one).astype(BF)

def query_rows(th1,th2,c,shift,r0):
    pos=r0+lax.broadcasted_iota(jnp.int32,(16,TQ),1)
    row=lax.broadcasted_iota(jnp.int32,(16,TQ),0)
    t=(pos>=th1).astype(jnp.int32)+(pos>=th2).astype(jnp.int32)+shift
    t=jnp.where(t>=c,t-c,t)
    return jnp.where(row==t,1.0,0.0), row

def split3(x):
    a=x.astype(BF).astype(F32); b=(x-a).astype(BF).astype(F32); cc=(x-a-b).astype(BF).astype(F32)
    return a,b,cc

def block_start(t,th1,th2):
    return jnp.where(t==0,0,jnp.where(t==1,th1,th2))

def tile_need(th1,th2,n,c,r0):
    last=r0+TQ-1
    whole=((r0<th1)==(last<th1))&((r0<th2)==(last<th2))
    end=jnp.minimum(th2,n)
    need=jnp.maximum(th1,jnp.maximum(end-(th1//16)*16,jnp.where(c==3,n-(th2//16)*16,0)))
    return jnp.where(whole,need,4096)

def head_base(th1,th2,c,shift,r0,limit):
    t=jnp.where(r0>=th1,1,0)+jnp.where(r0>=th2,1,0)+shift
    t=jnp.where(t>=c,t-c,t)
    ks=block_start(t,th1,th2)
    return pl.multiple_of(jnp.minimum((ks//16)*16,limit),16)

def run_window(need,length,body):
    prev=0
    for w in WINDOWS:
        if w>=length: continue
        @pl.when((need>prev)&(need<=w))
        def _(w=w):
            body(w)
        prev=w
    @pl.when(need>prev)
    def _():
        body(length)

def place(scr,pair_n,own_ref,peer_ref,own_off,peer_off,m,ext,half_pairs):
    for i in range(2):
        for who,(ref,off) in enumerate(((own_ref,own_off),(peer_ref,peer_off))):
            blk=2*i+jnp.where(m==who,0,1)
            dst=pl.ds(pl.multiple_of(blk*TQ,TQ),TQ)
            for p in range(pair_n):
                src=p if who==0 else (p+half_pairs)%pair_n
                scr[p,dst,0:128]=ref[i*TQ:(i+1)*TQ,off+src*128:off+(src+1)*128]
    for p in range(pair_n):
        scr[p,:,128:256]=ext

def attn_fwd_kernel(scal,q_ref,kv_ref,kvp_ref,mixed_ref,lse_ref,kb,vs):
    D=q_ref.shape[1]; pairs=D//128; length=kb.shape[1]
    th1=scal[0]; th2=scal[1]; n=scal[2]; c=scal[3]; m=scal[4]
    ext=key_ext(th1,th2,n,length)
    place(kb,pairs,kv_ref,kvp_ref,0,0,m,ext,pairs//2)
    for i in range(2):
        for who,ref in enumerate((kv_ref,kvp_ref)):
            blk=2*i+jnp.where(m==who,0,1)
            dst=pl.ds(pl.multiple_of(blk*TQ,TQ),TQ)
            for p in range(pairs):
                src=p if who==0 else (p+pairs//2)%pairs
                vs[p,dst,:]=ref[i*TQ:(i+1)*TQ,D+src*128:D+(src+1)*128]
    sub=lax.broadcasted_iota(jnp.int32,(128,TQ),0)
    for tile in range(2):
        r0=(2*tile+m)*TQ
        rows=slice(tile*TQ,(tile+1)*TQ)
        def body(w):
            @pl.loop(0,pairs,unroll=UNROLL_F if w<length else 1)
            def _(p):
                lanes=pl.ds(pl.multiple_of(p*128,128),128)
                qt=(q_ref[rows,lanes].astype(F32)*0.125).T
                outs=[]
                for hh in range(2):
                    shift=scal[8+2*p+hh]
                    oneh,_=query_rows(th1,th2,c,shift,r0)
                    qm=jnp.where((sub>=64)==(hh==1),qt,0.0).astype(BF)
                    rhs=jnp.concatenate([qm,oneh.astype(BF),jnp.zeros((112,TQ),BF)],axis=0)
                    win=pl.ds(head_base(th1,th2,c,shift,r0,length-w) if w<length else 0,w)
                    st=dotf(kb[p,win,:],rhs)
                    mx=jnp.max(st,axis=0,keepdims=True)
                    e=jnp.exp(st-mx).astype(BF)
                    vt=vs[p,win,:].T
                    vt=jnp.concatenate([vt[hh*64:(hh+1)*64],jnp.ones((16,w),BF)],axis=0)
                    o=dotf(vt,e)
                    l=o[64:65]
                    outs.append(o[:64]/l)
                    lse_ref[p,hh:hh+1,rows]=mx+jnp.log(l)
                mixed_ref[rows,lanes]=jnp.concatenate(outs,axis=0).T.astype(BF)
        run_window(tile_need(th1,th2,n,c,r0),length,body)

def attn_fwd(scal,q,kv,kvp):
    R,D=q.shape; pairs=D//128; L=2*R
    return pl.pallas_call(attn_fwd_kernel,
        out_shape=(jax.ShapeDtypeStruct((R,D),BF),jax.ShapeDtypeStruct((pairs,2,R),F32)),
        in_specs=[pl.BlockSpec(memory_space=pltpu.SMEM)]+[pl.BlockSpec(memory_space=pltpu.VMEM)]*3,
        out_specs=(pl.BlockSpec(memory_space=pltpu.VMEM),)*2,
        scratch_shapes=[pltpu.VMEM((pairs,L,256),BF),pltpu.VMEM((pairs,L,128),BF)],
        compiler_params=pltpu.CompilerParams(vmem_limit_bytes=48*2**20),
        cost_estimate=pl.CostEstimate(flops=4*R*512*D,bytes_accessed=R*D*10,transcendentals=R*512*12),
        name="attend_forward",
    )(scal,q,kv,kvp)

def attn_bwd_kernel(scal,q_ref,kv_ref,kvp_ref,do_ref,mixed_ref,lse_ref,dq_ref,own_ref,far_ref,kb,vb,dka,dva):
    D=q_ref.shape[1]; pairs=D//128; length=kb.shape[1]
    th1=scal[0]; th2=scal[1]; n=scal[2]; c=scal[3]; m=scal[4]
    ext=key_ext(th1,th2,n,length)
    place(kb,pairs,kv_ref,kvp_ref,0,0,m,ext,pairs//2)
    place(vb,pairs,kv_ref,kvp_ref,D,D,m,ext,pairs//2)
    dka[...]=jnp.zeros_like(dka); dva[...]=jnp.zeros_like(dva)
    sub=lax.broadcasted_iota(jnp.int32,(128,TQ),0)
    lane=lax.broadcasted_iota(jnp.int32,(TQ,128),1)
    for tile in range(2):
        r0=(2*tile+m)*TQ
        rows=slice(tile*TQ,(tile+1)*TQ)
        def body(w):
            @pl.loop(0,pairs,unroll=UNROLL_B if w<length else 1)
            def _(p):
                lanes=pl.ds(pl.multiple_of(p*128,128),128)
                qn=q_ref[rows,lanes].astype(F32)*0.125
                don=do_ref[rows,lanes].astype(F32)
                qt=qn.T; dot_=don.T
                prod=dot_*mixed_ref[rows,lanes].astype(F32).T
                outs=[]
                for hh in range(2):
                    shift=scal[8+2*p+hh]
                    oneh,row=query_rows(th1,th2,c,shift,r0)
                    la,lb,lc=split3(-lse_ref[p,hh:hh+1,rows])
                    oneh=oneh+jnp.where(row==3,la,jnp.where(row==4,lb,jnp.where(row==5,lc,0.0)))
                    keep=(sub>=64)==(hh==1)
                    zeros=jnp.zeros((112,TQ),BF)
                    rhs=jnp.concatenate([jnp.where(keep,qt,0.0).astype(BF),oneh.astype(BF),zeros],axis=0)
                    da,db,dc=split3(-jnp.sum(prod[hh*64:(hh+1)*64],axis=0,keepdims=True))
                    ext2=jnp.where(row==3,da,jnp.where(row==4,db,jnp.where(row==5,dc,0.0)))
                    rhs2=jnp.concatenate([jnp.where(keep,dot_,0.0).astype(BF),ext2.astype(BF),zeros],axis=0)
                    keepl=(lane>=64)==(hh==1)
                    qm=jnp.where(keepl,qn,0.0).astype(BF)
                    dom=jnp.where(keepl,don,0.0).astype(BF)
                    win=pl.ds(head_base(th1,th2,c,shift,r0,length-w) if w<length else 0,w)
                    kwin=kb[p,win,:]
                    pt=jnp.exp(dotf(kwin,rhs))
                    dst=(pt*dotf(vb[p,win,:],rhs2)).astype(BF)
                    dva[p,win,:]+=dotf(pt.astype(BF),dom)
                    dka[p,win,:]+=dotf(dst,qm)
                    kt=kwin[:,0:128].T[hh*64:(hh+1)*64]
                    outs.append(dotf(kt,dst))
                dq_ref[rows,lanes]=(jnp.concatenate(outs,axis=0)*0.125).T.astype(BF)
        run_window(tile_need(th1,th2,n,c,r0),length,body)
    for i in range(2):
        mine=pl.ds(pl.multiple_of((2*i+m)*TQ,TQ),TQ)
        theirs=pl.ds(pl.multiple_of((2*i+1-m)*TQ,TQ),TQ)
        for p in range(pairs):
            src=(p+pairs//2)%pairs
            for j,acc in enumerate((dka,dva)):
                own_ref[i*TQ:(i+1)*TQ,j*D+p*128:j*D+(p+1)*128]=acc[p,mine,:]
                far_ref[i*TQ:(i+1)*TQ,j*D+p*128:j*D+(p+1)*128]=acc[src,theirs,:].astype(BF)

def attn_bwd(scal,q,kv,kvp,do,mixed,lse):
    R,D=q.shape; pairs=D//128; L=2*R
    return pl.pallas_call(attn_bwd_kernel,
        out_shape=(jax.ShapeDtypeStruct((R,D),BF),jax.ShapeDtypeStruct((R,2*D),F32),jax.ShapeDtypeStruct((R,2*D),BF)),
        in_specs=[pl.BlockSpec(memory_space=pltpu.SMEM)]+[pl.BlockSpec(memory_space=pltpu.VMEM)]*6,
        out_specs=(pl.BlockSpec(memory_space=pltpu.VMEM),)*3,
        scratch_shapes=[pltpu.VMEM((pairs,L,256),BF),pltpu.VMEM((pairs,L,256),BF),pltpu.VMEM((pairs,L,128),F32),pltpu.VMEM((pairs,L,128),F32)],
        compiler_params=pltpu.CompilerParams(vmem_limit_bytes=48*2**20),
        cost_estimate=pl.CostEstimate(flops=10*R*512*D,bytes_accessed=R*D*26,transcendentals=R*512*12),
        name="attend_backward",
    )(scal,q,kv,kvp,do,mixed,lse)


SWAP = [(0, 1), (1, 0)]


def to_peer(x):
    return lax.ppermute(x, "mp", SWAP)


def forward_x(x):
    return lax.ppermute(x, "section", [(0, 1)])


def backward_x(x):
    return lax.ppermute(x, "section", [(1, 0)])


def dot_nn(a, b):
    return lax.dot_general(a, b, (((1,), (0,)), ((), ())), preferred_element_type=F32)


def dot_nt(a, b):
    return lax.dot_general(a, b, (((1,), (1,)), ((), ())), preferred_element_type=F32)


def dot_tn(a, b):
    return lax.dot_general(a, b, (((0,), (0,)), ((), ())), preferred_element_type=F32)


def norm_rows(residual):
    row_mean = jnp.mean(residual, axis=-1, keepdims=True)
    centred = residual - row_mean
    inverse = lax.rsqrt(jnp.mean(centred * centred, axis=-1, keepdims=True) + EPS)
    return centred * inverse, inverse


def norm_back(upstream, normed, inverse, gain_row):
    scaled = upstream * gain_row
    return inverse * (
        scaled
        - jnp.mean(scaled, axis=-1, keepdims=True)
        - normed * jnp.mean(scaled * normed, axis=-1, keepdims=True)
    )


def gelu_pair(pre_act):
    normal_cdf = 0.5 * (1.0 + lax.erf(pre_act * 2.0 ** (-0.5)))
    density = jnp.exp(-0.5 * pre_act * pre_act) * (2.0 * math.pi) ** (-0.5)
    return (pre_act * normal_cdf, normal_cdf + pre_act * density)


def swap_halves(x, parts):
    rows, width = x.shape
    y = x.reshape(rows, parts, 2, width // parts // 2)
    return jnp.concatenate([y[:, :, 1:], y[:, :, :1]], axis=2).reshape(rows, width)


def forward_tick(h, scal, w):
    q = (dot_nn(h, w["q"]) + w["bq"]).astype(BF)
    kv = (dot_nn(h, w["kv"]) + w["bkv"]).astype(BF)
    kvp = to_peer(kv)
    mixed, lse = attn_fwd(scal, q, kv, kvp)
    n1, inv1 = norm_rows(h.astype(F32) + dot_nn(mixed, w["out"]) + w["lb"][0])
    x1 = n1 * w["ng"][0] + w["lb"][1]
    x1_low = x1.astype(BF)
    act, slope = gelu_pair(dot_nn(x1_low, w["up"]) + w["bup"])
    act = act.astype(BF)
    slope = slope.astype(BF)
    n2, inv2 = norm_rows(x1 + dot_nn(act, w["down"]) + w["lb"][2])
    out = (n2 * w["ng"][1] + w["lb"][3]).astype(BF)
    return out, (h, q, kv, kvp, mixed, lse, n1, inv1, x1_low, act, slope, n2, inv2)


def backward_tick(g, scal, saved, w):
    h, q, kv, kvp, mixed, lse, n1, inv1, x1_low, act, slope, n2, inv2 = saved
    g = g.astype(F32)
    d2 = norm_back(g, n2, inv2, w["ng"][1])
    d2_low = d2.astype(BF)
    d_pre = (dot_nt(d2_low, w["down"]) * slope.astype(F32)).astype(BF)
    dx1 = d2 + dot_nt(d_pre, w["up"])
    d1 = norm_back(dx1, n1, inv1, w["ng"][0])
    d1_low = d1.astype(BF)
    d_mixed = dot_nt(d1_low, w["out"]).astype(BF)
    dq, own, far = attn_bwd(scal, q, kv, kvp, d_mixed, mixed, lse)
    near = to_peer(far)
    dkv = (own + near.astype(F32)).astype(BF)
    leaving = (d1 + dot_nt(dq, w["q"]) + dot_nt(dkv, w["kv"])).astype(BF)
    sums = jnp.stack(
        [
            jnp.sum(dx1 * n1, axis=0),
            jnp.sum(g * n2, axis=0),
            jnp.sum(d1, axis=0),
            jnp.sum(dx1, axis=0),
            jnp.sum(d2, axis=0),
            jnp.sum(g, axis=0),
        ]
    )
    return leaving, (h, mixed, x1_low, act, d2_low, d_pre, d1_low, dq, dkv), sums


def line_positions(size):
    half = size // 2
    inner = [(p, p + 1) for p in range(half - 1)]
    return half, inner


def reduce_dp(x, size):
    if size < 4 or size % 4:
        return lax.psum(x, "dp")
    rows = x.shape[0] // 2
    line = size // 2
    me = lax.axis_index("dp")
    side = lax.rem(me, 2)
    place = me // 2
    x = x.reshape((2, rows) + x.shape[1:])
    keep = lax.dynamic_index_in_dim(x, side, 0, keepdims=False)
    send = lax.dynamic_index_in_dim(x, 1 - side, 0, keepdims=False)
    add = lambda a, b: (a.astype(F32) + b.astype(F32)).astype(BF)
    total = add(keep, lax.ppermute(send, "dp", [(i, i ^ 1) for i in range(size)]))
    half = line // 2
    both = lambda pairs: [(2 * a + s, 2 * b + s) for a, b in pairs for s in range(2)]
    for k in range(half - 1):
        pairs = [(k, k + 1), (line - 1 - k, line - 2 - k)]
        total = add(total, lax.ppermute(total, "dp", both(pairs)))
    total = add(total, lax.ppermute(total, "dp", both([(half - 1, half), (half, half - 1)])))
    for k in reversed(range(half - 1)):
        pairs = [(k + 1, k), (line - 2 - k, line - 1 - k)]
        got = lax.ppermute(total, "dp", both(pairs))
        total = jnp.where((place == k) | (place == line - 1 - k), got, total)
    other = lax.ppermute(total, "dp", [(i, i ^ 1) for i in range(size)])
    first = jnp.where(side == 0, total, other)
    second = jnp.where(side == 0, other, total)
    return jnp.concatenate([first, second], axis=0).reshape((2 * rows,) + x.shape[2:])


def on_device(
    tokens,
    grad_out,
    attention_in,
    attention_bias,
    attention_out,
    up_weight,
    up_bias,
    down_weight,
    norm_gains,
    layer_biases,
    block_counts,
    lengths,
    head_shifts,
):
    dp_size = lax.axis_size("dp")
    section = lax.axis_index("section")
    core = lax.axis_index("mp")
    first = section == 0
    width = tokens.shape[2]
    half = attention_in.shape[3]
    hidden = up_weight.shape[2]
    rows = tokens.shape[1] * 2
    positions = rows * 2

    win, win_p = attention_in[0], to_peer(attention_in[0])
    shifts = jnp.concatenate([head_shifts[0], to_peer(head_shifts)[0]])
    ab, ab_p = attention_bias[0], to_peer(attention_bias)[0]
    bup = jnp.concatenate([up_bias[0], to_peer(up_bias)[0]])
    bv = jnp.concatenate([ab[1], ab_p[1]])
    w = {
        "q": jnp.concatenate([win[:, 0], win_p[:, 0]], axis=1),
        "kv": jnp.concatenate([win[:, 1], win_p[:, 1], win[:, 2], win_p[:, 2]], axis=1),
        "bq": jnp.concatenate([ab[0], ab_p[0]]),
        "bkv": jnp.concatenate([jnp.zeros_like(bv), bv]),
        "out": jnp.concatenate([attention_out[0], to_peer(attention_out)[0]], axis=0),
        "up": jnp.concatenate([up_weight[0], to_peer(up_weight)[0]], axis=1),
        "bup": bup,
        "down": jnp.concatenate([down_weight[0], to_peer(down_weight)[0]], axis=0),
        "ng": norm_gains[0],
        "lb": layer_biases[0],
    }

    def scalars(slot):
        count = lax.dynamic_index_in_dim(block_counts, slot, 0, keepdims=False)
        length = lax.dynamic_index_in_dim(lengths, slot, 0, keepdims=False)
        th1 = (length + count - 1) // count
        th2 = jnp.where(count == 3, (2 * length + 2) // 3, 1 << 20)
        zero = jnp.zeros_like(th1)
        return jnp.concatenate(
            [jnp.stack([th1, th2, length, count, core, zero, zero, zero]), shifts]
        ).astype(jnp.int32)

    tok = [jnp.concatenate([tokens[s], backward_x(tokens[s])], axis=0) for s in range(2)]
    cot = [jnp.concatenate([forward_x(grad_out[s]), grad_out[s]], axis=0) for s in range(2)]
    quarter = rows // 2

    scal_a = scalars(1 - section)
    scal_b = scalars(section)

    out1, _ = forward_tick(tok[0], scalars(jnp.int32(0)), w)
    in2 = jnp.where(first, tok[1], forward_x(out1))
    out2, saved2 = forward_tick(in2, scal_a, w)
    in4 = jnp.where(first, tok[0], forward_x(out2))
    g3, _, _ = backward_tick(cot[0], scal_a, saved2, w)
    out4, saved4 = forward_tick(in4, scal_b, w)
    g5, part5, sums5 = backward_tick(jnp.where(first, backward_x(g3), cot[1]), scal_b, saved4, w)
    g6, part6, sums6 = backward_tick(jnp.where(first, backward_x(g5), cot[0]), scal_a, saved2, w)

    layer_out = jnp.stack(
        [
            jnp.where(first, backward_x(out2[:quarter]), out2[quarter:]),
            jnp.where(first, backward_x(out4[:quarter]), out4[quarter:]),
        ]
    )
    grad_tokens = jnp.stack(
        [
            jnp.where(first, g5[:quarter], forward_x(g5[quarter:])),
            jnp.where(first, g6[:quarter], forward_x(g6[quarter:])),
        ]
    )

    def both(fn):
        return fn(part5) + fn(part6)

    def paired(fn):
        mine = both(lambda part: fn(part, 0))
        far = both(lambda part: fn(part, 1)).astype(BF)
        return mine, far

    h_, mixed_, x1_, act_, d2_, dpre_, d1_, dq_, dkv_ = range(9)
    cut = lambda x, which, size: lax.slice_in_dim(x, which * size, (which + 1) * size, axis=1)

    def add_peer(mine, far):
        return (mine + to_peer(far).astype(F32)).astype(BF)

    ones = jnp.ones((1, rows), BF)
    col = lambda x: jnp.sum(x.astype(F32), axis=0)
    down_g = add_peer(*paired(lambda p, i: dot_tn(cut(p[act_], i, hidden), p[d2_])))
    up_g = add_peer(*paired(lambda p, i: dot_tn(p[x1_], cut(p[dpre_], i, hidden))))
    out_g = add_peer(*paired(lambda p, i: dot_tn(cut(p[mixed_], i, half), p[d1_])))
    q_g = add_peer(*paired(lambda p, i: dot_tn(p[h_], cut(p[dq_], i, half))))
    k_g = add_peer(*paired(lambda p, i: dot_tn(p[h_], cut(p[dkv_], i, half))))
    v_g = add_peer(*paired(lambda p, i: dot_tn(p[h_], cut(p[dkv_], 2 + i, half))))
    ub = both(lambda p: col(p[dpre_]))
    qb = both(lambda p: col(p[dq_]))
    vb = both(lambda p: col(p[dkv_][:, width:]))
    mine_small = jnp.concatenate([ub[:hidden], qb[:half], vb[:half]])
    far_small = jnp.concatenate([ub[hidden:], qb[half:], vb[half:]])
    sums = (sums5 + sums6).reshape(-1)
    small = jnp.concatenate([mine_small, sums])
    small = small + to_peer(jnp.concatenate([far_small, sums]))
    count = small.shape[0]
    small_rows = -(-count // (width * 32)) * 32
    small = jnp.pad(small, (0, small_rows * width - count)).reshape(small_rows, width).astype(BF)

    down_g = reduce_dp(down_g, dp_size)
    up_g = reduce_dp(up_g, dp_size)
    in_g = reduce_dp(jnp.concatenate([q_g, k_g, v_g], axis=1), dp_size)
    out_g = reduce_dp(jnp.concatenate([out_g, small], axis=0), dp_size)
    small = out_g[half:].reshape(-1)[:count].astype(F32)
    ub, qb, vb = small[:hidden], small[hidden : hidden + half], small[hidden + half : hidden + 2 * half]
    sums = small[hidden + 2 * half :].reshape(6, width)
    return (
        layer_out,
        grad_tokens,
        in_g.reshape(width, 3, half).astype(F32)[None],
        jnp.stack([qb, vb])[None],
        out_g[:half].astype(F32)[None],
        up_g.astype(F32)[None],
        ub[None],
        down_g.astype(F32)[None],
        sums[:2][None],
        sums[2:][None],
    )


def solution(mesh):
    return jax.shard_map(
        on_device,
        mesh=mesh,
        in_specs=(
            P("dp", ("section", "mp"), None),
            P("dp", ("section", "mp"), None),
            P("section", None, None, "mp"),
            P("section", None, "mp"),
            P("section", "mp", None),
            P("section", None, "mp"),
            P("section", "mp"),
            P("section", "mp", None),
            P("section", None, None),
            P("section", None, None),
            P("dp"),
            P("dp"),
            P("section", "mp"),
        ),
        out_specs=(
            P("dp", ("section", "mp"), None),
            P("dp", ("section", "mp"), None),
            P("section", None, None, "mp"),
            P("section", None, "mp"),
            P("section", "mp", None),
            P("section", None, "mp"),
            P("section", "mp"),
            P("section", "mp", None),
            P("section", None, None),
            P("section", None, None),
        ),
        check_vma=False,
    )
```

```python
import functools
import math
from typing import Any, NamedTuple

import jax
import jax.numpy as jnp
from jax import lax
from jax.experimental import pallas as pl
from jax.experimental.pallas import tpu as pltpu
from jax.sharding import PartitionSpec as P

BF = jnp.bfloat16
F32 = jnp.float32
EPS = 1e-05
SHUT = -1e30
TILE = 256
FORWARD_WINDOWS = (512, 528)
BACKWARD_WINDOWS = (528,)
CHUNK = 512
BLOCK = 64
VMEM_BYTES = 58 * 2**20
NO_COST = pl.CostEstimate(flops=1, bytes_accessed=1, transcendentals=0)


def dot_nn(a, b):
    return lax.dot_general(a, b, (((1,), (0,)), ((), ())), preferred_element_type=F32)


def dot_nt(a, b):
    return lax.dot_general(a, b, (((1,), (1,)), ((), ())), preferred_element_type=F32)


def dot_tn(a, b):
    return lax.dot_general(a, b, (((0,), (0,)), ((), ())), preferred_element_type=F32)


def mask_numbers(slot, counts, lengths):
    c = counts[slot]
    n = lengths[slot]
    third = (n + 2) // 3
    th1 = jnp.where(c == 3, third, (n + 1) // 2)
    th2 = jnp.where(c == 3, (2 * n + 2) // 3, 1 << 20)
    return th1, th2, n, c, lax.axis_index("mp")


def key_columns(nums, rows):
    th1, th2, n = nums[:3]
    u = lax.broadcasted_iota(jnp.int32, (rows, 128), 0)
    col = lax.broadcasted_iota(jnp.int32, (rows, 128), 1)
    blk = (u >= th1).astype(jnp.int32) + (u >= th2).astype(jnp.int32)
    open_ = (blk == col) & (u < n)
    one = jnp.where(col < 8, 1.0, 0.0)
    return jnp.where(col < 3, jnp.where(open_, 0.0, SHUT), one).astype(BF)


def query_rows(nums, shift, r0):
    th1, th2, _, c, _ = nums
    pos = r0 + lax.broadcasted_iota(jnp.int32, (16, TILE), 1)
    row = lax.broadcasted_iota(jnp.int32, (16, TILE), 0)
    t = (pos >= th1).astype(jnp.int32) + (pos >= th2).astype(jnp.int32) + shift
    t = jnp.where(t >= c, t - c, t)
    return jnp.where(row == t, 1.0, 0.0), row


def split3(x):
    a = x.astype(BF).astype(F32)
    b = (x - a).astype(BF).astype(F32)
    return a, b, (x - a - b).astype(BF).astype(F32)


def window_need(nums, r0):
    th1, th2, n, c, _ = nums
    last = r0 + TILE - 1
    whole = ((r0 < th1) == (last < th1)) & ((r0 < th2) == (last < th2))
    need = jnp.maximum(th1, jnp.minimum(th2, n) - (th1 // 16) * 16)
    need = jnp.maximum(need, jnp.where(c == 3, n - (th2 // 16) * 16, 0))
    return jnp.where(whole, need, 1 << 20)


def window_base(nums, shift, r0, limit):
    th1, th2, _, c, _ = nums
    t = jnp.where(r0 >= th1, 1, 0) + jnp.where(r0 >= th2, 1, 0) + shift
    t = jnp.where(t >= c, t - c, t)
    start = jnp.where(t == 0, 0, jnp.where(t == 1, th1, th2))
    return pl.multiple_of(jnp.minimum((start // 16) * 16, limit), 16)


def by_window(need, length, windows, body):
    prev = 0
    for width in windows:
        if width < length:

            @pl.when((need > prev) & (need <= width))
            def _(width=width):
                body(width)

            prev = width

    @pl.when(need > prev)
    def _():
        body(length)


def place_rows(dst, lanes, own, far, offset, core):
    pairs = dst.shape[0]
    for i in range(2):
        for who, ref in enumerate((own, far)):
            blk = 2 * i + jnp.where(core == who, 0, 1)
            rows = pl.ds(pl.multiple_of(blk * TILE, TILE), TILE)
            for p in range(pairs):
                src = offset + (p if who == 0 else (p + pairs // 2) % pairs) * 128
                dst[p, rows, lanes] = ref[i * TILE : (i + 1) * TILE, src : src + 128]


def place_values(v0, v1, own, far, offset, core):
    pairs = v0.shape[0]
    lane = lax.broadcasted_iota(jnp.int32, (TILE, 128), 1)
    ones = jnp.ones((TILE, 128), BF)
    for i in range(2):
        for who, ref in enumerate((own, far)):
            blk = 2 * i + jnp.where(core == who, 0, 1)
            rows = pl.ds(pl.multiple_of(blk * TILE, TILE), TILE)
            for p in range(pairs):
                src = offset + (p if who == 0 else (p + pairs // 2) % pairs) * 128
                x = ref[i * TILE : (i + 1) * TILE, src : src + 128]
                v0[p, rows, :] = jnp.where(lane < 64, x, ones)
                v1[p, rows, :] = jnp.where(lane < 64, ones, x)


def head_shift(own, far, j):
    heads = own.shape[1]
    if isinstance(j, int):
        return own[0, j] if j < heads else far[0, j - heads]
    return jnp.where(j < heads, own[0, jnp.minimum(j, heads - 1)], far[0, jnp.maximum(j - heads, 0)])


def attend(nums, shifts, q, kb, v0, v1, score, weight, top, mixed, lse):
    pairs, length = kb.shape[:2]
    th1, th2, _, c, core = nums
    heads = 2 * pairs
    lane = lax.broadcasted_iota(jnp.int32, (TILE, 128), 1)
    sub = lax.broadcasted_iota(jnp.int32, (TILE, 128), 0)

    @pl.loop(0, 2)
    def _(tile):
        r0 = (2 * tile + core) * TILE
        rows = pl.ds(pl.multiple_of(tile * TILE, TILE), TILE)
        behind = ((r0 + sub) >= th1).astype(jnp.int32) + ((r0 + sub) >= th2).astype(jnp.int32) - lane

        def body(width):
            outs = [None] * heads

            def window(j):
                shift = head_shift(*shifts, j)
                return pl.ds(window_base(nums, shift, r0, length - width) if width < length else 0, width)

            def scores(j):
                p, hh = divmod(j, 2)
                qn = q[rows, p * 128 : (p + 1) * 128].astype(F32) * 0.125
                d = behind + head_shift(*shifts, j)
                target = jnp.where((lane < c) & ((d == 0) | (d == c)), 1.0, 0.0)
                qm = jnp.where((lane >= 64) == (hh == 1), qn, 0.0)
                lhs = jnp.concatenate([qm.astype(BF), target.astype(BF)], axis=1)
                score[j % 2, :, 0:width] = dot_nt(lhs, kb[p, window(j), :])

            def softmax(j):
                for r in range(0, TILE, 128):
                    part = score[j % 2, r : r + 128, 0:width]
                    largest = jnp.max(part, axis=1, keepdims=True)
                    top[j % 4, r : r + 128, :] = jnp.broadcast_to(largest, (128, 128))
                    weight[j % 2, r : r + 128, 0:width] = jnp.exp(part - largest).astype(BF)

            def product(j):
                p, hh = divmod(j, 2)
                outs[j] = dot_nn(weight[j % 2, :, 0:width], (v0, v1)[hh][p, window(j), :])
                if hh == 1:
                    total = jnp.where(lane < 64, pltpu.roll(outs[j - 1], 64, 1), pltpu.roll(outs[j], 64, 1))
                    value = jnp.where(lane < 64, outs[j - 1], outs[j])
                    mixed[rows, p * 128 : (p + 1) * 128] = (value / total).astype(BF)
                    if lse is not None:
                        both = (jnp.where(lane < 64, top[(j - 1) % 4], top[j % 4]) + jnp.log(total)).T
                        lse[p, 0:1, rows] = both[0:1]
                        lse[p, 1:2, rows] = both[64:65]

            for step in range(heads + 2):
                if step < heads:
                    scores(step)
                if 1 <= step <= heads:
                    softmax(step - 1)
                if step >= 2:
                    product(step - 2)

        by_window(window_need(nums, r0), length, FORWARD_WINDOWS, body)


def attend_back(nums, shifts, q, do, mixed, lse, kb, vb, dka, dva, dq):
    pairs, length = kb.shape[:2]
    core = nums[4]
    sub = lax.broadcasted_iota(jnp.int32, (128, TILE), 0)
    lane = lax.broadcasted_iota(jnp.int32, (TILE, 128), 1)
    for tile in range(2):
        r0 = (2 * tile + core) * TILE
        rows = slice(tile * TILE, (tile + 1) * TILE)

        def body(width):
            @pl.loop(0, pairs, unroll=2 if width < length else 1)
            def _(p):
                lanes = pl.ds(pl.multiple_of(p * 128, 128), 128)
                qn = q[rows, lanes].astype(F32) * 0.125
                don = do[rows, lanes].astype(F32)
                qt = qn.T
                dot_ = don.T
                prod = dot_ * mixed[rows, lanes].astype(F32).T
                outs = []
                for hh in range(2):
                    shift = head_shift(*shifts, 2 * p + hh)
                    target, row = query_rows(nums, shift, r0)
                    la, lb, lc = split3(-lse[p, hh : hh + 1, rows])
                    target = target + jnp.where(row == 3, la, jnp.where(row == 4, lb, jnp.where(row == 5, lc, 0.0)))
                    keep = (sub >= 64) == (hh == 1)
                    zeros = jnp.zeros((112, TILE), BF)
                    rhs = jnp.concatenate([jnp.where(keep, qt, 0.0).astype(BF), target.astype(BF), zeros], axis=0)
                    da, db, dc = split3(-jnp.sum(prod[hh * 64 : (hh + 1) * 64], axis=0, keepdims=True))
                    minus = jnp.where(row == 3, da, jnp.where(row == 4, db, jnp.where(row == 5, dc, 0.0)))
                    rhs2 = jnp.concatenate([jnp.where(keep, dot_, 0.0).astype(BF), minus.astype(BF), zeros], axis=0)
                    keepl = (lane >= 64) == (hh == 1)
                    qm = jnp.where(keepl, qn, 0.0).astype(BF)
                    dom = jnp.where(keepl, don, 0.0).astype(BF)
                    start = window_base(nums, shift, r0, length - width) if width < length else 0
                    win = pl.ds(start, width)
                    kwin = kb[p, win, :]
                    pt = jnp.exp(dot_nn(kwin, rhs))
                    ds = (pt * dot_nn(vb[p, win, :], rhs2)).astype(BF)
                    dva[p, win, :] += dot_nn(pt.astype(BF), dom)
                    dka[p, win, :] += dot_nn(ds, qm)
                    kt = kwin[:, 0:128].T[hh * 64 : (hh + 1) * 64]
                    outs.append(dot_nn(kt, ds))
                dq[rows, lanes] = (jnp.concatenate(outs, axis=0) * 0.125).T.astype(BF)

        by_window(window_need(nums, r0), length, BACKWARD_WINDOWS, body)


def gelu_pair(x):
    density = jnp.exp(x * x * (-0.5)) * (2.0 * math.pi) ** (-0.5)
    cdf = 0.5 + 0.5 * lax.erf(x * (2.0 ** (-0.5)))
    return x * cdf, cdf + x * density


def norm_rows(x):
    scale = 1.0 / x.shape[-1]
    centred = x - jnp.sum(x, axis=-1, keepdims=True) * scale
    inv = lax.rsqrt(jnp.sum(centred * centred, axis=-1, keepdims=True) * scale + EPS)
    return centred * inv, inv


def norm_back(up, normed, inv, gain):
    scale = 1.0 / normed.shape[-1]
    e = up * gain
    a = jnp.sum(e, axis=-1, keepdims=True) * scale
    b = jnp.sum(e * normed, axis=-1, keepdims=True) * scale
    return inv * (e - a - normed * b)


def copier(sems):
    used = [0]

    def start(src, dst):
        copy = pltpu.make_async_copy(src, dst, sems.at[used[0]])
        used[0] += 1
        copy.start()
        return copy

    return start


class ForwardIn(NamedTuple):
    q: Any
    kv: Any
    kvp: Any
    h: Any
    wout: Any
    wup: Any
    wdown: Any
    wout_far: Any
    wup_far: Any
    wdown_far: Any


class ForwardOut(NamedTuple):
    out: Any
    mixed: Any
    lse: Any
    x1_low: Any
    act: Any
    slope: Any
    n1: Any
    inv1: Any
    n2: Any
    inv2: Any


class ForwardWork(NamedTuple):
    kb: Any
    v0: Any
    v1: Any
    score: Any
    weight: Any
    top: Any
    pre: Any
    x1: Any
    acc: Any


def weight_copies(start, src, x):
    c_out, c_up, c_down = [], [], []
    for j, (out, up, down) in enumerate(((src.wout, src.wup, src.wdown), (src.wout_far, src.wup_far, src.wdown_far))):
        rows, cols = out.shape[0], up.shape[1]
        c_out.append(start(out, x.wout.at[j * rows : (j + 1) * rows, :]))
        c_up.append(start(up, x.wup.at[:, j * cols : (j + 1) * cols]))
        c_down.append(start(down, x.wdown.at[j * cols : (j + 1) * cols, :]))
    return c_out, c_up, c_down


def forward_kernel(save, slot_of, tokens, counts, lengths, shift_own, shift_far, lb, ng, bup_own, bup_far, *refs):
    refs = list(refs[tokens:])
    take = lambda kind: kind(*[refs.pop(0) for _ in range(len(kind._fields))])
    src = take(ForwardIn)
    dst = take(ForwardOut) if save else ForwardOut(refs.pop(0), *[None] * 9)
    x = ForwardIn(*[refs.pop(0) for _ in range(7)], None, None, None)
    y = take(ForwardOut)
    t = take(ForwardWork)
    start = copier(refs[0])
    rows, width = x.h.shape
    hidden = x.wup.shape[1]
    half = hidden // 2
    load = ForwardIn(*[None] * 10)._replace(
        kv=start(src.kv, x.kv),
        kvp=start(src.kvp, x.kvp),
        q=start(src.q, x.q),
        h=start(src.h, x.h),
    )
    c_out, c_up, c_down = weight_copies(start, src, x)
    done = []

    def ship(a, b):
        if b is not None:
            done.append(start(a, b))

    def ship_part(a, b, part):
        if b is not None:
            done.append(start(a.at[:, part], b.at[:, part]))

    nums = mask_numbers(slot_of(lax.axis_index("section")), counts, lengths)
    core = nums[4]
    ext = key_columns(nums, t.kb.shape[1])
    for p in range(t.kb.shape[0]):
        t.kb[p, :, 128:256] = ext
    load.kv.wait()
    load.kvp.wait()
    place_rows(t.kb, slice(0, 128), x.kv, x.kvp, 0, core)
    place_values(t.v0, t.v1, x.kv, x.kvp, width, core)
    load.q.wait()
    attend(
        nums, (shift_own, shift_far), x.q, t.kb, t.v0, t.v1, t.score, t.weight, t.top, y.mixed, y.lse if save else None
    )
    ship(y.mixed, dst.mixed)
    ship(y.lse, dst.lse)
    for copy in c_out:
        copy.wait()
    t.acc[...] = dot_nn(y.mixed[...], x.wout[...])
    load.h.wait()
    for r in range(0, rows, BLOCK):
        rs = slice(r, r + BLOCK)
        normed, inv = norm_rows(x.h[rs, :].astype(F32) + t.acc[rs, :] + lb[0:1, :])
        if save:
            y.n1[rs, :] = normed
            y.inv1[rs, :] = jnp.broadcast_to(inv, (BLOCK, 128))
        full = normed * ng[0:1, :] + lb[1:2, :]
        t.x1[rs, :] = full
        y.x1_low[rs, :] = full.astype(BF)
    ship(y.x1_low, dst.x1_low)
    ship(y.n1, dst.n1)
    ship(y.inv1, dst.inv1)
    chunks = hidden // CHUNK

    def up(j):
        t.pre[j % 2] = dot_nn(y.x1_low[...], x.wup[:, j * CHUNK : (j + 1) * CHUNK])

    def activate(j):
        part = slice(j * CHUNK, (j + 1) * CHUNK)
        low = (j * CHUNK) % half
        bias = (bup_own if j < chunks // 2 else bup_far)[0:1, low : low + CHUNK]
        for r in range(0, rows, BLOCK):
            rs = slice(r, r + BLOCK)
            act, slope = gelu_pair(t.pre[j % 2, rs, :] + bias)
            y.act[rs, part] = act.astype(BF)
            if save:
                y.slope[rs, part] = slope.astype(BF)

    c_up[0].wait()
    up(0)
    for j in range(chunks // 2):
        if j + 1 == chunks // 2:
            c_up[1].wait()
        up(j + 1)
        activate(j)
    ship_part(y.act, dst.act, slice(0, half))
    ship_part(y.slope, dst.slope, slice(0, half))
    c_down[0].wait()
    t.acc[...] = dot_nn(y.act[:, :half], x.wdown[:half, :])
    for j in range(chunks // 2, chunks):
        if j + 1 < chunks:
            up(j + 1)
        activate(j)
    ship_part(y.act, dst.act, slice(half, hidden))
    ship_part(y.slope, dst.slope, slice(half, hidden))
    c_down[1].wait()
    t.acc[...] += dot_nn(y.act[:, half:], x.wdown[half:, :])
    for r in range(0, rows, BLOCK):
        rs = slice(r, r + BLOCK)
        normed, inv = norm_rows(t.x1[rs, :] + t.acc[rs, :] + lb[2:3, :])
        if save:
            y.n2[rs, :] = normed
            y.inv2[rs, :] = jnp.broadcast_to(inv, (BLOCK, 128))
        y.out[rs, :] = (normed * ng[1:2, :] + lb[3:4, :]).astype(BF)
    ship(y.out, dst.out)
    ship(y.n2, dst.n2)
    ship(y.inv2, dst.inv2)
    for copy in done:
        copy.wait()


def buffers(shapes):
    return [pltpu.VMEM(*s) for s in shapes]


def results(shapes):
    return tuple(jax.ShapeDtypeStruct(*s) for s in shapes)


IN_SMEM = pl.BlockSpec(memory_space=pltpu.SMEM)
IN_VMEM = pl.BlockSpec(memory_space=pltpu.VMEM)
IN_HBM = pl.BlockSpec(memory_space=pltpu.HBM)


def forward_call(save, slot_of, w, q, kv, kvp, h, tokens=()):
    rows, width = h.shape
    hidden = 2 * w.up.shape[1]
    pairs, length = width // 128, 2 * rows
    low, wide, full = ((rows, width), BF), ((rows, hidden), BF), ((rows, width), F32)
    one, twice = ((rows, 128), F32), ((rows, 2 * width), BF)
    shapes_in = (low, twice, twice, low, ((width, width), BF), ((width, hidden), BF), ((hidden, width), BF))
    shapes_out = ForwardOut(low, low, ((pairs, 2, rows), F32), low, wide, wide, full, one, full, one)
    if not save:
        gone = ((16, 128), BF)
        scratch_out = shapes_out._replace(lse=gone, slope=gone, n1=gone, inv1=gone, n2=gone, inv2=gone)
    else:
        scratch_out = shapes_out
    work = ForwardWork(
        ((pairs, length, 256), BF),
        ((pairs, length, 128), BF),
        ((pairs, length, 128), BF),
        ((2, TILE, length), F32),
        ((2, TILE, length), BF),
        ((4, TILE, 128), F32),
        ((2, rows, CHUNK), F32),
        full,
        full,
    )
    outs = shapes_out if save else shapes_out[:1]
    res = pl.pallas_call(
        functools.partial(forward_kernel, save, slot_of, len(tokens)),
        out_shape=results(outs),
        in_specs=[IN_SMEM] * 4 + [IN_VMEM] * 4 + [IN_HBM] * (10 + len(tokens)),
        out_specs=(IN_HBM,) * len(outs),
        scratch_shapes=buffers(shapes_in) + buffers(scratch_out) + buffers(work) + [pltpu.SemaphoreType.DMA((24,))],
        compiler_params=pltpu.CompilerParams(vmem_limit_bytes=VMEM_BYTES),
        cost_estimate=NO_COST,
        name="layer_forward",
    )(
        w.counts, w.lengths, w.shift_own, w.shift_far, w.lb, w.ng, w.bup_own, w.bup_far, *tokens,
        q, kv, kvp, h, w.out, w.up, w.down, w.out_far, w.up_far, w.down_far,
    )
    return ForwardOut(*res) if save else ForwardOut(res[0], *[None] * 9)


class RowsIn(NamedTuple):
    g: Any
    n2: Any
    inv2: Any
    n1: Any
    inv1: Any
    slope: Any
    wout: Any
    wup: Any
    wdown: Any
    wout_far: Any
    wup_far: Any
    wdown_far: Any


class RowsOut(NamedTuple):
    d2_low: Any
    d_pre: Any
    d1: Any
    d1_low: Any


class HeadsIn(NamedTuple):
    mixed: Any
    lse: Any
    q: Any
    kv: Any
    kvp: Any


class HeadsOut(NamedTuple):
    dq: Any
    near: Any
    far: Any


class HeadsWork(NamedTuple):
    kb: Any
    vb: Any
    dka: Any
    dva: Any


def rows_back(start, src, dst, x, y, d_mixed, dx, ng, sums, bias_sums, behind):
    rows, width = x.g.shape
    hidden = x.wup.shape[1]
    half = hidden // 2
    chunks = hidden // CHUNK
    early = [start(src.g, x.g), start(src.n2, x.n2), start(src.inv2, x.inv2)]
    c_slope = [
        start(src.slope.at[:, part], x.slope.at[:, part]) for part in (slice(0, half), slice(half, hidden))
    ]
    c_out, c_up, c_down = weight_copies(start, src, x)
    late = [start(src.n1, x.n1), start(src.inv1, x.inv1)]
    behind()
    done = []
    zero = jnp.zeros((1, width), F32)
    s_gn, s_g, s_d2 = zero, zero, zero
    for copy in early:
        copy.wait()
    for r in range(0, rows, BLOCK):
        rs = slice(r, r + BLOCK)
        g = x.g[rs, :].astype(F32)
        normed = x.n2[rs, :]
        d2 = norm_back(g, normed, x.inv2[rs, 0:1], ng[1:2, :])
        dx[rs, :] = d2
        y.d2_low[rs, :] = d2.astype(BF)
        s_gn += jnp.sum(g * normed, axis=0, keepdims=True)
        s_g += jnp.sum(g, axis=0, keepdims=True)
        s_d2 += jnp.sum(d2, axis=0, keepdims=True)
    done.append(start(y.d2_low, dst.d2_low))
    for k in range(2):
        c_down[k].wait()
        c_slope[k].wait()
        for j in range(k * chunks // 2, (k + 1) * chunks // 2):
            part = slice(j * CHUNK, (j + 1) * CHUNK)
            d_act = dot_nt(y.d2_low[...], x.wdown[part, :])
            d_pre = (d_act * x.slope[:, part].astype(F32)).astype(BF)
            y.d_pre[:, part] = d_pre
            bias_sums[0:1, part] = jnp.sum(d_pre.astype(F32), axis=0, keepdims=True)
        part = slice(k * half, (k + 1) * half)
        done.append(start(y.d_pre.at[:, part], dst.d_pre.at[:, part]))
        c_up[k].wait()
        dx[...] += dot_nt(y.d_pre[:, part], x.wup[:, part])
    s_dn, s_dx, s_d1 = zero, zero, zero
    late[0].wait()
    late[1].wait()
    for r in range(0, rows, BLOCK):
        rs = slice(r, r + BLOCK)
        g = dx[rs, :]
        normed = x.n1[rs, :]
        d1 = norm_back(g, normed, x.inv1[rs, 0:1], ng[0:1, :])
        y.d1[rs, :] = d1
        y.d1_low[rs, :] = d1.astype(BF)
        s_dn += jnp.sum(g * normed, axis=0, keepdims=True)
        s_dx += jnp.sum(g, axis=0, keepdims=True)
        s_d1 += jnp.sum(d1, axis=0, keepdims=True)
    done += [start(y.d1, dst.d1), start(y.d1_low, dst.d1_low)]
    for i, s in enumerate((s_dn, s_gn, s_d1, s_dx, s_d2, s_g)):
        sums[i : i + 1, :] = s
    sums[6:8, :] = jnp.zeros((2, width), F32)
    for copy in c_out:
        copy.wait()
    d_mixed[...] = dot_nt(y.d1_low[...], x.wout[...]).astype(BF)
    return done


def heads_back(start, load, dst, x, y, t, d_mixed, nums, shifts):
    width = x.q.shape[1]
    core = nums[4]
    pairs = t.kb.shape[0]
    ext = key_columns(nums, t.kb.shape[1])
    for p in range(pairs):
        t.kb[p, :, 128:256] = ext
        t.vb[p, :, 128:256] = ext
    for copy in load:
        copy.wait()
    place_rows(t.kb, slice(0, 128), x.kv, x.kvp, 0, core)
    place_rows(t.vb, slice(0, 128), x.kv, x.kvp, width, core)
    t.dka[...] = jnp.zeros_like(t.dka)
    t.dva[...] = jnp.zeros_like(t.dva)
    attend_back(nums, shifts, x.q, d_mixed, x.mixed, x.lse, t.kb, t.vb, t.dka, t.dva, y.dq)
    done = [start(y.dq, dst.dq)]
    for to, side, turn in ((y.far, 1 - core, pairs // 2), (y.near, core, 0)):
        for i in range(2):
            mine = pl.ds(pl.multiple_of((2 * i + side) * TILE, TILE), TILE)
            for p in range(pairs):
                for j, total in enumerate((t.dka, t.dva)):
                    lanes = slice(j * width + p * 128, j * width + (p + 1) * 128)
                    to[i * TILE : (i + 1) * TILE, lanes] = total[(p + turn) % pairs, mine, :].astype(to.dtype)
    done += [start(y.far, dst.far), start(y.near, dst.near)]
    return done


ALL, ROWS, HEADS = 3, 1, 2


def backward_kernel(which, slot_of, tokens, counts, lengths, shift_own, shift_far, ng, *refs):
    refs = list(refs[tokens:])
    take = lambda kind: kind(*[refs.pop(0) for _ in range(len(kind._fields))])
    rows_on, heads_on = which & ROWS, which & HEADS
    if rows_on:
        r_src = take(RowsIn)
    if heads_on:
        h_src = take(HeadsIn)
    if which == HEADS:
        mixed_src = refs.pop(0)
    if rows_on:
        r_dst = take(RowsOut)
        sums, bias_sums = refs.pop(0), refs.pop(0)
    if which == ROWS:
        mixed_dst = refs.pop(0)
    if heads_on:
        h_dst = take(HeadsOut)
    d_mixed = refs.pop(0)
    if rows_on:
        r_x = RowsIn(*[refs.pop(0) for _ in range(9)], None, None, None)
        r_y, dx = take(RowsOut), refs.pop(0)
    if heads_on:
        h_x, h_y, h_t = take(HeadsIn), take(HeadsOut), take(HeadsWork)
    start = copier(refs[0])
    load, done = [], []

    def load_heads():
        if heads_on:
            load.extend(start(a, b) for a, b in zip(h_src, h_x))

    if rows_on:
        done += rows_back(start, r_src, r_dst, r_x, r_y, d_mixed, dx, ng, sums, bias_sums, load_heads)
    else:
        load_heads()
        load.append(start(mixed_src, d_mixed))
    if which == ROWS:
        done.append(start(d_mixed, mixed_dst))
    if heads_on:
        nums = mask_numbers(slot_of(lax.axis_index("section")), counts, lengths)
        done += heads_back(start, load, h_dst, h_x, h_y, h_t, d_mixed, nums, (shift_own, shift_far))
    for copy in done:
        copy.wait()


def gradient_kernel(*refs):
    refs = list(refs)
    src = [refs.pop(0) for _ in range(9)]
    dst = [refs.pop(0) for _ in range(5)]
    col_sums = refs.pop(0)
    x = [refs.pop(0) for _ in range(9)]
    y = [refs.pop(0) for _ in range(5)]
    start = copier(refs[0])
    load = [start(a, b) for a, b in zip(src, x)]
    done = []
    act, d2_low, x1_low, d_pre, mixed, d1_low, h, dq, dkv = range(9)
    for k, (left, right) in enumerate(((act, d2_low), (x1_low, d_pre), (mixed, d1_low), (h, dq), (h, dkv))):
        for i in (left, right):
            if load[i] is not None:
                load[i].wait()
                load[i] = None
        tall, broad = y[k].shape
        slab = CHUNK if max(tall, broad) % CHUNK == 0 else TILE
        for j in range(max(tall, broad) // slab):
            part = slice(j * slab, (j + 1) * slab)
            if tall > broad:
                y[k][part, :] = dot_tn(x[left][:, part], x[right][...]).astype(BF)
                done.append(start(y[k].at[part, :], dst[k].at[part, :]))
            else:
                y[k][:, part] = dot_tn(x[left][...], x[right][:, part]).astype(BF)
                done.append(start(y[k].at[:, part], dst[k].at[:, part]))
    width = x[h].shape[1]
    col_sums[0:1, :] = jnp.sum(x[dq][...].astype(F32), axis=0, keepdims=True)
    col_sums[1:2, :] = jnp.sum(x[dkv][:, width:].astype(F32), axis=0, keepdims=True)
    for copy in done:
        copy.wait()


def gradient_call(s, b):
    f = s.f
    rows, width = s.h.shape
    hidden = f.act.shape[1]
    args = (f.act, b.d2_low, f.x1_low, b.d_pre, f.mixed, b.d1_low, s.h, b.dq, b.dkv)
    shapes = [
        ((hidden, width), BF), ((width, hidden), BF), ((width, width), BF), ((width, width), BF), ((width, 2 * width), BF),
    ]
    return pl.pallas_call(
        gradient_kernel,
        out_shape=results(shapes + [((2, width), F32)]),
        in_specs=[IN_HBM] * 9,
        out_specs=(IN_HBM,) * 5 + (IN_VMEM,),
        scratch_shapes=buffers([(a.shape, BF) for a in args]) + buffers(shapes) + [pltpu.SemaphoreType.DMA((40,))],
        compiler_params=pltpu.CompilerParams(vmem_limit_bytes=VMEM_BYTES),
        cost_estimate=NO_COST,
        name="layer_gradient",
    )(*args)


def half_gradient_kernel(k, by_rows, token, left_h, right_h, early_h, out_h, left, right, early, out, sems):
    start = copier(sems)
    tall, broad = out.shape
    if by_rows:
        load = [start(left_h.at[:, k * tall : (k + 1) * tall], left), start(right_h, right)]
        before = start(early_h.at[k * tall : (k + 1) * tall, :], early)
    else:
        load = [start(left_h, left), start(right_h.at[:, k * broad : (k + 1) * broad], right)]
        before = start(early_h.at[:, k * broad : (k + 1) * broad], early)
    for copy in load:
        copy.wait()
    before.wait()
    done = []
    for j in range(2):
        if by_rows:
            part = slice(j * tall // 2, (j + 1) * tall // 2)
            out[part, :] = (dot_tn(left[:, part], right[...]) + early[part, :].astype(F32)).astype(BF)
            done.append(start(out.at[part, :], out_h.at[part, :]))
        else:
            part = slice(j * broad // 2, (j + 1) * broad // 2)
            out[:, part] = (dot_tn(left[...], right[:, part]) + early[:, part].astype(F32)).astype(BF)
            done.append(start(out.at[:, part], out_h.at[:, part]))
    for copy in done:
        copy.wait()


def half_gradient_call(token, left, right, early, k, by_rows):
    rows = left.shape[0]
    tall, broad = early.shape
    tall, broad = (tall // 2, broad) if by_rows else (tall, broad // 2)
    out = ((tall, broad), BF)
    return pl.pallas_call(
        functools.partial(half_gradient_kernel, k, by_rows),
        out_shape=jax.ShapeDtypeStruct(*out),
        in_specs=[IN_HBM] * 4,
        out_specs=IN_HBM,
        scratch_shapes=buffers([((rows, tall), BF), ((rows, broad), BF), out, out]) + [pltpu.SemaphoreType.DMA((5,))],
        compiler_params=pltpu.CompilerParams(vmem_limit_bytes=VMEM_BYTES),
        cost_estimate=NO_COST,
        name="half_gradient",
    )(token, left, right, early)


def last_gradient_kernel(*refs):
    token, mixed_h, d1_h, h_h, dq_h, dkv_h, eo_h, eq_h, ekv_h, c5, s5, s6, u5, u6, *refs = refs
    outs, refs = refs[:4], refs[4:]
    small_own, small_far, mixed, d1, h, dq, dkv, eo, eq, ekv, oo, fo, oi, fi, sems = refs
    start = copier(sems)
    pairs = ((h_h, h), (dq_h, dq), (eq_h, eq), (dkv_h, dkv), (ekv_h, ekv), (mixed_h, mixed), (d1_h, d1), (eo_h, eo))
    load = [start(a, b) for a, b in pairs]
    width = h.shape[1]
    half = width // 2
    done = []
    for copy in load[:5]:
        copy.wait()
    for k, to, away in ((1, fi, outs[3]), (0, oi, outs[2])):
        for part in range(3):
            right, before, at = ((dq, eq, 0), (dkv, ekv, 0), (dkv, ekv, width))[part]
            lanes = slice(at + k * half, at + (k + 1) * half)
            total = dot_tn(h[...], right[:, lanes]) + before[:, lanes].astype(F32)
            to[part * width : (part + 1) * width, :] = total.astype(BF)
        done.append(start(to, away))
    for copy in load[5:]:
        copy.wait()
    for k, to, away in ((1, fo, outs[1]), (0, oo, outs[0])):
        lanes = slice(k * half, (k + 1) * half)
        to[...] = (dot_tn(mixed[:, lanes], d1[...]) + eo[lanes, :].astype(F32)).astype(BF)
        done.append(start(to, away))
    qb = c5[0:1, :] + jnp.sum(dq[...].astype(F32), axis=0, keepdims=True)
    vb = c5[1:2, :] + jnp.sum(dkv[:, width:].astype(F32), axis=0, keepdims=True)
    ub = u5[...] + u6[...]
    for k, to in ((0, small_own), (1, small_far)):
        to[...] = jnp.zeros_like(to)
        to[0:6, :] = s5[0:6, :] + s6[0:6, :]
        for j in range(2):
            to[6 + j : 7 + j, :] = ub[:, (2 * k + j) * width : (2 * k + j + 1) * width]
        to[8:9, :half] = qb[:, k * half : (k + 1) * half]
        to[8:9, half:] = vb[:, k * half : (k + 1) * half]
    for copy in done:
        copy.wait()


def last_gradient_call(token, s, b, early, b5):
    rows, width = s.h.shape
    half = width // 2
    args = (s.f.mixed, b.d1_low, s.h, b.dq, b.dkv, early[2], early[3], early[4])
    shapes = [((half, width), BF), ((half, width), BF), ((3 * width, half), BF), ((3 * width, half), BF)]
    return pl.pallas_call(
        last_gradient_kernel,
        out_shape=results(shapes + [((16, width), F32)] * 2),
        in_specs=[IN_HBM] * 9 + [IN_VMEM] * 5,
        out_specs=(IN_HBM,) * 4 + (IN_VMEM,) * 2,
        scratch_shapes=buffers([(a.shape, BF) for a in args]) + buffers(shapes) + [pltpu.SemaphoreType.DMA((16,))],
        compiler_params=pltpu.CompilerParams(vmem_limit_bytes=VMEM_BYTES),
        cost_estimate=NO_COST,
        name="last_gradient",
    )(token, *args, early[5], b5.sums, b.sums, b5.bias_sums, b.bias_sums)


class Back(NamedTuple):
    d2_low: Any
    d_pre: Any
    d1: Any
    d1_low: Any
    sums: Any
    bias_sums: Any
    dq: Any
    near: Any
    far: Any
    dkv: Any


def backward_call(which, slot_of, w, g, f, q, kv, kvp, d_mixed=None, tokens=()):
    rows, width = f.n1.shape
    hidden = 2 * w.up.shape[1]
    pairs, length = width // 128, 2 * rows
    low, wide, full = ((rows, width), BF), ((rows, hidden), BF), ((rows, width), F32)
    one = ((rows, 128), F32)
    twice = ((rows, 2 * width), BF)
    r_in = (low, full, one, full, one, wide, ((width, width), BF), ((width, hidden), BF), ((hidden, width), BF))
    r_out = RowsOut(low, wide, full, low)
    h_in = HeadsIn(low, ((pairs, 2, rows), F32), low, twice, twice)
    h_out = HeadsOut(low, ((rows, 2 * width), F32), twice)
    h_work = HeadsWork(*[((pairs, length, 256), BF)] * 2, *[((pairs, length, 128), F32)] * 2)
    args, outs, out_specs, scratch = [], [], [], [low]
    if which & ROWS:
        args += [g, f.n2, f.inv2, f.n1, f.inv1, f.slope, w.out, w.up, w.down, w.out_far, w.up_far, w.down_far]
        outs += list(r_out) + [((8, width), F32), ((1, hidden), F32)]
        out_specs += [IN_HBM] * len(r_out) + [IN_VMEM] * 2
        scratch += list(r_in) + list(r_out) + [full]
    if which & HEADS:
        args += [f.mixed, f.lse, q, kv, kvp]
        scratch += list(h_in) + list(h_out) + list(h_work)
    if which == HEADS:
        args.append(d_mixed)
    if which == ROWS:
        outs.append(low)
        out_specs.append(IN_HBM)
    if which & HEADS:
        outs += list(h_out)
        out_specs += [IN_HBM] * len(h_out)
    return pl.pallas_call(
        functools.partial(backward_kernel, which, slot_of, len(tokens)),
        out_shape=results(outs),
        in_specs=[IN_SMEM] * 4 + [IN_VMEM] + [IN_HBM] * (len(tokens) + len(args)),
        out_specs=tuple(out_specs),
        scratch_shapes=buffers(scratch) + [pltpu.SemaphoreType.DMA((32,))],
        compiler_params=pltpu.CompilerParams(vmem_limit_bytes=VMEM_BYTES),
        cost_estimate=NO_COST,
        name="layer_backward",
    )(w.counts, w.lengths, w.shift_own, w.shift_far, w.ng, *tokens, *args)


SWAP = [(0, 1), (1, 0)]


def to_peer(x):
    return lax.ppermute(x, "mp", SWAP)


def next_section(x):
    return lax.ppermute(x, "section", [(0, 1)])


def last_section(x):
    return lax.ppermute(x, "section", [(1, 0)])


def add_low(a, b):
    return (a.astype(F32) + b.astype(F32)).astype(BF)


def gate_kernel(*refs):
    pass


def tied(*xs):
    hbm = pl.BlockSpec(memory_space=pl.ANY)
    return pl.pallas_call(
        gate_kernel,
        out_shape=tuple(jax.ShapeDtypeStruct(x.shape, x.dtype) for x in xs),
        in_specs=[hbm] * len(xs),
        out_specs=(hbm,) * len(xs),
        input_output_aliases={i: i for i in range(len(xs))},
        cost_estimate=NO_COST,
        name="gate",
    )(*xs)


class Sum:
    def __init__(self, x, size):
        self.whole = None
        if size < 4 or size % 4:
            self.whole = self.sent = lax.psum(x, "dp")
            return
        self.size = size
        self.steps = self.walk(x)
        self.got = next(self.steps)

    def walk(self, x):
        size = self.size
        line = size // 2
        half = line // 2
        me = lax.axis_index("dp")
        side = lax.rem(me, 2)
        place = me // 2
        pairs = [(i, i ^ 1) for i in range(size)]
        on_line = lambda moves: [(2 * a + s, 2 * b + s) for a, b in moves for s in range(2)]
        rows = x.shape[0] // 2
        x = x.reshape((2, rows) + x.shape[1:])
        keep = lax.dynamic_index_in_dim(x, side, 0, keepdims=False)
        send = lax.dynamic_index_in_dim(x, 1 - side, 0, keepdims=False)
        self.sent = send
        total = add_low(keep, (yield lax.ppermute(send, "dp", pairs)))
        self.sent = total
        for k in range(half - 1):
            moves = on_line([(k, k + 1), (line - 1 - k, line - 2 - k)])
            total = add_low(total, (yield lax.ppermute(total, "dp", moves)))
            self.sent = total
        moves = on_line([(half - 1, half), (half, half - 1)])
        total = add_low(total, (yield lax.ppermute(total, "dp", moves)))
        self.sent = total
        for k in reversed(range(half - 1)):
            moves = on_line([(k + 1, k), (line - 2 - k, line - 1 - k)])
            total = jnp.where((place == k) | (place == line - 1 - k), (yield lax.ppermute(total, "dp", moves)), total)
        got = yield lax.ppermute(total, "dp", pairs)
        self.whole = jnp.concatenate([jnp.where(side == 0, total, got), jnp.where(side == 0, got, total)], axis=0)
        yield None

    def take(self, got):
        self.got = self.steps.send(got)


def step_sums(sums, *others):
    moving = [one for one in sums if one.whole is None]
    res = tied(*[one.got for one in moving], *others)
    for one, got in zip(moving, res):
        one.take(got)
    return res[len(moving) :]


class Layer(NamedTuple):
    q: Any
    kv: Any
    bq: Any
    bkv: Any
    out: Any
    up: Any
    down: Any
    out_far: Any
    up_far: Any
    down_far: Any
    bup_own: Any
    bup_far: Any
    ng: Any
    lb: Any
    counts: Any
    lengths: Any
    shift_own: Any
    shift_far: Any


class Saved(NamedTuple):
    h: Any
    q: Any
    kv: Any
    kvp: Any
    f: Any


def forward_tick(save, slot_of, h, w, beside=()):
    kv = (dot_nn(h, w.kv) + w.bkv).astype(BF)
    kvp = to_peer(kv)
    q = (dot_nn(h, w.q) + w.bq).astype(BF)
    q, *beside = tied(q, *beside) if beside else (q,)
    f = forward_call(save, slot_of, w, q, kv, kvp, h)
    return f.out, Saved(h, q, kv, kvp, f), beside


def backward_end(b, w):
    other = to_peer(b.far)
    from_q = dot_nt(b.dq, w.q)
    dkv = (b.near + other.astype(F32)).astype(BF)
    return (b.d1 + from_q + dot_nt(dkv, w.kv)).astype(BF), b._replace(dkv=dkv)


def backward_tick(slot_of, g, s, w):
    b = Back(*backward_call(ALL, slot_of, w, g, s.f, s.q, s.kv, s.kvp), None)
    return backward_end(b, w)


def cut(x, which, size):
    return lax.slice_in_dim(x, which * size, (which + 1) * size, axis=1)


def on_device(
    tokens,
    grad_out,
    attention_in,
    attention_bias,
    attention_out,
    up_weight,
    up_bias,
    down_weight,
    norm_gains,
    layer_biases,
    block_counts,
    lengths,
    head_shifts,
):
    dp_size = lax.axis_size("dp")
    first = lax.axis_index("section") == 0
    width = tokens.shape[2]
    quarter = tokens.shape[1]
    half = attention_in.shape[3]
    hidden = up_weight.shape[2]

    crossed = [lax.ppermute(jnp.where(first, grad_out[s], tokens[s]), "section", SWAP) for s in range(2)]
    from_rows = lambda x, s: jnp.concatenate([tokens[s], x], axis=0)
    cot_rows = lambda x, s: jnp.concatenate([x, grad_out[s]], axis=0)
    tok0, cot0 = from_rows(crossed[0], 0), cot_rows(crossed[0], 0)
    win, win_far = attention_in[0], to_peer(attention_in[0])
    ab, ab_far = attention_bias[0], to_peer(attention_bias)[0]
    bv = jnp.concatenate([ab[1], ab_far[1]])
    w = Layer(
        q=jnp.concatenate([win[:, 0], win_far[:, 0]], axis=1),
        kv=jnp.concatenate([win[:, 1], win_far[:, 1], win[:, 2], win_far[:, 2]], axis=1),
        bq=jnp.concatenate([ab[0], ab_far[0]]),
        bkv=jnp.concatenate([jnp.zeros_like(bv), bv]),
        out=attention_out[0],
        up=up_weight[0],
        down=down_weight[0],
        out_far=to_peer(attention_out[0]),
        up_far=to_peer(up_weight[0]),
        down_far=to_peer(down_weight[0]),
        bup_own=up_bias,
        bup_far=to_peer(up_bias),
        ng=norm_gains[0],
        lb=layer_biases[0],
        counts=block_counts,
        lengths=lengths,
        shift_own=head_shifts,
        shift_far=to_peer(head_shifts),
    )
    slot_one = lambda s: 0
    slot_a = lambda s: 1 - s
    slot_b = lambda s: s

    out1, _, (crossed1,) = forward_tick(False, slot_one, tok0, w, (crossed[1],))
    tok1, cot1 = from_rows(crossed1, 1), cot_rows(crossed1, 1)
    out2, saved2, _ = forward_tick(True, slot_a, jnp.where(first, tok1, next_section(out1)), w)
    away2 = next_section(out2)
    g3, b3 = backward_tick(slot_a, cot0, saved2, w)
    away2, _ = tied(away2, b3.d1_low)
    out4, saved4, _ = forward_tick(True, slot_b, jnp.where(first, tok0, away2), w)
    g5, b5 = backward_tick(slot_b, jnp.where(first, last_section(g3), cot1), saved4, w)

    early = gradient_call(saved4, b5)
    g6_in = jnp.where(first, last_section(g5), cot0)

    f6 = saved2.f
    d2_low = norm_back(g6_in.astype(F32), f6.n2, f6.inv2[:, :1], w.ng[1]).astype(BF)
    down_far = half_gradient_call(d2_low, f6.act, d2_low, early[0], 1, True)
    down_own = half_gradient_call(down_far, f6.act, d2_low, early[0], 0, True)
    down = Sum(add_low(down_own, to_peer(down_far)), dp_size)
    r6 = backward_call(ROWS, slot_a, w, g6_in, f6, None, None, None, None, (down.sent,))
    b6 = Back(*r6[:6], None, None, None, None)
    up_far = half_gradient_call(b6.d1_low, f6.x1_low, b6.d_pre, early[1], 1, False)
    (up_far,) = step_sums([down], up_far)
    up_in = to_peer(up_far)
    up_own = half_gradient_call(up_far, f6.x1_low, b6.d_pre, early[1], 0, False)
    up = Sum(add_low(up_own, up_in), dp_size)
    quarters = jnp.concatenate([out2[:quarter], out4[:quarter]], axis=0)
    dq, near, far = backward_call(
        HEADS, slot_a, w, None, f6, saved2.q, saved2.kv, saved2.kvp, r6[6], (down.sent, up.sent)
    )
    dq, near, far, quarters = step_sums([down, up], dq, near, far, quarters)
    layer_far = last_section(quarters)
    g6, b6 = backward_end(b6._replace(dq=dq, near=near, far=far), w)
    out_own, out_far, in_own, in_far, small_own, small_far = last_gradient_call(up.sent, saved2, b6, early, b5)
    out_far, in_far, small_far = step_sums([down, up], out_far, in_far, small_far)
    tokens_far = next_section(jnp.concatenate([g5[quarter:], g6[quarter:]], axis=0))
    in_g = add_low(in_own, to_peer(in_far))
    small = small_own + to_peer(small_far)
    out_g = jnp.concatenate(
        [add_low(out_own, to_peer(out_far)), small.astype(BF), jnp.zeros((16, width), BF)], axis=0
    )
    part = lambda x, i: x[i * x.shape[0] // 2 : (i + 1) * x.shape[0] // 2]
    in_a, in_b = Sum(part(in_g, 0), dp_size), Sum(part(in_g, 1), dp_size)
    last = Sum(out_g, dp_size)
    step_sums([down, up, in_a])
    step_sums([up, in_a, in_b])
    (layer_far,) = step_sums([down, in_a, in_b, last], layer_far)
    step_sums([up, in_a, in_b, last])
    (tokens_far,) = step_sums([in_a, in_b, last], tokens_far)
    sums = [down, up, in_a, in_b, last]
    while any(one.whole is None for one in sums):
        step_sums(sums)
    down_s = down.whole.astype(F32)
    up_s = up.whole.astype(F32)
    in_s = jnp.concatenate([in_a.whole, in_b.whole], axis=0).astype(F32)
    out_s = last.whole.astype(F32)
    small = out_s[half : half + 16]

    pair = lambda x, y: jnp.stack([x, y])
    layer_out = jnp.where(first, layer_far.reshape(tokens.shape), pair(out2[quarter:], out4[quarter:]))
    grad_tokens = jnp.where(first, pair(g5[:quarter], g6[:quarter]), tokens_far.reshape(tokens.shape))
    return (
        layer_out,
        grad_tokens,
        in_s.reshape(3, width, half).transpose(1, 0, 2)[None],
        small[8].reshape(1, 2, half),
        out_s[:half][None],
        up_s[None],
        small[6:8].reshape(1, hidden),
        down_s[None],
        small[:2][None],
        small[2:6][None],
    )


def solution(mesh):
    tokens = P("dp", ("section", "mp"), None)
    weights = (
        P("section", None, None, "mp"),
        P("section", None, "mp"),
        P("section", "mp", None),
        P("section", None, "mp"),
        P("section", "mp"),
        P("section", "mp", None),
        P("section", None, None),
        P("section", None, None),
    )
    return jax.shard_map(
        on_device,
        mesh=mesh,
        in_specs=(tokens, tokens) + weights + (P("dp"), P("dp"), P("section", "mp")),
        out_specs=(tokens, tokens) + weights,
        check_vma=False,
    )
```

```python
import functools
import math
from typing import Any, NamedTuple

import jax
import jax.numpy as jnp
from jax import lax
from jax.experimental import pallas as pl
from jax.experimental.pallas import tpu as pltpu
from jax.sharding import PartitionSpec as P

BF = jnp.bfloat16
F32 = jnp.float32
EPS = 1e-05
SHUT = -1e30
TILE = 256
FORWARD_WINDOWS = (512, 528)
BACKWARD_WINDOWS = (528,)
CHUNK = 512
BLOCK = 64
VMEM_BYTES = 58 * 2**20
NO_COST = pl.CostEstimate(flops=1, bytes_accessed=1, transcendentals=0)


def dot_nn(a, b):
    return lax.dot_general(a, b, (((1,), (0,)), ((), ())), preferred_element_type=F32)


def dot_nt(a, b):
    return lax.dot_general(a, b, (((1,), (1,)), ((), ())), preferred_element_type=F32)


def dot_tn(a, b):
    return lax.dot_general(a, b, (((0,), (0,)), ((), ())), preferred_element_type=F32)


def mask_numbers(slot, counts, lengths):
    c = counts[slot]
    n = lengths[slot]
    third = (n + 2) // 3
    th1 = jnp.where(c == 3, third, (n + 1) // 2)
    th2 = jnp.where(c == 3, (2 * n + 2) // 3, 1 << 20)
    return th1, th2, n, c, lax.axis_index("mp")


def key_columns(nums, rows):
    th1, th2, n = nums[:3]
    u = lax.broadcasted_iota(jnp.int32, (rows, 128), 0)
    col = lax.broadcasted_iota(jnp.int32, (rows, 128), 1)
    blk = (u >= th1).astype(jnp.int32) + (u >= th2).astype(jnp.int32)
    open_ = (blk == col) & (u < n)
    one = jnp.where(col < 8, 1.0, 0.0)
    return jnp.where(col < 3, jnp.where(open_, 0.0, SHUT), one).astype(BF)


def query_rows(nums, shift, r0):
    th1, th2, _, c, _ = nums
    pos = r0 + lax.broadcasted_iota(jnp.int32, (16, TILE), 1)
    row = lax.broadcasted_iota(jnp.int32, (16, TILE), 0)
    t = (pos >= th1).astype(jnp.int32) + (pos >= th2).astype(jnp.int32) + shift
    t = jnp.where(t >= c, t - c, t)
    return jnp.where(row == t, 1.0, 0.0), row


def split3(x):
    a = x.astype(BF).astype(F32)
    b = (x - a).astype(BF).astype(F32)
    return a, b, (x - a - b).astype(BF).astype(F32)


def window_need(nums, r0):
    th1, th2, n, c, _ = nums
    last = r0 + TILE - 1
    whole = ((r0 < th1) == (last < th1)) & ((r0 < th2) == (last < th2))
    need = jnp.maximum(th1, jnp.minimum(th2, n) - (th1 // 16) * 16)
    need = jnp.maximum(need, jnp.where(c == 3, n - (th2 // 16) * 16, 0))
    return jnp.where(whole, need, 1 << 20)


def window_base(nums, shift, r0, limit):
    th1, th2, _, c, _ = nums
    t = jnp.where(r0 >= th1, 1, 0) + jnp.where(r0 >= th2, 1, 0) + shift
    t = jnp.where(t >= c, t - c, t)
    start = jnp.where(t == 0, 0, jnp.where(t == 1, th1, th2))
    return pl.multiple_of(jnp.minimum((start // 16) * 16, limit), 16)


def by_window(need, length, windows, body):
    prev = 0
    for width in windows:
        if width < length:

            @pl.when((need > prev) & (need <= width))
            def _(width=width):
                body(width)

            prev = width

    @pl.when(need > prev)
    def _():
        body(length)


def place_rows(dst, lanes, own, far, offset, core):
    pairs = dst.shape[0]
    for i in range(2):
        for who, ref in enumerate((own, far)):
            blk = 2 * i + jnp.where(core == who, 0, 1)
            rows = pl.ds(pl.multiple_of(blk * TILE, TILE), TILE)
            for p in range(pairs):
                src = offset + (p if who == 0 else (p + pairs // 2) % pairs) * 128
                dst[p, rows, lanes] = ref[i * TILE : (i + 1) * TILE, src : src + 128]


def place_values(v0, v1, own, far, offset, core):
    pairs = v0.shape[0]
    lane = lax.broadcasted_iota(jnp.int32, (TILE, 128), 1)
    ones = jnp.ones((TILE, 128), BF)
    for i in range(2):
        for who, ref in enumerate((own, far)):
            blk = 2 * i + jnp.where(core == who, 0, 1)
            rows = pl.ds(pl.multiple_of(blk * TILE, TILE), TILE)
            for p in range(pairs):
                src = offset + (p if who == 0 else (p + pairs // 2) % pairs) * 128
                x = ref[i * TILE : (i + 1) * TILE, src : src + 128]
                v0[p, rows, :] = jnp.where(lane < 64, x, ones)
                v1[p, rows, :] = jnp.where(lane < 64, ones, x)


def head_shift(own, far, j):
    heads = own.shape[1]
    if isinstance(j, int):
        return own[0, j] if j < heads else far[0, j - heads]
    return jnp.where(j < heads, own[0, jnp.minimum(j, heads - 1)], far[0, jnp.maximum(j - heads, 0)])


def attend(nums, shifts, q, kb, v0, v1, score, weight, top, mixed, lse):
    pairs, length = kb.shape[:2]
    th1, th2, _, c, core = nums
    heads = 2 * pairs
    lane = lax.broadcasted_iota(jnp.int32, (TILE, 128), 1)
    sub = lax.broadcasted_iota(jnp.int32, (TILE, 128), 0)

    @pl.loop(0, 2)
    def _(tile):
        r0 = (2 * tile + core) * TILE
        rows = pl.ds(pl.multiple_of(tile * TILE, TILE), TILE)
        behind = ((r0 + sub) >= th1).astype(jnp.int32) + ((r0 + sub) >= th2).astype(jnp.int32) - lane

        def body(width):
            outs = [None] * heads

            def window(j):
                shift = head_shift(*shifts, j)
                return pl.ds(window_base(nums, shift, r0, length - width) if width < length else 0, width)

            def scores(j):
                p, hh = divmod(j, 2)
                qn = q[rows, p * 128 : (p + 1) * 128].astype(F32) * 0.125
                d = behind + head_shift(*shifts, j)
                target = jnp.where((lane < c) & ((d == 0) | (d == c)), 1.0, 0.0)
                qm = jnp.where((lane >= 64) == (hh == 1), qn, 0.0)
                lhs = jnp.concatenate([qm.astype(BF), target.astype(BF)], axis=1)
                score[j % 2, :, 0:width] = dot_nt(lhs, kb[p, window(j), :])

            def softmax(j):
                for r in range(0, TILE, 128):
                    part = score[j % 2, r : r + 128, 0:width]
                    largest = jnp.max(part, axis=1, keepdims=True)
                    top[j % 4, r : r + 128, :] = jnp.broadcast_to(largest, (128, 128))
                    weight[j % 2, r : r + 128, 0:width] = jnp.exp(part - largest).astype(BF)

            def product(j):
                p, hh = divmod(j, 2)
                outs[j] = dot_nn(weight[j % 2, :, 0:width], (v0, v1)[hh][p, window(j), :])
                if hh == 1:
                    total = jnp.where(lane < 64, pltpu.roll(outs[j - 1], 64, 1), pltpu.roll(outs[j], 64, 1))
                    value = jnp.where(lane < 64, outs[j - 1], outs[j])
                    mixed[rows, p * 128 : (p + 1) * 128] = (value / total).astype(BF)
                    if lse is not None:
                        both = (jnp.where(lane < 64, top[(j - 1) % 4], top[j % 4]) + jnp.log(total)).T
                        lse[p, 0:1, rows] = both[0:1]
                        lse[p, 1:2, rows] = both[64:65]

            for step in range(heads + 2):
                if step < heads:
                    scores(step)
                if 1 <= step <= heads:
                    softmax(step - 1)
                if step >= 2:
                    product(step - 2)

        by_window(window_need(nums, r0), length, FORWARD_WINDOWS, body)


def attend_back(nums, shifts, q, do, mixed, lse, kb, vb, dka, dva, dq):
    pairs, length = kb.shape[:2]
    core = nums[4]
    sub = lax.broadcasted_iota(jnp.int32, (128, TILE), 0)
    lane = lax.broadcasted_iota(jnp.int32, (TILE, 128), 1)
    for tile in range(2):
        r0 = (2 * tile + core) * TILE
        rows = slice(tile * TILE, (tile + 1) * TILE)

        def body(width):
            @pl.loop(0, pairs, unroll=2)
            def _(p):
                lanes = pl.ds(pl.multiple_of(p * 128, 128), 128)
                qn = q[rows, lanes].astype(F32) * 0.125
                don = do[rows, lanes].astype(F32)
                qt = qn.T
                dot_ = don.T
                prod = dot_ * mixed[rows, lanes].astype(F32).T
                outs = []
                for hh in range(2):
                    shift = head_shift(*shifts, 2 * p + hh)
                    target, row = query_rows(nums, shift, r0)
                    la, lb, lc = split3(-lse[p, hh : hh + 1, rows])
                    target = target + jnp.where(row == 3, la, jnp.where(row == 4, lb, jnp.where(row == 5, lc, 0.0)))
                    keep = (sub >= 64) == (hh == 1)
                    zeros = jnp.zeros((112, TILE), BF)
                    rhs = jnp.concatenate([jnp.where(keep, qt, 0.0).astype(BF), target.astype(BF), zeros], axis=0)
                    da, db, dc = split3(-jnp.sum(prod[hh * 64 : (hh + 1) * 64], axis=0, keepdims=True))
                    minus = jnp.where(row == 3, da, jnp.where(row == 4, db, jnp.where(row == 5, dc, 0.0)))
                    rhs2 = jnp.concatenate([jnp.where(keep, dot_, 0.0).astype(BF), minus.astype(BF), zeros], axis=0)
                    keepl = (lane >= 64) == (hh == 1)
                    qm = jnp.where(keepl, qn, 0.0).astype(BF)
                    dom = jnp.where(keepl, don, 0.0).astype(BF)
                    start = window_base(nums, shift, r0, length - width) if width < length else 0
                    win = pl.ds(start, width)
                    kwin = kb[p, win, :]
                    pt = jnp.exp(dot_nn(kwin, rhs))
                    ds = (pt * dot_nn(vb[p, win, :], rhs2)).astype(BF)
                    dva[p, win, :] += dot_nn(pt.astype(BF), dom)
                    dka[p, win, :] += dot_nn(ds, qm)
                    kt = kwin[:, 0:128].T[hh * 64 : (hh + 1) * 64]
                    outs.append(dot_nn(kt, ds))
                dq[rows, lanes] = (jnp.concatenate(outs, axis=0) * 0.125).T.astype(BF)

        by_window(window_need(nums, r0), length, BACKWARD_WINDOWS, body)


def gelu_pair(x):
    density = jnp.exp(x * x * (-0.5)) * (2.0 * math.pi) ** (-0.5)
    cdf = 0.5 + 0.5 * lax.erf(x * (2.0 ** (-0.5)))
    return x * cdf, cdf + x * density


def norm_rows(x):
    scale = 1.0 / x.shape[-1]
    centred = x - jnp.sum(x, axis=-1, keepdims=True) * scale
    inv = lax.rsqrt(jnp.sum(centred * centred, axis=-1, keepdims=True) * scale + EPS)
    return centred * inv, inv


def norm_back(up, normed, inv, gain):
    scale = 1.0 / normed.shape[-1]
    e = up * gain
    a = jnp.sum(e, axis=-1, keepdims=True) * scale
    b = jnp.sum(e * normed, axis=-1, keepdims=True) * scale
    return inv * (e - a - normed * b)


def copier(sems):
    used = [0]

    def start(src, dst):
        copy = pltpu.make_async_copy(src, dst, sems.at[used[0]])
        used[0] += 1
        copy.start()
        return copy

    return start


class ForwardIn(NamedTuple):
    q: Any
    kv: Any
    kvp: Any
    h: Any
    wout: Any
    wup: Any
    wdown: Any
    wout_far: Any
    wup_far: Any
    wdown_far: Any


class ForwardOut(NamedTuple):
    out: Any
    mixed: Any
    lse: Any
    x1_low: Any
    act: Any
    slope: Any
    n1: Any
    inv1: Any
    n2: Any
    inv2: Any


class ForwardWork(NamedTuple):
    kb: Any
    v0: Any
    v1: Any
    score: Any
    weight: Any
    top: Any
    pre: Any
    x1: Any
    acc: Any


def weight_copies(start, src, x):
    c_out, c_up, c_down = [], [], []
    for j, (out, up, down) in enumerate(((src.wout, src.wup, src.wdown), (src.wout_far, src.wup_far, src.wdown_far))):
        rows, cols = out.shape[0], up.shape[1]
        c_out.append(start(out, x.wout.at[j * rows : (j + 1) * rows, :]))
        c_up.append(start(up, x.wup.at[:, j * cols : (j + 1) * cols]))
        c_down.append(start(down, x.wdown.at[j * cols : (j + 1) * cols, :]))
    return c_out, c_up, c_down


def forward_kernel(save, slot_of, tokens, counts, lengths, shift_own, shift_far, lb, ng, bup_own, bup_far, *refs):
    refs = list(refs[tokens:])
    take = lambda kind: kind(*[refs.pop(0) for _ in range(len(kind._fields))])
    src = take(ForwardIn)
    dst = take(ForwardOut) if save else ForwardOut(refs.pop(0), *[None] * 9)
    x = ForwardIn(*[refs.pop(0) for _ in range(7)], None, None, None)
    y = take(ForwardOut)
    t = take(ForwardWork)
    start = copier(refs[0])
    rows, width = x.h.shape
    hidden = x.wup.shape[1]
    half = hidden // 2
    load = ForwardIn(*[None] * 10)._replace(
        kv=start(src.kv, x.kv),
        kvp=start(src.kvp, x.kvp),
        q=start(src.q, x.q),
        h=start(src.h, x.h),
    )
    c_out, c_up, c_down = weight_copies(start, src, x)
    done = []

    def ship(a, b):
        if b is not None:
            done.append(start(a, b))

    def ship_part(a, b, part):
        if b is not None:
            done.append(start(a.at[:, part], b.at[:, part]))

    nums = mask_numbers(slot_of(lax.axis_index("section")), counts, lengths)
    core = nums[4]
    ext = key_columns(nums, t.kb.shape[1])
    for p in range(t.kb.shape[0]):
        t.kb[p, :, 128:256] = ext
    load.kv.wait()
    load.kvp.wait()
    place_rows(t.kb, slice(0, 128), x.kv, x.kvp, 0, core)
    place_values(t.v0, t.v1, x.kv, x.kvp, width, core)
    load.q.wait()
    attend(
        nums, (shift_own, shift_far), x.q, t.kb, t.v0, t.v1, t.score, t.weight, t.top, y.mixed, y.lse if save else None
    )
    ship(y.mixed, dst.mixed)
    ship(y.lse, dst.lse)
    for copy in c_out:
        copy.wait()
    t.acc[...] = dot_nn(y.mixed[...], x.wout[...])
    load.h.wait()
    for r in range(0, rows, BLOCK):
        rs = slice(r, r + BLOCK)
        normed, inv = norm_rows(x.h[rs, :].astype(F32) + t.acc[rs, :] + lb[0:1, :])
        if save:
            y.n1[rs, :] = normed.astype(BF)
            y.inv1[rs, :] = jnp.broadcast_to(inv, (BLOCK, 128))
        full = normed * ng[0:1, :] + lb[1:2, :]
        t.x1[rs, :] = full
        y.x1_low[rs, :] = full.astype(BF)
    ship(y.x1_low, dst.x1_low)
    ship(y.n1, dst.n1)
    ship(y.inv1, dst.inv1)
    chunks = hidden // CHUNK

    def up(j):
        t.pre[j % 2] = dot_nn(y.x1_low[...], x.wup[:, j * CHUNK : (j + 1) * CHUNK])

    def activate(j):
        part = slice(j * CHUNK, (j + 1) * CHUNK)
        low = (j * CHUNK) % half
        bias = (bup_own if j < chunks // 2 else bup_far)[0:1, low : low + CHUNK]
        for r in range(0, rows, BLOCK):
            rs = slice(r, r + BLOCK)
            act, slope = gelu_pair(t.pre[j % 2, rs, :] + bias)
            y.act[rs, part] = act.astype(BF)
            if save:
                y.slope[rs, part] = slope.astype(BF)

    c_up[0].wait()
    up(0)
    for j in range(chunks // 2):
        if j + 1 == chunks // 2:
            c_up[1].wait()
        up(j + 1)
        activate(j)
    ship_part(y.act, dst.act, slice(0, half))
    ship_part(y.slope, dst.slope, slice(0, half))
    c_down[0].wait()
    t.acc[...] = dot_nn(y.act[:, :half], x.wdown[:half, :])
    for j in range(chunks // 2, chunks):
        if j + 1 < chunks:
            up(j + 1)
        activate(j)
    ship_part(y.act, dst.act, slice(half, hidden))
    ship_part(y.slope, dst.slope, slice(half, hidden))
    c_down[1].wait()
    t.acc[...] += dot_nn(y.act[:, half:], x.wdown[half:, :])
    for r in range(0, rows, BLOCK):
        rs = slice(r, r + BLOCK)
        normed, inv = norm_rows(t.x1[rs, :] + t.acc[rs, :] + lb[2:3, :])
        if save:
            y.n2[rs, :] = normed.astype(BF)
            y.inv2[rs, :] = jnp.broadcast_to(inv, (BLOCK, 128))
        y.out[rs, :] = (normed * ng[1:2, :] + lb[3:4, :]).astype(BF)
    ship(y.out, dst.out)
    ship(y.n2, dst.n2)
    ship(y.inv2, dst.inv2)
    for copy in done:
        copy.wait()


def buffers(shapes):
    return [pltpu.VMEM(*s) for s in shapes]


def results(shapes):
    return tuple(jax.ShapeDtypeStruct(*s) for s in shapes)


IN_SMEM = pl.BlockSpec(memory_space=pltpu.SMEM)
IN_VMEM = pl.BlockSpec(memory_space=pltpu.VMEM)
IN_HBM = pl.BlockSpec(memory_space=pltpu.HBM)


def forward_call(save, slot_of, w, q, kv, kvp, h, tokens=()):
    rows, width = h.shape
    hidden = 2 * w.up.shape[1]
    pairs, length = width // 128, 2 * rows
    low, wide, full = ((rows, width), BF), ((rows, hidden), BF), ((rows, width), F32)
    one, twice = ((rows, 128), F32), ((rows, 2 * width), BF)
    shapes_in = (low, twice, twice, low, ((width, width), BF), ((width, hidden), BF), ((hidden, width), BF))
    shapes_out = ForwardOut(low, low, ((pairs, 2, rows), F32), low, wide, wide, low, one, low, one)
    if not save:
        gone = ((16, 128), BF)
        scratch_out = shapes_out._replace(lse=gone, slope=gone, n1=gone, inv1=gone, n2=gone, inv2=gone)
    else:
        scratch_out = shapes_out
    work = ForwardWork(
        ((pairs, length, 256), BF),
        ((pairs, length, 128), BF),
        ((pairs, length, 128), BF),
        ((2, TILE, length), F32),
        ((2, TILE, length), BF),
        ((4, TILE, 128), F32),
        ((2, rows, CHUNK), F32),
        full,
        full,
    )
    outs = shapes_out if save else shapes_out[:1]
    res = pl.pallas_call(
        functools.partial(forward_kernel, save, slot_of, len(tokens)),
        out_shape=results(outs),
        in_specs=[IN_SMEM] * 4 + [IN_VMEM] * 4 + [IN_HBM] * (10 + len(tokens)),
        out_specs=(IN_HBM,) * len(outs),
        scratch_shapes=buffers(shapes_in) + buffers(scratch_out) + buffers(work) + [pltpu.SemaphoreType.DMA((24,))],
        compiler_params=pltpu.CompilerParams(vmem_limit_bytes=VMEM_BYTES),
        cost_estimate=NO_COST,
        name="layer_forward",
    )(
        w.counts, w.lengths, w.shift_own, w.shift_far, w.lb, w.ng, w.bup_own, w.bup_far, *tokens,
        q, kv, kvp, h, w.out, w.up, w.down, w.out_far, w.up_far, w.down_far,
    )
    return ForwardOut(*res) if save else ForwardOut(res[0], *[None] * 9)


class RowsIn(NamedTuple):
    g: Any
    n2: Any
    inv2: Any
    n1: Any
    inv1: Any
    slope: Any
    wout: Any
    wup: Any
    wdown: Any
    wout_far: Any
    wup_far: Any
    wdown_far: Any


class RowsOut(NamedTuple):
    d2_low: Any
    d_pre: Any
    d1_low: Any


class HeadsIn(NamedTuple):
    mixed: Any
    lse: Any
    q: Any
    kv: Any
    kvp: Any


class HeadsOut(NamedTuple):
    dq: Any
    near: Any
    far: Any


class HeadsWork(NamedTuple):
    kb: Any
    vb: Any
    dka: Any
    dva: Any


def rows_back(start, src, dst, x, y, d_mixed, dx, ng, sums, bias_sums, behind, up_refs):
    rows, width = x.g.shape
    hidden = x.wup.shape[1]
    half = hidden // 2
    chunks = hidden // CHUNK
    soon = [start(src.g, x.g), start(src.n2, x.n2), start(src.inv2, x.inv2)]
    c_slope = [
        start(src.slope.at[:, part], x.slope.at[:, part]) for part in (slice(0, half), slice(half, hidden))
    ]
    c_out, c_up, c_down = weight_copies(start, src, x)
    late = [start(src.n1, x.n1), start(src.inv1, x.inv1)]
    if up_refs:
        x1_h, early_h, outs_h, x1, early, outs = up_refs
        up_load = [start(x1_h, x1), start(early_h, early)]
    behind()
    done = []
    zero = jnp.zeros((1, width), F32)
    s_gn, s_g, s_d2 = zero, zero, zero
    for copy in soon:
        copy.wait()
    for r in range(0, rows, BLOCK):
        rs = slice(r, r + BLOCK)
        g = x.g[rs, :].astype(F32)
        normed = x.n2[rs, :].astype(F32)
        d2 = norm_back(g, normed, x.inv2[rs, 0:1], ng[1:2, :])
        dx[rs, :] = d2
        y.d2_low[rs, :] = d2.astype(BF)
        s_gn += jnp.sum(g * normed, axis=0, keepdims=True)
        s_g += jnp.sum(g, axis=0, keepdims=True)
        s_d2 += jnp.sum(d2, axis=0, keepdims=True)
    done.append(start(y.d2_low, dst.d2_low))
    for k in range(2):
        c_down[k].wait()
        c_slope[k].wait()
        for j in range(k * chunks // 2, (k + 1) * chunks // 2):
            part = slice(j * CHUNK, (j + 1) * CHUNK)
            d_act = dot_nt(y.d2_low[...], x.wdown[part, :])
            d_pre = (d_act * x.slope[:, part].astype(F32)).astype(BF)
            y.d_pre[:, part] = d_pre
            bias_sums[0:1, part] = jnp.sum(d_pre.astype(F32), axis=0, keepdims=True)
        part = slice(k * half, (k + 1) * half)
        done.append(start(y.d_pre.at[:, part], dst.d_pre.at[:, part]))
        c_up[k].wait()
        dx[...] += dot_nt(y.d_pre[:, part], x.wup[:, part])
    def up_gradient(k):
        if up_refs:
            for j in range(2):
                to = slice(j * half // 2, (j + 1) * half // 2)
                at = slice(k * half + j * half // 2, k * half + (j + 1) * half // 2)
                outs[k][:, to] = (dot_tn(x1[...], y.d_pre[:, at]) + early[:, at].astype(F32)).astype(BF)
            done.append(start(outs[k], outs_h[k]))

    if up_refs:
        for copy in up_load:
            copy.wait()
    up_gradient(1)
    s_dn, s_dx, s_d1 = zero, zero, zero
    late[0].wait()
    late[1].wait()
    for r in range(0, rows, BLOCK):
        rs = slice(r, r + BLOCK)
        g = dx[rs, :]
        normed = x.n1[rs, :].astype(F32)
        d1 = norm_back(g, normed, x.inv1[rs, 0:1], ng[0:1, :])
        y.d1_low[rs, :] = d1.astype(BF)
        s_dn += jnp.sum(g * normed, axis=0, keepdims=True)
        s_dx += jnp.sum(g, axis=0, keepdims=True)
        s_d1 += jnp.sum(d1, axis=0, keepdims=True)
    done.append(start(y.d1_low, dst.d1_low))
    for i, s in enumerate((s_dn, s_gn, s_d1, s_dx, s_d2, s_g)):
        sums[i : i + 1, :] = s
    sums[6:8, :] = jnp.zeros((2, width), F32)
    for copy in c_out:
        copy.wait()
    d_mixed[...] = dot_nt(y.d1_low[...], x.wout[...]).astype(BF)
    up_gradient(0)
    return done


def heads_back(start, load, dst, x, y, t, d_mixed, nums, shifts):
    width = x.q.shape[1]
    core = nums[4]
    pairs = t.kb.shape[0]
    ext = key_columns(nums, t.kb.shape[1])
    for p in range(pairs):
        t.kb[p, :, 128:256] = ext
        t.vb[p, :, 128:256] = ext
    for copy in load:
        copy.wait()
    place_rows(t.kb, slice(0, 128), x.kv, x.kvp, 0, core)
    place_rows(t.vb, slice(0, 128), x.kv, x.kvp, width, core)
    t.dka[...] = jnp.zeros_like(t.dka)
    t.dva[...] = jnp.zeros_like(t.dva)
    attend_back(nums, shifts, x.q, d_mixed, x.mixed, x.lse, t.kb, t.vb, t.dka, t.dva, y.dq)
    done = [start(y.dq, dst.dq)]
    for to, side, turn in ((y.far, 1 - core, pairs // 2), (y.near, core, 0)):
        for i in range(2):
            mine = pl.ds(pl.multiple_of((2 * i + side) * TILE, TILE), TILE)
            for p in range(pairs):
                for j, total in enumerate((t.dka, t.dva)):
                    lanes = slice(j * width + p * 128, j * width + (p + 1) * 128)
                    to[i * TILE : (i + 1) * TILE, lanes] = total[(p + turn) % pairs, mine, :].astype(to.dtype)
    done += [start(y.far, dst.far), start(y.near, dst.near)]
    return done


ALL, ROWS, HEADS = 3, 1, 2


def backward_kernel(which, slot_of, tokens, counts, lengths, shift_own, shift_far, ng, *refs):
    refs = list(refs[tokens:])
    take = lambda kind: kind(*[refs.pop(0) for _ in range(len(kind._fields))])
    rows_on, heads_on = which & ROWS, which & HEADS
    if rows_on:
        r_src = take(RowsIn)
    if heads_on:
        h_src = take(HeadsIn)
    if which == HEADS:
        mixed_src = refs.pop(0)
    if which == ROWS:
        up_refs = [refs.pop(0), refs.pop(0)]
    if rows_on:
        r_dst = take(RowsOut)
        sums, bias_sums = refs.pop(0), refs.pop(0)
    if which == ROWS:
        mixed_dst = refs.pop(0)
        up_refs.append([refs.pop(0), refs.pop(0)])
    if heads_on:
        h_dst = take(HeadsOut)
    d_mixed = refs.pop(0)
    if rows_on:
        r_x = RowsIn(*[refs.pop(0) for _ in range(9)], None, None, None)
        r_y, dx = take(RowsOut), refs.pop(0)
    if which == ROWS:
        up_refs += [refs.pop(0), refs.pop(0), [refs.pop(0), refs.pop(0)]]
    if heads_on:
        h_x, h_y, h_t = take(HeadsIn), take(HeadsOut), take(HeadsWork)
    start = copier(refs[0])
    load, done = [], []

    def load_heads():
        if heads_on:
            load.extend(start(a, b) for a, b in zip(h_src, h_x))

    if rows_on:
        up_refs = up_refs if which == ROWS else None
        done += rows_back(start, r_src, r_dst, r_x, r_y, d_mixed, dx, ng, sums, bias_sums, load_heads, up_refs)
    else:
        load_heads()
        load.append(start(mixed_src, d_mixed))
    if which == ROWS:
        done.append(start(d_mixed, mixed_dst))
    if heads_on:
        nums = mask_numbers(slot_of(lax.axis_index("section")), counts, lengths)
        done += heads_back(start, load, h_dst, h_x, h_y, h_t, d_mixed, nums, (shift_own, shift_far))
    for copy in done:
        copy.wait()


def gradient_kernel(*refs):
    refs = list(refs)
    src = [refs.pop(0) for _ in range(9)]
    dst = [refs.pop(0) for _ in range(5)]
    col_sums = refs.pop(0)
    x = [refs.pop(0) for _ in range(9)]
    y = [refs.pop(0) for _ in range(5)]
    start = copier(refs[0])
    load = [start(a, b) for a, b in zip(src, x)]
    done = []
    act, d2_low, x1_low, d_pre, mixed, d1_low, h, dq, dkv = range(9)
    for k, (left, right) in enumerate(((act, d2_low), (x1_low, d_pre), (mixed, d1_low), (h, dq), (h, dkv))):
        for i in (left, right):
            if load[i] is not None:
                load[i].wait()
                load[i] = None
        tall, broad = y[k].shape
        slab = CHUNK if max(tall, broad) % CHUNK == 0 else TILE
        for j in range(max(tall, broad) // slab):
            part = slice(j * slab, (j + 1) * slab)
            if tall > broad:
                y[k][part, :] = dot_tn(x[left][:, part], x[right][...]).astype(BF)
                done.append(start(y[k].at[part, :], dst[k].at[part, :]))
            else:
                y[k][:, part] = dot_tn(x[left][...], x[right][:, part]).astype(BF)
                done.append(start(y[k].at[:, part], dst[k].at[:, part]))
    width = x[h].shape[1]
    col_sums[0:1, :] = jnp.sum(x[dq][...].astype(F32), axis=0, keepdims=True)
    col_sums[1:2, :] = jnp.sum(x[dkv][:, width:].astype(F32), axis=0, keepdims=True)
    for copy in done:
        copy.wait()


def gradient_call(s, b):
    f = s.f
    rows, width = s.h.shape
    hidden = f.act.shape[1]
    args = (f.act, b.d2_low, f.x1_low, b.d_pre, f.mixed, b.d1_low, s.h, b.dq, b.dkv)
    shapes = [
        ((hidden, width), BF), ((width, hidden), BF), ((width, width), BF), ((width, width), BF), ((width, 2 * width), BF),
    ]
    return pl.pallas_call(
        gradient_kernel,
        out_shape=results(shapes + [((2, width), F32)]),
        in_specs=[IN_HBM] * 9,
        out_specs=(IN_HBM,) * 5 + (IN_VMEM,),
        scratch_shapes=buffers([(a.shape, BF) for a in args]) + buffers(shapes) + [pltpu.SemaphoreType.DMA((40,))],
        compiler_params=pltpu.CompilerParams(vmem_limit_bytes=VMEM_BYTES),
        cost_estimate=NO_COST,
        name="layer_gradient",
    )(*args)


def half_gradient_kernel(k, by_rows, token, left_h, right_h, early_h, out_h, left, right, early, out, sems):
    start = copier(sems)
    tall, broad = out.shape
    if by_rows:
        load = [start(left_h.at[:, k * tall : (k + 1) * tall], left), start(right_h, right)]
        before = start(early_h.at[k * tall : (k + 1) * tall, :], early)
    else:
        load = [start(left_h, left), start(right_h.at[:, k * broad : (k + 1) * broad], right)]
        before = start(early_h.at[:, k * broad : (k + 1) * broad], early)
    for copy in load:
        copy.wait()
    before.wait()
    done = []
    for j in range(2):
        if by_rows:
            part = slice(j * tall // 2, (j + 1) * tall // 2)
            out[part, :] = (dot_tn(left[:, part], right[...]) + early[part, :].astype(F32)).astype(BF)
            done.append(start(out.at[part, :], out_h.at[part, :]))
        else:
            part = slice(j * broad // 2, (j + 1) * broad // 2)
            out[:, part] = (dot_tn(left[...], right[:, part]) + early[:, part].astype(F32)).astype(BF)
            done.append(start(out.at[:, part], out_h.at[:, part]))
    for copy in done:
        copy.wait()


def half_gradient_call(token, left, right, early, k, by_rows):
    rows = left.shape[0]
    tall, broad = early.shape
    tall, broad = (tall // 2, broad) if by_rows else (tall, broad // 2)
    out = ((tall, broad), BF)
    return pl.pallas_call(
        functools.partial(half_gradient_kernel, k, by_rows),
        out_shape=jax.ShapeDtypeStruct(*out),
        in_specs=[IN_HBM] * 4,
        out_specs=IN_HBM,
        scratch_shapes=buffers([((rows, tall), BF), ((rows, broad), BF), out, out]) + [pltpu.SemaphoreType.DMA((5,))],
        compiler_params=pltpu.CompilerParams(vmem_limit_bytes=VMEM_BYTES),
        cost_estimate=NO_COST,
        name="half_gradient",
    )(token, left, right, early)


def last_gradient_kernel(*refs):
    token, mixed_h, d1_h, h_h, dq_h, dkv_h, eo_h, eq_h, ekv_h, c5, s5, s6, u5, u6, *refs = refs
    outs, refs = refs[:4], refs[4:]
    small_own, small_far, mixed, d1, h, dq, dkv, eo, eq, ekv, oo, fo, oi, fi, sems = refs
    start = copier(sems)
    pairs = ((h_h, h), (dq_h, dq), (eq_h, eq), (dkv_h, dkv), (ekv_h, ekv), (mixed_h, mixed), (d1_h, d1), (eo_h, eo))
    load = [start(a, b) for a, b in pairs]
    width = h.shape[1]
    half = width // 2
    done = []
    for copy in load[:5]:
        copy.wait()
    for k, to, away in ((1, fi, outs[3]), (0, oi, outs[2])):
        for part in range(3):
            right, before, at = ((dq, eq, 0), (dkv, ekv, 0), (dkv, ekv, width))[part]
            lanes = slice(at + k * half, at + (k + 1) * half)
            total = dot_tn(h[...], right[:, lanes]) + before[:, lanes].astype(F32)
            to[part * width : (part + 1) * width, :] = total.astype(BF)
        done.append(start(to, away))
    for copy in load[5:]:
        copy.wait()
    for k, to, away in ((1, fo, outs[1]), (0, oo, outs[0])):
        lanes = slice(k * half, (k + 1) * half)
        to[...] = (dot_tn(mixed[:, lanes], d1[...]) + eo[lanes, :].astype(F32)).astype(BF)
        done.append(start(to, away))
    qb = c5[0:1, :] + jnp.sum(dq[...].astype(F32), axis=0, keepdims=True)
    vb = c5[1:2, :] + jnp.sum(dkv[:, width:].astype(F32), axis=0, keepdims=True)
    ub = u5[...] + u6[...]
    for k, to in ((0, small_own), (1, small_far)):
        to[...] = jnp.zeros_like(to)
        to[0:6, :] = s5[0:6, :] + s6[0:6, :]
        for j in range(2):
            to[6 + j : 7 + j, :] = ub[:, (2 * k + j) * width : (2 * k + j + 1) * width]
        to[8:9, :half] = qb[:, k * half : (k + 1) * half]
        to[8:9, half:] = vb[:, k * half : (k + 1) * half]
    for copy in done:
        copy.wait()


def last_gradient_call(token, s, b, early, b5):
    rows, width = s.h.shape
    half = width // 2
    args = (s.f.mixed, b.d1_low, s.h, b.dq, b.dkv, early[2], early[3], early[4])
    shapes = [((half, width), BF), ((half, width), BF), ((3 * width, half), BF), ((3 * width, half), BF)]
    return pl.pallas_call(
        last_gradient_kernel,
        out_shape=results(shapes + [((16, width), F32)] * 2),
        in_specs=[IN_HBM] * 9 + [IN_VMEM] * 5,
        out_specs=(IN_HBM,) * 4 + (IN_VMEM,) * 2,
        scratch_shapes=buffers([(a.shape, BF) for a in args]) + buffers(shapes) + [pltpu.SemaphoreType.DMA((16,))],
        compiler_params=pltpu.CompilerParams(vmem_limit_bytes=VMEM_BYTES),
        cost_estimate=NO_COST,
        name="last_gradient",
    )(token, *args, early[5], b5.sums, b.sums, b5.bias_sums, b.bias_sums)


class Back(NamedTuple):
    d2_low: Any
    d_pre: Any
    d1_low: Any
    sums: Any
    bias_sums: Any
    dq: Any
    near: Any
    far: Any
    dkv: Any


def backward_call(which, slot_of, w, g, f, q, kv, kvp, d_mixed=None, tokens=(), early=None):
    rows, width = f.n1.shape
    hidden = 2 * w.up.shape[1]
    pairs, length = width // 128, 2 * rows
    low, wide, full = ((rows, width), BF), ((rows, hidden), BF), ((rows, width), F32)
    one = ((rows, 128), F32)
    twice = ((rows, 2 * width), BF)
    r_in = (low, low, one, low, one, wide, ((width, width), BF), ((width, hidden), BF), ((hidden, width), BF))
    r_out = RowsOut(low, wide, low)
    h_in = HeadsIn(low, ((pairs, 2, rows), F32), low, twice, twice)
    h_out = HeadsOut(low, twice, twice)
    h_work = HeadsWork(*[((pairs, length, 256), BF)] * 2, *[((pairs, length, 128), F32)] * 2)
    args, outs, out_specs, scratch = [], [], [], [low]
    if which & ROWS:
        args += [g, f.n2, f.inv2, f.n1, f.inv1, f.slope, w.out, w.up, w.down, w.out_far, w.up_far, w.down_far]
        outs += list(r_out) + [((8, width), F32), ((1, hidden), F32)]
        out_specs += [IN_HBM] * len(r_out) + [IN_VMEM] * 2
        scratch += list(r_in) + list(r_out) + [full]
    if which & HEADS:
        args += [f.mixed, f.lse, q, kv, kvp]
        scratch += list(h_in) + list(h_out) + list(h_work)
    if which == HEADS:
        args.append(d_mixed)
    if which == ROWS:
        half_up = ((width, hidden // 2), BF)
        args += [f.x1_low, early]
        outs += [low, half_up, half_up]
        out_specs += [IN_HBM] * 3
        scratch += [low, ((width, hidden), BF), half_up, half_up]
    if which & HEADS:
        outs += list(h_out)
        out_specs += [IN_HBM] * len(h_out)
    return pl.pallas_call(
        functools.partial(backward_kernel, which, slot_of, len(tokens)),
        out_shape=results(outs),
        in_specs=[IN_SMEM] * 4 + [IN_VMEM] + [IN_HBM] * (len(tokens) + len(args)),
        out_specs=tuple(out_specs),
        scratch_shapes=buffers(scratch) + [pltpu.SemaphoreType.DMA((32,))],
        compiler_params=pltpu.CompilerParams(vmem_limit_bytes=VMEM_BYTES),
        cost_estimate=NO_COST,
        name="layer_backward",
    )(w.counts, w.lengths, w.shift_own, w.shift_far, w.ng, *tokens, *args)


SWAP = [(0, 1), (1, 0)]


def to_peer(x):
    return lax.ppermute(x, "mp", SWAP)


def next_section(x):
    return lax.ppermute(x, "section", [(0, 1)])


def last_section(x):
    return lax.ppermute(x, "section", [(1, 0)])


def add_low(a, b):
    return (a.astype(F32) + b.astype(F32)).astype(BF)


def gate_kernel(*refs):
    pass


def tied(*xs):
    hbm = pl.BlockSpec(memory_space=pl.ANY)
    return pl.pallas_call(
        gate_kernel,
        out_shape=tuple(jax.ShapeDtypeStruct(x.shape, x.dtype) for x in xs),
        in_specs=[hbm] * len(xs),
        out_specs=(hbm,) * len(xs),
        input_output_aliases={i: i for i in range(len(xs))},
        cost_estimate=NO_COST,
        name="gate",
    )(*xs)


class Sum:
    def __init__(self, x, size):
        self.whole = None
        if size < 4 or size % 4:
            self.whole = self.sent = lax.psum(x, "dp")
            return
        self.size = size
        self.steps = self.walk(x)
        self.got = next(self.steps)

    def walk(self, x):
        size = self.size
        line = size // 2
        half = line // 2
        me = lax.axis_index("dp")
        side = lax.rem(me, 2)
        place = me // 2
        pairs = [(i, i ^ 1) for i in range(size)]
        on_line = lambda moves: [(2 * a + s, 2 * b + s) for a, b in moves for s in range(2)]
        rows = x.shape[0] // 2
        x = x.reshape((2, rows) + x.shape[1:])
        keep = lax.dynamic_index_in_dim(x, side, 0, keepdims=False)
        send = lax.dynamic_index_in_dim(x, 1 - side, 0, keepdims=False)
        self.sent = send
        total = add_low(keep, (yield lax.ppermute(send, "dp", pairs)))
        self.sent = total
        for k in range(half - 1):
            moves = on_line([(k, k + 1), (line - 1 - k, line - 2 - k)])
            total = add_low(total, (yield lax.ppermute(total, "dp", moves)))
            self.sent = total
        moves = on_line([(half - 1, half), (half, half - 1)])
        total = add_low(total, (yield lax.ppermute(total, "dp", moves)))
        self.sent = total
        for k in reversed(range(half - 1)):
            moves = on_line([(k + 1, k), (line - 2 - k, line - 1 - k)])
            total = jnp.where((place == k) | (place == line - 1 - k), (yield lax.ppermute(total, "dp", moves)), total)
        got = yield lax.ppermute(total, "dp", pairs)
        self.whole = jnp.concatenate([jnp.where(side == 0, total, got), jnp.where(side == 0, got, total)], axis=0)
        yield None

    def take(self, got):
        self.got = self.steps.send(got)


def step_sums(sums, *others):
    moving = [one for one in sums if one.whole is None]
    res = tied(*[one.got for one in moving], *others)
    for one, got in zip(moving, res):
        one.take(got)
    return res[len(moving) :]


class Layer(NamedTuple):
    q: Any
    kv: Any
    bq: Any
    bkv: Any
    out: Any
    up: Any
    down: Any
    out_far: Any
    up_far: Any
    down_far: Any
    bup_own: Any
    bup_far: Any
    ng: Any
    lb: Any
    counts: Any
    lengths: Any
    shift_own: Any
    shift_far: Any


class Saved(NamedTuple):
    h: Any
    q: Any
    kv: Any
    kvp: Any
    f: Any


def forward_tick(save, slot_of, h, w):
    kv = (dot_nn(h, w.kv) + w.bkv).astype(BF)
    kvp = to_peer(kv)
    q = (dot_nn(h, w.q) + w.bq).astype(BF)
    f = forward_call(save, slot_of, w, q, kv, kvp, h)
    return f.out, Saved(h, q, kv, kvp, f)


def backward_end(b, w):
    other = to_peer(b.far)
    from_q = dot_nt(b.dq, w.q)
    dkv = add_low(b.near, other)
    return (b.d1_low.astype(F32) + from_q + dot_nt(dkv, w.kv)).astype(BF), b._replace(dkv=dkv)


def backward_tick(slot_of, g, s, w):
    b = Back(*backward_call(ALL, slot_of, w, g, s.f, s.q, s.kv, s.kvp), None)
    return backward_end(b, w)


def cut(x, which, size):
    return lax.slice_in_dim(x, which * size, (which + 1) * size, axis=1)


def on_device(
    tokens,
    grad_out,
    attention_in,
    attention_bias,
    attention_out,
    up_weight,
    up_bias,
    down_weight,
    norm_gains,
    layer_biases,
    block_counts,
    lengths,
    head_shifts,
):
    dp_size = lax.axis_size("dp")
    first = lax.axis_index("section") == 0
    width = tokens.shape[2]
    quarter = tokens.shape[1]
    half = attention_in.shape[3]
    hidden = up_weight.shape[2]

    crossed = lax.ppermute(jnp.where(first, grad_out[0], tokens[0]), "section", SWAP)
    from_rows = lambda x, s: jnp.concatenate([tokens[s], x], axis=0)
    cot_rows = lambda x, s: jnp.concatenate([x, grad_out[s]], axis=0)
    tok0, cot0 = from_rows(crossed, 0), cot_rows(crossed, 0)
    win, win_far = attention_in[0], to_peer(attention_in[0])
    ab, ab_far = attention_bias[0], to_peer(attention_bias)[0]
    bv = jnp.concatenate([ab[1], ab_far[1]])
    w = Layer(
        q=jnp.concatenate([win[:, 0], win_far[:, 0]], axis=1),
        kv=jnp.concatenate([win[:, 1], win_far[:, 1], win[:, 2], win_far[:, 2]], axis=1),
        bq=jnp.concatenate([ab[0], ab_far[0]]),
        bkv=jnp.concatenate([jnp.zeros_like(bv), bv]),
        out=attention_out[0],
        up=up_weight[0],
        down=down_weight[0],
        out_far=to_peer(attention_out[0]),
        up_far=to_peer(up_weight[0]),
        down_far=to_peer(down_weight[0]),
        bup_own=up_bias,
        bup_far=to_peer(up_bias),
        ng=norm_gains[0],
        lb=layer_biases[0],
        counts=block_counts,
        lengths=lengths,
        shift_own=head_shifts,
        shift_far=to_peer(head_shifts),
    )
    slot_one = lambda s: 0
    slot_a = lambda s: 1 - s
    slot_b = lambda s: s

    out1, _ = forward_tick(False, slot_one, tok0, w)
    tok1 = from_rows(last_section(tokens[1]), 1)
    out2, saved2 = forward_tick(True, slot_a, jnp.where(first, tok1, next_section(out1)), w)
    away2 = next_section(out2)
    g3, b3 = backward_tick(slot_a, cot0, saved2, w)
    away2, rows1, _ = tied(away2, grad_out[1], b3.d2_low)
    cot1 = cot_rows(next_section(rows1), 1)
    out4, saved4 = forward_tick(True, slot_b, jnp.where(first, tok0, away2), w)
    g5, b5 = backward_tick(slot_b, jnp.where(first, last_section(g3), cot1), saved4, w)

    early = gradient_call(saved4, b5)
    g6_in = jnp.where(first, last_section(g5), cot0)

    f6 = saved2.f
    d2_low = norm_back(g6_in.astype(F32), f6.n2.astype(F32), f6.inv2[:, :1], w.ng[1]).astype(BF)
    down_far = half_gradient_call(d2_low, f6.act, d2_low, early[0], 1, True)
    down_own = half_gradient_call(down_far, f6.act, d2_low, early[0], 0, True)
    down = Sum(add_low(down_own, to_peer(down_far)), dp_size)
    r6 = backward_call(ROWS, slot_a, w, g6_in, f6, None, None, None, None, (down.sent,), early[1])
    b6 = Back(*r6[:5], None, None, None, None)
    d_mixed, up_own, up_far = r6[5:]
    (up_far,) = step_sums([down], up_far)
    up_in = to_peer(up_far)
    up = Sum(add_low(up_own, up_in), dp_size)
    quarters = jnp.concatenate([out2[:quarter], out4[:quarter]], axis=0)
    dq, near, far = backward_call(
        HEADS, slot_a, w, None, f6, saved2.q, saved2.kv, saved2.kvp, d_mixed, (down.sent, up.sent)
    )
    dq, near, far, quarters = step_sums([down, up], dq, near, far, quarters)
    layer_far = last_section(quarters)
    g6, b6 = backward_end(b6._replace(dq=dq, near=near, far=far), w)
    out_own, out_far, in_own, in_far, small_own, small_far = last_gradient_call(up.sent, saved2, b6, early, b5)
    out_far, in_far, small_far, tick = step_sums([down, up], out_far, in_far, small_far, b6.bias_sums)
    tokens_far = next_section(jnp.concatenate([g5[quarter:], g6[quarter:]], axis=0))
    in_g = add_low(in_own, to_peer(in_far))
    small = small_own + to_peer(small_far)
    out_g = jnp.concatenate(
        [add_low(out_own, to_peer(out_far)), small.astype(BF), jnp.zeros((16, width), BF)], axis=0
    )
    part = lambda x, i: x[i * x.shape[0] // 2 : (i + 1) * x.shape[0] // 2]
    in_a, in_b = Sum(part(in_g, 0), dp_size), Sum(part(in_g, 1), dp_size)
    last = Sum(out_g, dp_size)
    (tick,) = step_sums([in_a], tick)
    (tick,) = step_sums([in_b], tick)
    (tick,) = step_sums([down, up], tick)
    (tick,) = step_sums([in_a, last], tick)
    tick, layer_far = step_sums([in_b], tick, layer_far)
    (tick,) = step_sums([in_a, last], tick)
    (tick,) = step_sums([up, in_b], tick)
    (tick,) = step_sums([in_a, last], tick)
    (tick,) = step_sums([down, in_b], tick)
    tick, tokens_far = step_sums([last], tick, tokens_far)
    sums = [up, in_a, in_b, last, down]
    while any(one.whole is None for one in sums):
        (tick,) = step_sums(sums, tick)
    down_s = down.whole.astype(F32)
    up_s = up.whole.astype(F32)
    in_s = jnp.concatenate([in_a.whole, in_b.whole], axis=0).astype(F32)
    out_s = last.whole.astype(F32)
    small = out_s[half : half + 16]

    pair = lambda x, y: jnp.stack([x, y])
    layer_out = jnp.where(first, layer_far.reshape(tokens.shape), pair(out2[quarter:], out4[quarter:]))
    grad_tokens = jnp.where(first, pair(g5[:quarter], g6[:quarter]), tokens_far.reshape(tokens.shape))
    return (
        layer_out,
        grad_tokens,
        in_s.reshape(3, width, half).transpose(1, 0, 2)[None],
        small[8].reshape(1, 2, half),
        out_s[:half][None],
        up_s[None],
        small[6:8].reshape(1, hidden),
        down_s[None],
        small[:2][None],
        small[2:6][None],
    )


def solution(mesh):
    tokens = P("dp", ("section", "mp"), None)
    weights = (
        P("section", None, None, "mp"),
        P("section", None, "mp"),
        P("section", "mp", None),
        P("section", None, "mp"),
        P("section", "mp"),
        P("section", "mp", None),
        P("section", None, None),
        P("section", None, None),
    )
    return jax.shard_map(
        on_device,
        mesh=mesh,
        in_specs=(tokens, tokens) + weights + (P("dp"), P("dp"), P("section", "mp")),
        out_specs=(tokens, tokens) + weights,
        check_vma=False,
    )
```

```python
import functools
import math
from typing import Any, NamedTuple

import jax
import jax.numpy as jnp
from jax import lax
from jax.experimental import pallas as pl
from jax.experimental.pallas import tpu as pltpu
from jax.sharding import PartitionSpec as P

BF = jnp.bfloat16
F32 = jnp.float32
EPS = 1e-05
SHUT = -1e30
TILE = 256
FORWARD_WINDOWS = (512, 528)
BACKWARD_WINDOWS = (528,)
CHUNK = 512
BLOCK = 64
VMEM_BYTES = 50 * 2**20
NO_COST = pl.CostEstimate(flops=1, bytes_accessed=1, transcendentals=0)


def dot_nn(a, b):
    return lax.dot_general(a, b, (((1,), (0,)), ((), ())), preferred_element_type=F32)


def dot_nt(a, b):
    return lax.dot_general(a, b, (((1,), (1,)), ((), ())), preferred_element_type=F32)


def dot_tn(a, b):
    return lax.dot_general(a, b, (((0,), (0,)), ((), ())), preferred_element_type=F32)


def mask_numbers(slot, counts, lengths):
    c = counts[slot]
    n = lengths[slot]
    third = (n + 2) // 3
    th1 = jnp.where(c == 3, third, (n + 1) // 2)
    th2 = jnp.where(c == 3, (2 * n + 2) // 3, 1 << 20)
    return th1, th2, n, c, lax.axis_index("mp")


def key_columns(nums, rows):
    th1, th2, n = nums[:3]
    u = lax.broadcasted_iota(jnp.int32, (rows, 128), 0)
    col = lax.broadcasted_iota(jnp.int32, (rows, 128), 1)
    blk = (u >= th1).astype(jnp.int32) + (u >= th2).astype(jnp.int32)
    open_ = (blk == col) & (u < n)
    one = jnp.where(col < 8, 1.0, 0.0)
    return jnp.where(col < 3, jnp.where(open_, 0.0, SHUT), one).astype(BF)


def query_rows(nums, shift, r0):
    th1, th2, _, c, _ = nums
    pos = r0 + lax.broadcasted_iota(jnp.int32, (16, TILE), 1)
    row = lax.broadcasted_iota(jnp.int32, (16, TILE), 0)
    t = (pos >= th1).astype(jnp.int32) + (pos >= th2).astype(jnp.int32) + shift
    t = jnp.where(t >= c, t - c, t)
    return jnp.where(row == t, 1.0, 0.0), row


def split3(x):
    a = x.astype(BF).astype(F32)
    b = (x - a).astype(BF).astype(F32)
    return a, b, (x - a - b).astype(BF).astype(F32)


def window_need(nums, r0):
    th1, th2, n, c, _ = nums
    last = r0 + TILE - 1
    whole = ((r0 < th1) == (last < th1)) & ((r0 < th2) == (last < th2))
    need = jnp.maximum(th1, jnp.minimum(th2, n) - (th1 // 16) * 16)
    need = jnp.maximum(need, jnp.where(c == 3, n - (th2 // 16) * 16, 0))
    return jnp.where(whole, need, 1 << 20)


def window_base(nums, shift, r0, limit):
    th1, th2, _, c, _ = nums
    t = jnp.where(r0 >= th1, 1, 0) + jnp.where(r0 >= th2, 1, 0) + shift
    t = jnp.where(t >= c, t - c, t)
    start = jnp.where(t == 0, 0, jnp.where(t == 1, th1, th2))
    return pl.multiple_of(jnp.minimum((start // 16) * 16, limit), 16)


def by_window(need, length, windows, body):
    prev = 0
    for width in windows:
        if width < length:

            @pl.when((need > prev) & (need <= width))
            def _(width=width):
                body(width)

            prev = width

    @pl.when(need > prev)
    def _():
        body(length)


def place_rows(dst, lanes, own, far, offset, core):
    pairs = dst.shape[0]
    for i in range(2):
        for who, ref in enumerate((own, far)):
            blk = 2 * i + jnp.where(core == who, 0, 1)
            rows = pl.ds(pl.multiple_of(blk * TILE, TILE), TILE)
            for p in range(pairs):
                src = offset + (p if who == 0 else (p + pairs // 2) % pairs) * 128
                dst[p, rows, lanes] = ref[i * TILE : (i + 1) * TILE, src : src + 128]


def place_values(v0, v1, own, far, offset, core):
    pairs = v0.shape[0]
    lane = lax.broadcasted_iota(jnp.int32, (TILE, 128), 1)
    ones = jnp.ones((TILE, 128), BF)
    for i in range(2):
        for who, ref in enumerate((own, far)):
            blk = 2 * i + jnp.where(core == who, 0, 1)
            rows = pl.ds(pl.multiple_of(blk * TILE, TILE), TILE)
            for p in range(pairs):
                src = offset + (p if who == 0 else (p + pairs // 2) % pairs) * 128
                x = ref[i * TILE : (i + 1) * TILE, src : src + 128]
                v0[p, rows, :] = jnp.where(lane < 64, x, ones)
                v1[p, rows, :] = jnp.where(lane < 64, ones, x)


def head_shift(own, far, j):
    heads = own.shape[1]
    if isinstance(j, int):
        return own[0, j] if j < heads else far[0, j - heads]
    return jnp.where(j < heads, own[0, jnp.minimum(j, heads - 1)], far[0, jnp.maximum(j - heads, 0)])


def attend(nums, shifts, q, kb, v0, v1, score, weight, top, mixed, lse):
    pairs, length = kb.shape[:2]
    th1, th2, _, c, core = nums
    heads = 2 * pairs
    lane = lax.broadcasted_iota(jnp.int32, (TILE, 128), 1)
    sub = lax.broadcasted_iota(jnp.int32, (TILE, 128), 0)

    @pl.loop(0, 2)
    def _(tile):
        r0 = (2 * tile + core) * TILE
        rows = pl.ds(pl.multiple_of(tile * TILE, TILE), TILE)
        behind = ((r0 + sub) >= th1).astype(jnp.int32) + ((r0 + sub) >= th2).astype(jnp.int32) - lane

        def body(width):
            outs = [None] * heads

            def window(j):
                shift = head_shift(*shifts, j)
                return pl.ds(window_base(nums, shift, r0, length - width) if width < length else 0, width)

            def scores(j):
                p, hh = divmod(j, 2)
                qn = q[rows, p * 128 : (p + 1) * 128].astype(F32) * 0.125
                d = behind + head_shift(*shifts, j)
                target = jnp.where((lane < c) & ((d == 0) | (d == c)), 1.0, 0.0)
                qm = jnp.where((lane >= 64) == (hh == 1), qn, 0.0)
                lhs = jnp.concatenate([qm.astype(BF), target.astype(BF)], axis=1)
                score[j % 2, :, 0:width] = dot_nt(lhs, kb[p, window(j), :])

            def softmax(j):
                for r in range(0, TILE, 128):
                    part = score[j % 2, r : r + 128, 0:width]
                    largest = jnp.max(part, axis=1, keepdims=True)
                    top[j % 4, r : r + 128, :] = jnp.broadcast_to(largest, (128, 128))
                    weight[j % 2, r : r + 128, 0:width] = jnp.exp(part - largest).astype(BF)

            def product(j):
                p, hh = divmod(j, 2)
                outs[j] = dot_nn(weight[j % 2, :, 0:width], (v0, v1)[hh][p, window(j), :])
                if hh == 1:
                    total = jnp.where(lane < 64, pltpu.roll(outs[j - 1], 64, 1), pltpu.roll(outs[j], 64, 1))
                    value = jnp.where(lane < 64, outs[j - 1], outs[j])
                    mixed[rows, p * 128 : (p + 1) * 128] = (value / total).astype(BF)
                    if lse is not None:
                        both = (jnp.where(lane < 64, top[(j - 1) % 4], top[j % 4]) + jnp.log(total)).T
                        lse[p, 0:1, rows] = both[0:1]
                        lse[p, 1:2, rows] = both[64:65]

            for step in range(heads + 2):
                if step < heads:
                    scores(step)
                if 1 <= step <= heads:
                    softmax(step - 1)
                if step >= 2:
                    product(step - 2)

        by_window(window_need(nums, r0), length, FORWARD_WINDOWS, body)


def attend_back(nums, shifts, q, do, mixed, lse, kb, vb, dka, dva, dq):
    pairs, length = kb.shape[:2]
    core = nums[4]
    sub = lax.broadcasted_iota(jnp.int32, (128, TILE), 0)
    lane = lax.broadcasted_iota(jnp.int32, (TILE, 128), 1)
    for tile in range(2):
        r0 = (2 * tile + core) * TILE
        rows = slice(tile * TILE, (tile + 1) * TILE)

        def body(width):
            @pl.loop(0, pairs, unroll=2)
            def _(p):
                lanes = pl.ds(pl.multiple_of(p * 128, 128), 128)
                qn = q[rows, lanes].astype(F32) * 0.125
                don = do[rows, lanes].astype(F32)
                qt = qn.T
                dot_ = don.T
                prod = dot_ * mixed[rows, lanes].astype(F32).T
                outs = []
                for hh in range(2):
                    shift = head_shift(*shifts, 2 * p + hh)
                    target, row = query_rows(nums, shift, r0)
                    la, lb, lc = split3(-lse[p, hh : hh + 1, rows])
                    target = target + jnp.where(row == 3, la, jnp.where(row == 4, lb, jnp.where(row == 5, lc, 0.0)))
                    keep = (sub >= 64) == (hh == 1)
                    zeros = jnp.zeros((112, TILE), BF)
                    rhs = jnp.concatenate([jnp.where(keep, qt, 0.0).astype(BF), target.astype(BF), zeros], axis=0)
                    da, db, dc = split3(-jnp.sum(prod[hh * 64 : (hh + 1) * 64], axis=0, keepdims=True))
                    minus = jnp.where(row == 3, da, jnp.where(row == 4, db, jnp.where(row == 5, dc, 0.0)))
                    rhs2 = jnp.concatenate([jnp.where(keep, dot_, 0.0).astype(BF), minus.astype(BF), zeros], axis=0)
                    keepl = (lane >= 64) == (hh == 1)
                    qm = jnp.where(keepl, qn, 0.0).astype(BF)
                    dom = jnp.where(keepl, don, 0.0).astype(BF)
                    start = window_base(nums, shift, r0, length - width) if width < length else 0
                    win = pl.ds(start, width)
                    kwin = kb[p, win, :]
                    pt = jnp.exp(dot_nn(kwin, rhs))
                    ds = (pt * dot_nn(vb[p, win, :], rhs2)).astype(BF)
                    dva[p, win, :] += dot_nn(pt.astype(BF), dom)
                    dka[p, win, :] += dot_nn(ds, qm)
                    kt = kwin[:, 0:128].T[hh * 64 : (hh + 1) * 64]
                    outs.append(dot_nn(kt, ds))
                dq[rows, lanes] = (jnp.concatenate(outs, axis=0) * 0.125).T.astype(BF)

        by_window(window_need(nums, r0), length, BACKWARD_WINDOWS, body)


def gelu_pair(x):
    density = jnp.exp(x * x * (-0.5)) * (2.0 * math.pi) ** (-0.5)
    cdf = 0.5 + 0.5 * lax.erf(x * (2.0 ** (-0.5)))
    return x * cdf, cdf + x * density


def norm_rows(x):
    scale = 1.0 / x.shape[-1]
    centred = x - jnp.sum(x, axis=-1, keepdims=True) * scale
    inv = lax.rsqrt(jnp.sum(centred * centred, axis=-1, keepdims=True) * scale + EPS)
    return centred * inv, inv


def norm_back(up, normed, inv, gain):
    scale = 1.0 / normed.shape[-1]
    e = up * gain
    a = jnp.sum(e, axis=-1, keepdims=True) * scale
    b = jnp.sum(e * normed, axis=-1, keepdims=True) * scale
    return inv * (e - a - normed * b)


def copier(sems):
    used = [0]

    def start(src, dst):
        copy = pltpu.make_async_copy(src, dst, sems.at[used[0]])
        used[0] += 1
        copy.start()
        return copy

    return start


class ForwardIn(NamedTuple):
    q: Any
    kv: Any
    kvp: Any
    h: Any
    wout: Any
    wup: Any
    wdown: Any
    wout_far: Any
    wup_far: Any
    wdown_far: Any


class ForwardOut(NamedTuple):
    out: Any
    mixed: Any
    lse: Any
    x1_low: Any
    act: Any
    slope: Any
    n1: Any
    inv1: Any
    n2: Any
    inv2: Any


class ForwardWork(NamedTuple):
    kb: Any
    v0: Any
    v1: Any
    score: Any
    weight: Any
    top: Any
    pre: Any
    x1: Any
    acc: Any


def weight_copies(start, src, x):
    c_out, c_up, c_down = [], [], []
    for j, (out, up, down) in enumerate(((src.wout, src.wup, src.wdown), (src.wout_far, src.wup_far, src.wdown_far))):
        rows, cols = out.shape[0], up.shape[1]
        c_out.append(start(out, x.wout.at[j * rows : (j + 1) * rows, :]))
        c_up.append(start(up, x.wup.at[:, j * cols : (j + 1) * cols]))
        c_down.append(start(down, x.wdown.at[j * cols : (j + 1) * cols, :]))
    return c_out, c_up, c_down


def forward_kernel(save, slot_of, tokens, counts, lengths, shift_own, shift_far, lb, ng, bup_own, bup_far, *refs):
    refs = list(refs[tokens:])
    take = lambda kind: kind(*[refs.pop(0) for _ in range(len(kind._fields))])
    src = take(ForwardIn)
    dst = take(ForwardOut) if save else ForwardOut(refs.pop(0), *[None] * 9)
    x = ForwardIn(*[refs.pop(0) for _ in range(7)], None, None, None)
    y = take(ForwardOut)
    t = take(ForwardWork)
    start = copier(refs[0])
    rows, width = x.h.shape
    hidden = x.wup.shape[1]
    half = hidden // 2
    load = ForwardIn(*[None] * 10)._replace(
        kv=start(src.kv, x.kv),
        kvp=start(src.kvp, x.kvp),
        q=start(src.q, x.q),
        h=start(src.h, x.h),
    )
    c_out, c_up, c_down = weight_copies(start, src, x)
    done = []

    def ship(a, b):
        if b is not None:
            done.append(start(a, b))

    def ship_part(a, b, part):
        if b is not None:
            done.append(start(a.at[:, part], b.at[:, part]))

    nums = mask_numbers(slot_of(lax.axis_index("section")), counts, lengths)
    core = nums[4]
    ext = key_columns(nums, t.kb.shape[1])
    for p in range(t.kb.shape[0]):
        t.kb[p, :, 128:256] = ext
    load.kv.wait()
    load.kvp.wait()
    place_rows(t.kb, slice(0, 128), x.kv, x.kvp, 0, core)
    place_values(t.v0, t.v1, x.kv, x.kvp, width, core)
    load.q.wait()
    attend(
        nums, (shift_own, shift_far), x.q, t.kb, t.v0, t.v1, t.score, t.weight, t.top, y.mixed, y.lse if save else None
    )
    ship(y.mixed, dst.mixed)
    ship(y.lse, dst.lse)
    for copy in c_out:
        copy.wait()
    t.acc[...] = dot_nn(y.mixed[...], x.wout[...])
    load.h.wait()
    for r in range(0, rows, BLOCK):
        rs = slice(r, r + BLOCK)
        normed, inv = norm_rows(x.h[rs, :].astype(F32) + t.acc[rs, :] + lb[0:1, :])
        if save:
            y.n1[rs, :] = normed.astype(BF)
            y.inv1[rs, :] = jnp.broadcast_to(inv, (BLOCK, 128))
        full = normed * ng[0:1, :] + lb[1:2, :]
        t.x1[rs, :] = full
        y.x1_low[rs, :] = full.astype(BF)
    ship(y.x1_low, dst.x1_low)
    ship(y.n1, dst.n1)
    ship(y.inv1, dst.inv1)
    chunks = hidden // CHUNK

    def up(j):
        t.pre[j % 2] = dot_nn(y.x1_low[...], x.wup[:, j * CHUNK : (j + 1) * CHUNK])

    def activate(j):
        part = slice(j * CHUNK, (j + 1) * CHUNK)
        low = (j * CHUNK) % half
        bias = (bup_own if j < chunks // 2 else bup_far)[0:1, low : low + CHUNK]
        for r in range(0, rows, BLOCK):
            rs = slice(r, r + BLOCK)
            act, slope = gelu_pair(t.pre[j % 2, rs, :] + bias)
            y.act[rs, part] = act.astype(BF)
            if save:
                y.slope[rs, part] = slope.astype(BF)

    c_up[0].wait()
    up(0)
    for j in range(chunks // 2):
        if j + 1 == chunks // 2:
            c_up[1].wait()
        up(j + 1)
        activate(j)
    ship_part(y.act, dst.act, slice(0, half))
    ship_part(y.slope, dst.slope, slice(0, half))
    c_down[0].wait()
    t.acc[...] = dot_nn(y.act[:, :half], x.wdown[:half, :])
    for j in range(chunks // 2, chunks):
        if j + 1 < chunks:
            up(j + 1)
        activate(j)
    ship_part(y.act, dst.act, slice(half, hidden))
    ship_part(y.slope, dst.slope, slice(half, hidden))
    c_down[1].wait()
    t.acc[...] += dot_nn(y.act[:, half:], x.wdown[half:, :])
    for r in range(0, rows, BLOCK):
        rs = slice(r, r + BLOCK)
        normed, inv = norm_rows(t.x1[rs, :] + t.acc[rs, :] + lb[2:3, :])
        if save:
            y.n2[rs, :] = normed.astype(BF)
            y.inv2[rs, :] = jnp.broadcast_to(inv, (BLOCK, 128))
        y.out[rs, :] = (normed * ng[1:2, :] + lb[3:4, :]).astype(BF)
    ship(y.out, dst.out)
    ship(y.n2, dst.n2)
    ship(y.inv2, dst.inv2)
    for copy in done:
        copy.wait()


def buffers(shapes):
    return [pltpu.VMEM(*s) for s in shapes]


def results(shapes):
    return tuple(jax.ShapeDtypeStruct(*s) for s in shapes)


IN_SMEM = pl.BlockSpec(memory_space=pltpu.SMEM)
IN_VMEM = pl.BlockSpec(memory_space=pltpu.VMEM)
IN_HBM = pl.BlockSpec(memory_space=pltpu.HBM)


def forward_call(save, slot_of, w, q, kv, kvp, h, tokens=()):
    rows, width = h.shape
    hidden = 2 * w.up.shape[1]
    pairs, length = width // 128, 2 * rows
    low, wide, full = ((rows, width), BF), ((rows, hidden), BF), ((rows, width), F32)
    one, twice = ((rows, 128), F32), ((rows, 2 * width), BF)
    shapes_in = (low, twice, twice, low, ((width, width), BF), ((width, hidden), BF), ((hidden, width), BF))
    shapes_out = ForwardOut(low, low, ((pairs, 2, rows), F32), low, wide, wide, low, one, low, one)
    if not save:
        gone = ((16, 128), BF)
        scratch_out = shapes_out._replace(lse=gone, slope=gone, n1=gone, inv1=gone, n2=gone, inv2=gone)
    else:
        scratch_out = shapes_out
    work = ForwardWork(
        ((pairs, length, 256), BF),
        ((pairs, length, 128), BF),
        ((pairs, length, 128), BF),
        ((2, TILE, length), F32),
        ((2, TILE, length), BF),
        ((4, TILE, 128), F32),
        ((2, rows, CHUNK), F32),
        full,
        full,
    )
    outs = shapes_out if save else shapes_out[:1]
    res = pl.pallas_call(
        functools.partial(forward_kernel, save, slot_of, len(tokens)),
        out_shape=results(outs),
        in_specs=[IN_SMEM] * 4 + [IN_VMEM] * 4 + [IN_HBM] * (10 + len(tokens)),
        out_specs=(IN_HBM,) * len(outs),
        scratch_shapes=buffers(shapes_in) + buffers(scratch_out) + buffers(work) + [pltpu.SemaphoreType.DMA((24,))],
        compiler_params=pltpu.CompilerParams(vmem_limit_bytes=VMEM_BYTES),
        cost_estimate=NO_COST,
        name="layer_forward",
    )(
        w.counts, w.lengths, w.shift_own, w.shift_far, w.lb, w.ng, w.bup_own, w.bup_far, *tokens,
        q, kv, kvp, h, w.out, w.up, w.down, w.out_far, w.up_far, w.down_far,
    )
    return ForwardOut(*res) if save else ForwardOut(res[0], *[None] * 9)


class RowsIn(NamedTuple):
    g: Any
    n2: Any
    inv2: Any
    n1: Any
    inv1: Any
    slope: Any
    wout: Any
    wup: Any
    wdown: Any
    wout_far: Any
    wup_far: Any
    wdown_far: Any


class RowsOut(NamedTuple):
    d2_low: Any
    d_pre: Any
    d1_low: Any


class HeadsIn(NamedTuple):
    mixed: Any
    lse: Any
    q: Any
    kv: Any
    kvp: Any


class HeadsOut(NamedTuple):
    dq: Any
    near: Any
    far: Any


class HeadsWork(NamedTuple):
    kb: Any
    vb: Any
    dka: Any
    dva: Any


def rows_back(start, src, dst, x, y, d_mixed, dx, ng, sums, bias_sums, behind, up_refs):
    rows, width = x.g.shape
    hidden = x.wup.shape[1]
    half = hidden // 2
    chunks = hidden // CHUNK
    soon = [start(src.g, x.g), start(src.n2, x.n2), start(src.inv2, x.inv2)]
    c_slope = [
        start(src.slope.at[:, part], x.slope.at[:, part]) for part in (slice(0, half), slice(half, hidden))
    ]
    c_out, c_up, c_down = weight_copies(start, src, x)
    late = [start(src.n1, x.n1), start(src.inv1, x.inv1)]
    if up_refs:
        x1_h, early_h, outs_h, x1, early, outs = up_refs
        up_load = [start(x1_h, x1), start(early_h, early)]
    behind()
    done = []
    zero = jnp.zeros((1, width), F32)
    s_gn, s_g, s_d2 = zero, zero, zero
    for copy in soon:
        copy.wait()
    for r in range(0, rows, BLOCK):
        rs = slice(r, r + BLOCK)
        g = x.g[rs, :].astype(F32)
        normed = x.n2[rs, :].astype(F32)
        d2 = norm_back(g, normed, x.inv2[rs, 0:1], ng[1:2, :])
        dx[rs, :] = d2
        y.d2_low[rs, :] = d2.astype(BF)
        s_gn += jnp.sum(g * normed, axis=0, keepdims=True)
        s_g += jnp.sum(g, axis=0, keepdims=True)
        s_d2 += jnp.sum(d2, axis=0, keepdims=True)
    done.append(start(y.d2_low, dst.d2_low))
    for k in range(2):
        c_down[k].wait()
        c_slope[k].wait()
        for j in range(k * chunks // 2, (k + 1) * chunks // 2):
            part = slice(j * CHUNK, (j + 1) * CHUNK)
            d_act = dot_nt(y.d2_low[...], x.wdown[part, :])
            d_pre = (d_act * x.slope[:, part].astype(F32)).astype(BF)
            y.d_pre[:, part] = d_pre
            bias_sums[0:1, part] = jnp.sum(d_pre.astype(F32), axis=0, keepdims=True)
        part = slice(k * half, (k + 1) * half)
        done.append(start(y.d_pre.at[:, part], dst.d_pre.at[:, part]))
        c_up[k].wait()
        dx[...] += dot_nt(y.d_pre[:, part], x.wup[:, part])
    def up_gradient(k):
        if up_refs:
            for j in range(2):
                to = slice(j * half // 2, (j + 1) * half // 2)
                at = slice(k * half + j * half // 2, k * half + (j + 1) * half // 2)
                outs[k][:, to] = (dot_tn(x1[...], y.d_pre[:, at]) + early[:, at].astype(F32)).astype(BF)
            done.append(start(outs[k], outs_h[k]))

    if up_refs:
        for copy in up_load:
            copy.wait()
    up_gradient(1)
    s_dn, s_dx, s_d1 = zero, zero, zero
    late[0].wait()
    late[1].wait()
    for r in range(0, rows, BLOCK):
        rs = slice(r, r + BLOCK)
        g = dx[rs, :]
        normed = x.n1[rs, :].astype(F32)
        d1 = norm_back(g, normed, x.inv1[rs, 0:1], ng[0:1, :])
        y.d1_low[rs, :] = d1.astype(BF)
        s_dn += jnp.sum(g * normed, axis=0, keepdims=True)
        s_dx += jnp.sum(g, axis=0, keepdims=True)
        s_d1 += jnp.sum(d1, axis=0, keepdims=True)
    done.append(start(y.d1_low, dst.d1_low))
    for i, s in enumerate((s_dn, s_gn, s_d1, s_dx, s_d2, s_g)):
        sums[i : i + 1, :] = s
    sums[6:8, :] = jnp.zeros((2, width), F32)
    for copy in c_out:
        copy.wait()
    d_mixed[...] = dot_nt(y.d1_low[...], x.wout[...]).astype(BF)
    up_gradient(0)
    return done


def heads_back(start, load, dst, x, y, t, d_mixed, nums, shifts):
    width = x.q.shape[1]
    core = nums[4]
    pairs = t.kb.shape[0]
    ext = key_columns(nums, t.kb.shape[1])
    for p in range(pairs):
        t.kb[p, :, 128:256] = ext
        t.vb[p, :, 128:256] = ext
    for copy in load:
        copy.wait()
    place_rows(t.kb, slice(0, 128), x.kv, x.kvp, 0, core)
    place_rows(t.vb, slice(0, 128), x.kv, x.kvp, width, core)
    t.dka[...] = jnp.zeros_like(t.dka)
    t.dva[...] = jnp.zeros_like(t.dva)
    attend_back(nums, shifts, x.q, d_mixed, x.mixed, x.lse, t.kb, t.vb, t.dka, t.dva, y.dq)
    done = [start(y.dq, dst.dq)]
    for to, side, turn in ((y.far, 1 - core, pairs // 2), (y.near, core, 0)):
        for i in range(2):
            mine = pl.ds(pl.multiple_of((2 * i + side) * TILE, TILE), TILE)
            for p in range(pairs):
                for j, total in enumerate((t.dka, t.dva)):
                    lanes = slice(j * width + p * 128, j * width + (p + 1) * 128)
                    to[i * TILE : (i + 1) * TILE, lanes] = total[(p + turn) % pairs, mine, :].astype(to.dtype)
    done += [start(y.far, dst.far), start(y.near, dst.near)]
    return done


ALL, ROWS, HEADS = 3, 1, 2


def backward_kernel(which, slot_of, tokens, counts, lengths, shift_own, shift_far, ng, *refs):
    refs = list(refs[tokens:])
    take = lambda kind: kind(*[refs.pop(0) for _ in range(len(kind._fields))])
    rows_on, heads_on = which & ROWS, which & HEADS
    if rows_on:
        r_src = take(RowsIn)
    if heads_on:
        h_src = take(HeadsIn)
    if which == HEADS:
        mixed_src = refs.pop(0)
    if which == ROWS:
        up_refs = [refs.pop(0), refs.pop(0)]
    if rows_on:
        r_dst = take(RowsOut)
        sums, bias_sums = refs.pop(0), refs.pop(0)
    if which == ROWS:
        mixed_dst = refs.pop(0)
        up_refs.append([refs.pop(0), refs.pop(0)])
    if heads_on:
        h_dst = take(HeadsOut)
    d_mixed = refs.pop(0)
    if rows_on:
        r_x = RowsIn(*[refs.pop(0) for _ in range(9)], None, None, None)
        r_y, dx = take(RowsOut), refs.pop(0)
    if which == ROWS:
        up_refs += [refs.pop(0), refs.pop(0), [refs.pop(0), refs.pop(0)]]
    if heads_on:
        h_x, h_y, h_t = take(HeadsIn), take(HeadsOut), take(HeadsWork)
    start = copier(refs[0])
    load, done = [], []

    def load_heads():
        if heads_on:
            load.extend(start(a, b) for a, b in zip(h_src, h_x))

    if rows_on:
        up_refs = up_refs if which == ROWS else None
        done += rows_back(start, r_src, r_dst, r_x, r_y, d_mixed, dx, ng, sums, bias_sums, load_heads, up_refs)
    else:
        load_heads()
        load.append(start(mixed_src, d_mixed))
    if which == ROWS:
        done.append(start(d_mixed, mixed_dst))
    if heads_on:
        nums = mask_numbers(slot_of(lax.axis_index("section")), counts, lengths)
        done += heads_back(start, load, h_dst, h_x, h_y, h_t, d_mixed, nums, (shift_own, shift_far))
    for copy in done:
        copy.wait()


def gradient_kernel(*refs):
    refs = list(refs)
    src = [refs.pop(0) for _ in range(9)]
    dst = [refs.pop(0) for _ in range(5)]
    col_sums = refs.pop(0)
    x = [refs.pop(0) for _ in range(9)]
    y = [refs.pop(0) for _ in range(5)]
    start = copier(refs[0])
    load = [start(a, b) for a, b in zip(src, x)]
    done = []
    act, d2_low, x1_low, d_pre, mixed, d1_low, h, dq, dkv = range(9)
    for k, (left, right) in enumerate(((act, d2_low), (x1_low, d_pre), (mixed, d1_low), (h, dq), (h, dkv))):
        for i in (left, right):
            if load[i] is not None:
                load[i].wait()
                load[i] = None
        tall, broad = y[k].shape
        slab = CHUNK if max(tall, broad) % CHUNK == 0 else TILE
        for j in range(max(tall, broad) // slab):
            part = slice(j * slab, (j + 1) * slab)
            if tall > broad:
                y[k][part, :] = dot_tn(x[left][:, part], x[right][...]).astype(BF)
                done.append(start(y[k].at[part, :], dst[k].at[part, :]))
            else:
                y[k][:, part] = dot_tn(x[left][...], x[right][:, part]).astype(BF)
                done.append(start(y[k].at[:, part], dst[k].at[:, part]))
    width = x[h].shape[1]
    col_sums[0:1, :] = jnp.sum(x[dq][...].astype(F32), axis=0, keepdims=True)
    col_sums[1:2, :] = jnp.sum(x[dkv][:, width:].astype(F32), axis=0, keepdims=True)
    for copy in done:
        copy.wait()


def gradient_call(s, b):
    f = s.f
    rows, width = s.h.shape
    hidden = f.act.shape[1]
    args = (f.act, b.d2_low, f.x1_low, b.d_pre, f.mixed, b.d1_low, s.h, b.dq, b.dkv)
    shapes = [
        ((hidden, width), BF), ((width, hidden), BF), ((width, width), BF), ((width, width), BF), ((width, 2 * width), BF),
    ]
    return pl.pallas_call(
        gradient_kernel,
        out_shape=results(shapes + [((2, width), F32)]),
        in_specs=[IN_HBM] * 9,
        out_specs=(IN_HBM,) * 5 + (IN_VMEM,),
        scratch_shapes=buffers([(a.shape, BF) for a in args]) + buffers(shapes) + [pltpu.SemaphoreType.DMA((40,))],
        compiler_params=pltpu.CompilerParams(vmem_limit_bytes=VMEM_BYTES),
        cost_estimate=NO_COST,
        name="layer_gradient",
    )(*args)


def half_gradient_kernel(k, by_rows, token, left_h, right_h, early_h, out_h, left, right, early, out, sems):
    start = copier(sems)
    tall, broad = out.shape
    if by_rows:
        load = [start(left_h.at[:, k * tall : (k + 1) * tall], left), start(right_h, right)]
        before = start(early_h.at[k * tall : (k + 1) * tall, :], early)
    else:
        load = [start(left_h, left), start(right_h.at[:, k * broad : (k + 1) * broad], right)]
        before = start(early_h.at[:, k * broad : (k + 1) * broad], early)
    for copy in load:
        copy.wait()
    before.wait()
    done = []
    for j in range(2):
        if by_rows:
            part = slice(j * tall // 2, (j + 1) * tall // 2)
            out[part, :] = (dot_tn(left[:, part], right[...]) + early[part, :].astype(F32)).astype(BF)
            done.append(start(out.at[part, :], out_h.at[part, :]))
        else:
            part = slice(j * broad // 2, (j + 1) * broad // 2)
            out[:, part] = (dot_tn(left[...], right[:, part]) + early[:, part].astype(F32)).astype(BF)
            done.append(start(out.at[:, part], out_h.at[:, part]))
    for copy in done:
        copy.wait()


def half_gradient_call(token, left, right, early, k, by_rows):
    rows = left.shape[0]
    tall, broad = early.shape
    tall, broad = (tall // 2, broad) if by_rows else (tall, broad // 2)
    out = ((tall, broad), BF)
    return pl.pallas_call(
        functools.partial(half_gradient_kernel, k, by_rows),
        out_shape=jax.ShapeDtypeStruct(*out),
        in_specs=[IN_HBM] * 4,
        out_specs=IN_HBM,
        scratch_shapes=buffers([((rows, tall), BF), ((rows, broad), BF), out, out]) + [pltpu.SemaphoreType.DMA((5,))],
        compiler_params=pltpu.CompilerParams(vmem_limit_bytes=VMEM_BYTES),
        cost_estimate=NO_COST,
        name="half_gradient",
    )(token, left, right, early)


def last_gradient_kernel(*refs):
    token, mixed_h, d1_h, h_h, dq_h, dkv_h, eo_h, eq_h, ekv_h, c5, s5, s6, u5, u6, *refs = refs
    outs, refs = refs[:4], refs[4:]
    small_own, small_far, mixed, d1, h, dq, dkv, eo, eq, ekv, oo, fo, oi, fi, sems = refs
    start = copier(sems)
    pairs = ((h_h, h), (dq_h, dq), (eq_h, eq), (dkv_h, dkv), (ekv_h, ekv), (mixed_h, mixed), (d1_h, d1), (eo_h, eo))
    load = [start(a, b) for a, b in pairs]
    width = h.shape[1]
    half = width // 2
    done = []
    for copy in load[:5]:
        copy.wait()
    for k, to, away in ((1, fi, outs[3]), (0, oi, outs[2])):
        for part, (right, before) in enumerate(((dq, eq), (dkv, ekv))):
            lanes = slice(k * half, (k + 1) * half)
            total = dot_tn(h[...], right[:, lanes]) + before[:, lanes].astype(F32)
            to[part * width : (part + 1) * width, :] = total.astype(BF)
        done.append(start(to, away))
    for copy in load[5:]:
        copy.wait()
    for k, to, away in ((1, fo, outs[1]), (0, oo, outs[0])):
        lanes = slice(width + k * half, width + (k + 1) * half)
        total = (dot_tn(h[...], dkv[:, lanes]) + ekv[:, lanes].astype(F32)).astype(BF)
        to[0:half, 0:half] = total[0:half]
        to[0:half, half:] = total[half:]
        lanes = slice(k * half, (k + 1) * half)
        to[half : 2 * half, :] = (dot_tn(mixed[:, lanes], d1[...]) + eo[lanes, :].astype(F32)).astype(BF)
        done.append(start(to, away))
    qb = c5[0:1, :] + jnp.sum(dq[...].astype(F32), axis=0, keepdims=True)
    vb = c5[1:2, :] + jnp.sum(dkv[:, width:].astype(F32), axis=0, keepdims=True)
    ub = u5[...] + u6[...]
    for k, to in ((0, small_own), (1, small_far)):
        to[...] = jnp.zeros_like(to)
        to[0:6, :] = s5[0:6, :] + s6[0:6, :]
        for j in range(2):
            to[6 + j : 7 + j, :] = ub[:, (2 * k + j) * width : (2 * k + j + 1) * width]
        to[8:9, :half] = qb[:, k * half : (k + 1) * half]
        to[8:9, half:] = vb[:, k * half : (k + 1) * half]
    for copy in done:
        copy.wait()


def last_gradient_call(token, s, b, early, b5):
    rows, width = s.h.shape
    half = width // 2
    args = (s.f.mixed, b.d1_low, s.h, b.dq, b.dkv, early[2], early[3], early[4])
    shapes = [((2 * half, width), BF)] * 2 + [((2 * width, half), BF)] * 2
    return pl.pallas_call(
        last_gradient_kernel,
        out_shape=results(shapes + [((16, width), F32)] * 2),
        in_specs=[IN_HBM] * 9 + [IN_VMEM] * 5,
        out_specs=(IN_HBM,) * 4 + (IN_VMEM,) * 2,
        scratch_shapes=buffers([(a.shape, BF) for a in args]) + buffers(shapes) + [pltpu.SemaphoreType.DMA((16,))],
        compiler_params=pltpu.CompilerParams(vmem_limit_bytes=VMEM_BYTES),
        cost_estimate=NO_COST,
        name="last_gradient",
    )(token, *args, early[5], b5.sums, b.sums, b5.bias_sums, b.bias_sums)


class Back(NamedTuple):
    d2_low: Any
    d_pre: Any
    d1_low: Any
    sums: Any
    bias_sums: Any
    dq: Any
    near: Any
    far: Any
    dkv: Any


def backward_call(which, slot_of, w, g, f, q, kv, kvp, d_mixed=None, tokens=(), early=None):
    rows, width = f.n1.shape
    hidden = 2 * w.up.shape[1]
    pairs, length = width // 128, 2 * rows
    low, wide, full = ((rows, width), BF), ((rows, hidden), BF), ((rows, width), F32)
    one = ((rows, 128), F32)
    twice = ((rows, 2 * width), BF)
    r_in = (low, low, one, low, one, wide, ((width, width), BF), ((width, hidden), BF), ((hidden, width), BF))
    r_out = RowsOut(low, wide, low)
    h_in = HeadsIn(low, ((pairs, 2, rows), F32), low, twice, twice)
    h_out = HeadsOut(low, twice, twice)
    h_work = HeadsWork(*[((pairs, length, 256), BF)] * 2, *[((pairs, length, 128), F32)] * 2)
    args, outs, out_specs, scratch = [], [], [], [low]
    if which & ROWS:
        args += [g, f.n2, f.inv2, f.n1, f.inv1, f.slope, w.out, w.up, w.down, w.out_far, w.up_far, w.down_far]
        outs += list(r_out) + [((8, width), F32), ((1, hidden), F32)]
        out_specs += [IN_HBM] * len(r_out) + [IN_VMEM] * 2
        scratch += list(r_in) + list(r_out) + [full]
    if which & HEADS:
        args += [f.mixed, f.lse, q, kv, kvp]
        scratch += list(h_in) + list(h_out) + list(h_work)
    if which == HEADS:
        args.append(d_mixed)
    if which == ROWS:
        half_up = ((width, hidden // 2), BF)
        args += [f.x1_low, early]
        outs += [low, half_up, half_up]
        out_specs += [IN_HBM] * 3
        scratch += [low, ((width, hidden), BF), half_up, half_up]
    if which & HEADS:
        outs += list(h_out)
        out_specs += [IN_HBM] * len(h_out)
    return pl.pallas_call(
        functools.partial(backward_kernel, which, slot_of, len(tokens)),
        out_shape=results(outs),
        in_specs=[IN_SMEM] * 4 + [IN_VMEM] + [IN_HBM] * (len(tokens) + len(args)),
        out_specs=tuple(out_specs),
        scratch_shapes=buffers(scratch) + [pltpu.SemaphoreType.DMA((32,))],
        compiler_params=pltpu.CompilerParams(vmem_limit_bytes=VMEM_BYTES),
        cost_estimate=NO_COST,
        name="layer_backward",
    )(w.counts, w.lengths, w.shift_own, w.shift_far, w.ng, *tokens, *args)


SWAP = [(0, 1), (1, 0)]


def to_peer(x):
    return lax.ppermute(x, "mp", SWAP)


def next_section(x):
    return lax.ppermute(x, "section", [(0, 1)])


def last_section(x):
    return lax.ppermute(x, "section", [(1, 0)])


def add_low(a, b):
    return (a.astype(F32) + b.astype(F32)).astype(BF)


def gate_kernel(*refs):
    pass


def tied(*xs, unread=()):
    hbm = pl.BlockSpec(memory_space=pl.ANY)
    return pl.pallas_call(
        gate_kernel,
        out_shape=tuple(jax.ShapeDtypeStruct(x.shape, x.dtype) for x in xs),
        in_specs=[hbm] * (len(xs) + len(unread)),
        out_specs=(hbm,) * len(xs),
        input_output_aliases={i: i for i in range(len(xs))},
        cost_estimate=NO_COST,
        name="gate",
    )(*xs, *unread)


class Sum:
    def __init__(self, x, size):
        self.whole = None
        if size < 4 or size % 4:
            self.whole = self.sent = lax.psum(x, "dp")
            return
        self.size = size
        self.steps = self.walk(x)
        self.got = next(self.steps)

    def walk(self, x):
        size = self.size
        line = size // 2
        half = line // 2
        me = lax.axis_index("dp")
        side = lax.rem(me, 2)
        place = me // 2
        pairs = [(i, i ^ 1) for i in range(size)]
        on_line = lambda moves: [(2 * a + s, 2 * b + s) for a, b in moves for s in range(2)]
        rows = x.shape[0] // 2
        x = x.reshape((2, rows) + x.shape[1:])
        keep = lax.dynamic_index_in_dim(x, side, 0, keepdims=False)
        send = lax.dynamic_index_in_dim(x, 1 - side, 0, keepdims=False)
        self.sent = send
        total = add_low(keep, (yield lax.ppermute(send, "dp", pairs)))
        self.sent = total
        for k in range(half - 1):
            moves = on_line([(k, k + 1), (line - 1 - k, line - 2 - k)])
            total = add_low(total, (yield lax.ppermute(total, "dp", moves)))
            self.sent = total
        moves = on_line([(half - 1, half), (half, half - 1)])
        total = add_low(total, (yield lax.ppermute(total, "dp", moves)))
        self.sent = total
        for k in reversed(range(half - 1)):
            moves = on_line([(k + 1, k), (line - 2 - k, line - 1 - k)])
            total = jnp.where((place == k) | (place == line - 1 - k), (yield lax.ppermute(total, "dp", moves)), total)
        got = yield lax.ppermute(total, "dp", pairs)
        self.whole = jnp.concatenate([jnp.where(side == 0, total, got), jnp.where(side == 0, got, total)], axis=0)
        yield None

    def take(self, got):
        self.got = self.steps.send(got)


def step_sums(sums, *others, unread=()):
    moving = [one for one in sums if one.whole is None]
    res = tied(*[one.got for one in moving], *others, unread=unread)
    for one, got in zip(moving, res):
        one.take(got)
    return res[len(moving) :]


class Layer(NamedTuple):
    q: Any
    kv: Any
    bq: Any
    bkv: Any
    out: Any
    up: Any
    down: Any
    out_far: Any
    up_far: Any
    down_far: Any
    bup_own: Any
    bup_far: Any
    ng: Any
    lb: Any
    counts: Any
    lengths: Any
    shift_own: Any
    shift_far: Any


class Saved(NamedTuple):
    h: Any
    q: Any
    kv: Any
    kvp: Any
    f: Any


def forward_tick(save, slot_of, h, w):
    kv = (dot_nn(h, w.kv) + w.bkv).astype(BF)
    kvp = to_peer(kv)
    q = (dot_nn(h, w.q) + w.bq).astype(BF)
    f = forward_call(save, slot_of, w, q, kv, kvp, h)
    return f.out, Saved(h, q, kv, kvp, f)


def rows_gradient(b, dq, dkv, w):
    return (b.d1_low.astype(F32) + dot_nt(dq, w.q) + dot_nt(dkv, w.kv)).astype(BF)


def backward_tick(slot_of, g, s, w):
    b = Back(*backward_call(ALL, slot_of, w, g, s.f, s.q, s.kv, s.kvp), None)
    b = b._replace(dkv=add_low(b.near, to_peer(b.far)))
    return rows_gradient(b, b.dq, b.dkv, w), b


def cut(x, which, size):
    return lax.slice_in_dim(x, which * size, (which + 1) * size, axis=1)


def on_device(
    tokens,
    grad_out,
    attention_in,
    attention_bias,
    attention_out,
    up_weight,
    up_bias,
    down_weight,
    norm_gains,
    layer_biases,
    block_counts,
    lengths,
    head_shifts,
):
    dp_size = lax.axis_size("dp")
    first = lax.axis_index("section") == 0
    width = tokens.shape[2]
    quarter = tokens.shape[1]
    half = attention_in.shape[3]
    hidden = up_weight.shape[2]

    crossed = lax.ppermute(jnp.where(first, grad_out[0], tokens[0]), "section", SWAP)
    from_rows = lambda x, s: jnp.concatenate([tokens[s], x], axis=0)
    cot_rows = lambda x, s: jnp.concatenate([x, grad_out[s]], axis=0)
    tok0, cot0 = from_rows(crossed, 0), cot_rows(crossed, 0)
    win, win_far = attention_in[0], to_peer(attention_in[0])
    ab, ab_far = attention_bias[0], to_peer(attention_bias)[0]
    bv = jnp.concatenate([ab[1], ab_far[1]])
    w = Layer(
        q=jnp.concatenate([win[:, 0], win_far[:, 0]], axis=1),
        kv=jnp.concatenate([win[:, 1], win_far[:, 1], win[:, 2], win_far[:, 2]], axis=1),
        bq=jnp.concatenate([ab[0], ab_far[0]]),
        bkv=jnp.concatenate([jnp.zeros_like(bv), bv]),
        out=attention_out[0],
        up=up_weight[0],
        down=down_weight[0],
        out_far=to_peer(attention_out[0]),
        up_far=to_peer(up_weight[0]),
        down_far=to_peer(down_weight[0]),
        bup_own=up_bias,
        bup_far=to_peer(up_bias),
        ng=norm_gains[0],
        lb=layer_biases[0],
        counts=block_counts,
        lengths=lengths,
        shift_own=head_shifts,
        shift_far=to_peer(head_shifts),
    )
    slot_one = lambda s: 0
    slot_a = lambda s: 1 - s
    slot_b = lambda s: s

    out1, _ = forward_tick(False, slot_one, tok0, w)
    tok1 = from_rows(last_section(tokens[1]), 1)
    out2, saved2 = forward_tick(True, slot_a, jnp.where(first, tok1, next_section(out1)), w)
    away2 = next_section(jnp.concatenate([out2, grad_out[1]], axis=0))
    g3, b3 = backward_tick(slot_a, cot0, saved2, w)
    away2, _ = tied(away2, b3.d2_low)
    away2, rows1 = away2[: 2 * quarter], away2[2 * quarter :]
    cot1 = cot_rows(rows1, 1)
    out4, saved4 = forward_tick(True, slot_b, jnp.where(first, tok0, away2), w)
    (away3,) = tied(last_section(g3), unread=(out4,))
    g5, b5 = backward_tick(slot_b, jnp.where(first, away3, cot1), saved4, w)

    early = gradient_call(saved4, b5)
    g6_in = jnp.where(first, last_section(g5), cot0)

    f6 = saved2.f
    d2_low = norm_back(g6_in.astype(F32), f6.n2.astype(F32), f6.inv2[:, :1], w.ng[1]).astype(BF)
    down_far = half_gradient_call(d2_low, f6.act, d2_low, early[0], 1, True)
    down_own = half_gradient_call(down_far, f6.act, d2_low, early[0], 0, True)
    down = Sum(add_low(down_own, to_peer(down_far)), dp_size)
    r6 = backward_call(ROWS, slot_a, w, g6_in, f6, None, None, None, None, (down.sent,), early[1])
    b6 = Back(*r6[:5], None, None, None, None)
    d_mixed, up_own, up_far = r6[5:]
    (up_far,) = step_sums([down], up_far)
    up_in = to_peer(up_far)
    up = Sum(add_low(up_own, up_in), dp_size)
    dq, near, far = backward_call(
        HEADS, slot_a, w, None, f6, saved2.q, saved2.kv, saved2.kvp, d_mixed, (down.sent, up.sent)
    )
    dq, near, far = step_sums([down, up], dq, near, far)
    b6 = b6._replace(dq=dq, dkv=add_low(near, to_peer(far)))
    out_own, out_far, in_own, in_far, small_own, small_far = last_gradient_call(up.sent, saved2, b6, early, b5)
    out_far, in_far, small_far, tick = step_sums([down, up], out_far, in_far, small_far, b6.bias_sums)
    inner = Sum(add_low(in_own, to_peer(in_far)), dp_size)
    small = small_own + to_peer(small_far)
    out_g = jnp.concatenate(
        [add_low(out_own, to_peer(out_far)), small.astype(BF), jnp.zeros((16, width), BF)], axis=0
    )
    last = Sum(out_g, dp_size)
    (tick,) = step_sums([inner], tick, unread=(last.sent,))
    (tick,) = step_sums([down, up, last], tick)
    (tick,) = step_sums([inner], tick)
    (tick,) = step_sums([last], tick)
    tick, dq, dkv = step_sums([up, inner], tick, b6.dq, b6.dkv)
    quarters = jnp.concatenate([out2[:quarter], out4[:quarter]], axis=0)
    tick, quarters = tied(tick, quarters, unread=(inner.sent, up.sent))
    layer_far = last_section(quarters)
    g6 = rows_gradient(b6, dq, dkv, w)
    tokens_far = next_section(jnp.concatenate([g5[quarter:], g6[quarter:]], axis=0))
    tick, layer_far = step_sums([last], tick, layer_far)
    tick, tokens_far = step_sums([down, inner], tick, tokens_far)
    (tick,) = step_sums([last], tick)
    while up.whole is None or down.whole is None:
        (tick,) = step_sums([up, down], tick)
    pair = lambda x, y: jnp.stack([x, y])
    layer_out = jnp.where(first, layer_far.reshape(tokens.shape), pair(out2[quarter:], out4[quarter:]))
    grad_tokens = jnp.where(first, pair(g5[:quarter], g6[:quarter]), tokens_far.reshape(tokens.shape))
    down_s = down.whole.astype(F32)
    up_s = up.whole.astype(F32)
    while inner.whole is None or last.whole is None:
        tick, down_s, up_s, layer_out, grad_tokens = step_sums(
            [inner, last], tick, down_s, up_s, layer_out, grad_tokens
        )
    out_s = last.whole
    in_s = jnp.concatenate([inner.whole, out_s[:half, :half], out_s[:half, half:]], axis=0).astype(F32)
    small = out_s[2 * half : 2 * half + 16].astype(F32)
    out_s = out_s[half : 2 * half].astype(F32)

    return (
        layer_out,
        grad_tokens,
        in_s.reshape(3, width, half).transpose(1, 0, 2)[None],
        small[8].reshape(1, 2, half),
        out_s[None],
        up_s[None],
        small[6:8].reshape(1, hidden),
        down_s[None],
        small[:2][None],
        small[2:6][None],
    )


def solution(mesh):
    tokens = P("dp", ("section", "mp"), None)
    weights = (
        P("section", None, None, "mp"),
        P("section", None, "mp"),
        P("section", "mp", None),
        P("section", None, "mp"),
        P("section", "mp"),
        P("section", "mp", None),
        P("section", None, None),
        P("section", None, None),
    )
    return jax.shard_map(
        on_device,
        mesh=mesh,
        in_specs=(tokens, tokens) + weights + (P("dp"), P("dp"), P("section", "mp")),
        out_specs=(tokens, tokens) + weights,
        check_vma=False,
    )
```

```python
import functools
import math
from typing import Any, NamedTuple

import jax
import jax.numpy as jnp
from jax import lax
from jax.experimental import pallas as pl
from jax.experimental.pallas import tpu as pltpu
from jax.sharding import PartitionSpec as P

BF = jnp.bfloat16
F32 = jnp.float32
EPS = 1e-05
SHUT = -1e30
TILE = 256
FORWARD_WINDOWS = (512, 528)
BACKWARD_WINDOWS = (528,)
CHUNK = 512
BLOCK = 64
VMEM_BYTES = 50 * 2**20
NO_COST = pl.CostEstimate(flops=1, bytes_accessed=1, transcendentals=0)


def dot_nn(a, b):
    return lax.dot_general(a, b, (((1,), (0,)), ((), ())), preferred_element_type=F32)


def dot_nt(a, b):
    return lax.dot_general(a, b, (((1,), (1,)), ((), ())), preferred_element_type=F32)


def dot_tn(a, b):
    return lax.dot_general(a, b, (((0,), (0,)), ((), ())), preferred_element_type=F32)


def mask_numbers(slot, counts, lengths):
    c = counts[slot]
    n = lengths[slot]
    third = (n + 2) // 3
    th1 = jnp.where(c == 3, third, (n + 1) // 2)
    th2 = jnp.where(c == 3, (2 * n + 2) // 3, 1 << 20)
    return th1, th2, n, c, lax.axis_index("mp")


def key_columns(nums, rows):
    th1, th2, n = nums[:3]
    u = lax.broadcasted_iota(jnp.int32, (rows, 128), 0)
    col = lax.broadcasted_iota(jnp.int32, (rows, 128), 1)
    blk = (u >= th1).astype(jnp.int32) + (u >= th2).astype(jnp.int32)
    open_ = (blk == col) & (u < n)
    one = jnp.where(col < 8, 1.0, 0.0)
    return jnp.where(col < 3, jnp.where(open_, 0.0, SHUT), one).astype(BF)


def query_rows(nums, shift, r0):
    th1, th2, _, c, _ = nums
    pos = r0 + lax.broadcasted_iota(jnp.int32, (16, TILE), 1)
    row = lax.broadcasted_iota(jnp.int32, (16, TILE), 0)
    t = (pos >= th1).astype(jnp.int32) + (pos >= th2).astype(jnp.int32) + shift
    t = jnp.where(t >= c, t - c, t)
    return jnp.where(row == t, 1.0, 0.0), row


def split3(x):
    a = x.astype(BF).astype(F32)
    b = (x - a).astype(BF).astype(F32)
    return a, b, (x - a - b).astype(BF).astype(F32)


def window_need(nums, r0):
    th1, th2, n, c, _ = nums
    last = r0 + TILE - 1
    whole = ((r0 < th1) == (last < th1)) & ((r0 < th2) == (last < th2))
    need = jnp.maximum(th1, jnp.minimum(th2, n) - (th1 // 16) * 16)
    need = jnp.maximum(need, jnp.where(c == 3, n - (th2 // 16) * 16, 0))
    return jnp.where(whole, need, 1 << 20)


def window_base(nums, shift, r0, limit):
    th1, th2, _, c, _ = nums
    t = jnp.where(r0 >= th1, 1, 0) + jnp.where(r0 >= th2, 1, 0) + shift
    t = jnp.where(t >= c, t - c, t)
    start = jnp.where(t == 0, 0, jnp.where(t == 1, th1, th2))
    return pl.multiple_of(jnp.minimum((start // 16) * 16, limit), 16)


def by_window(need, length, windows, body):
    prev = 0
    for width in windows:
        if width < length:

            @pl.when((need > prev) & (need <= width))
            def _(width=width):
                body(width)

            prev = width

    @pl.when(need > prev)
    def _():
        body(length)


def place_rows(dst, lanes, own, far, offset, core):
    pairs = dst.shape[0]
    for i in range(2):
        for who, ref in enumerate((own, far)):
            blk = 2 * i + jnp.where(core == who, 0, 1)
            rows = pl.ds(pl.multiple_of(blk * TILE, TILE), TILE)
            for p in range(pairs):
                src = offset + (p if who == 0 else (p + pairs // 2) % pairs) * 128
                dst[p, rows, lanes] = ref[i * TILE : (i + 1) * TILE, src : src + 128]


def place_values(v0, v1, own, far, offset, core):
    pairs = v0.shape[0]
    lane = lax.broadcasted_iota(jnp.int32, (TILE, 128), 1)
    ones = jnp.ones((TILE, 128), BF)
    for i in range(2):
        for who, ref in enumerate((own, far)):
            blk = 2 * i + jnp.where(core == who, 0, 1)
            rows = pl.ds(pl.multiple_of(blk * TILE, TILE), TILE)
            for p in range(pairs):
                src = offset + (p if who == 0 else (p + pairs // 2) % pairs) * 128
                x = ref[i * TILE : (i + 1) * TILE, src : src + 128]
                v0[p, rows, :] = jnp.where(lane < 64, x, ones)
                v1[p, rows, :] = jnp.where(lane < 64, ones, x)


def head_shift(own, far, j):
    heads = own.shape[1]
    if isinstance(j, int):
        return own[0, j] if j < heads else far[0, j - heads]
    return jnp.where(j < heads, own[0, jnp.minimum(j, heads - 1)], far[0, jnp.maximum(j - heads, 0)])


def attend(nums, shifts, q, kb, v0, v1, score, weight, top, mixed, lse):
    pairs, length = kb.shape[:2]
    th1, th2, _, c, core = nums
    heads = 2 * pairs
    lane = lax.broadcasted_iota(jnp.int32, (TILE, 128), 1)
    sub = lax.broadcasted_iota(jnp.int32, (TILE, 128), 0)

    @pl.loop(0, 2)
    def _(tile):
        r0 = (2 * tile + core) * TILE
        rows = pl.ds(pl.multiple_of(tile * TILE, TILE), TILE)
        behind = ((r0 + sub) >= th1).astype(jnp.int32) + ((r0 + sub) >= th2).astype(jnp.int32) - lane

        def body(width):
            outs = [None] * heads

            def window(j):
                shift = head_shift(*shifts, j)
                return pl.ds(window_base(nums, shift, r0, length - width) if width < length else 0, width)

            def scores(j):
                p, hh = divmod(j, 2)
                qn = q[rows, p * 128 : (p + 1) * 128].astype(F32) * 0.125
                d = behind + head_shift(*shifts, j)
                target = jnp.where((lane < c) & ((d == 0) | (d == c)), 1.0, 0.0)
                qm = jnp.where((lane >= 64) == (hh == 1), qn, 0.0)
                lhs = jnp.concatenate([qm.astype(BF), target.astype(BF)], axis=1)
                score[j % 2, :, 0:width] = dot_nt(lhs, kb[p, window(j), :])

            def softmax(j):
                for r in range(0, TILE, 128):
                    part = score[j % 2, r : r + 128, 0:width]
                    largest = jnp.max(part, axis=1, keepdims=True)
                    top[j % 4, r : r + 128, :] = jnp.broadcast_to(largest, (128, 128))
                    weight[j % 2, r : r + 128, 0:width] = jnp.exp(part - largest).astype(BF)

            def product(j):
                p, hh = divmod(j, 2)
                outs[j] = dot_nn(weight[j % 2, :, 0:width], (v0, v1)[hh][p, window(j), :])
                if hh == 1:
                    total = jnp.where(lane < 64, pltpu.roll(outs[j - 1], 64, 1), pltpu.roll(outs[j], 64, 1))
                    value = jnp.where(lane < 64, outs[j - 1], outs[j])
                    mixed[rows, p * 128 : (p + 1) * 128] = (value / total).astype(BF)
                    if lse is not None:
                        both = (jnp.where(lane < 64, top[(j - 1) % 4], top[j % 4]) + jnp.log(total)).T
                        lse[p, 0:1, rows] = both[0:1]
                        lse[p, 1:2, rows] = both[64:65]

            for step in range(heads + 2):
                if step < heads:
                    scores(step)
                if 1 <= step <= heads:
                    softmax(step - 1)
                if step >= 2:
                    product(step - 2)

        by_window(window_need(nums, r0), length, FORWARD_WINDOWS, body)


def attend_back(nums, shifts, q, do, mixed, lse, kb, vb, dka, dva, dq):
    pairs, length = kb.shape[:2]
    core = nums[4]
    sub = lax.broadcasted_iota(jnp.int32, (128, TILE), 0)
    lane = lax.broadcasted_iota(jnp.int32, (TILE, 128), 1)
    for tile in range(2):
        r0 = (2 * tile + core) * TILE
        rows = slice(tile * TILE, (tile + 1) * TILE)

        def body(width):
            @pl.loop(0, pairs, unroll=2)
            def _(p):
                lanes = pl.ds(pl.multiple_of(p * 128, 128), 128)
                qn = q[rows, lanes].astype(F32) * 0.125
                don = do[rows, lanes].astype(F32)
                qt = qn.T
                dot_ = don.T
                prod = dot_ * mixed[rows, lanes].astype(F32).T
                outs = []
                for hh in range(2):
                    shift = head_shift(*shifts, 2 * p + hh)
                    target, row = query_rows(nums, shift, r0)
                    la, lb, lc = split3(-lse[p, hh : hh + 1, rows])
                    target = target + jnp.where(row == 3, la, jnp.where(row == 4, lb, jnp.where(row == 5, lc, 0.0)))
                    keep = (sub >= 64) == (hh == 1)
                    zeros = jnp.zeros((112, TILE), BF)
                    rhs = jnp.concatenate([jnp.where(keep, qt, 0.0).astype(BF), target.astype(BF), zeros], axis=0)
                    da, db, dc = split3(-jnp.sum(prod[hh * 64 : (hh + 1) * 64], axis=0, keepdims=True))
                    minus = jnp.where(row == 3, da, jnp.where(row == 4, db, jnp.where(row == 5, dc, 0.0)))
                    rhs2 = jnp.concatenate([jnp.where(keep, dot_, 0.0).astype(BF), minus.astype(BF), zeros], axis=0)
                    keepl = (lane >= 64) == (hh == 1)
                    qm = jnp.where(keepl, qn, 0.0).astype(BF)
                    dom = jnp.where(keepl, don, 0.0).astype(BF)
                    start = window_base(nums, shift, r0, length - width) if width < length else 0
                    win = pl.ds(start, width)
                    kwin = kb[p, win, :]
                    pt = jnp.exp(dot_nn(kwin, rhs))
                    ds = (pt * dot_nn(vb[p, win, :], rhs2)).astype(BF)
                    dva[p, win, :] += dot_nn(pt.astype(BF), dom)
                    dka[p, win, :] += dot_nn(ds, qm)
                    kt = kwin[:, 0:128].T[hh * 64 : (hh + 1) * 64]
                    outs.append(dot_nn(kt, ds))
                dq[rows, lanes] = (jnp.concatenate(outs, axis=0) * 0.125).T.astype(BF)

        by_window(window_need(nums, r0), length, BACKWARD_WINDOWS, body)


def gelu_pair(x):
    density = jnp.exp(x * x * (-0.5)) * (2.0 * math.pi) ** (-0.5)
    cdf = 0.5 + 0.5 * lax.erf(x * (2.0 ** (-0.5)))
    return x * cdf, cdf + x * density


def norm_rows(x):
    scale = 1.0 / x.shape[-1]
    centred = x - jnp.sum(x, axis=-1, keepdims=True) * scale
    inv = lax.rsqrt(jnp.sum(centred * centred, axis=-1, keepdims=True) * scale + EPS)
    return centred * inv, inv


def norm_back(up, normed, inv, gain):
    scale = 1.0 / normed.shape[-1]
    e = up * gain
    a = jnp.sum(e, axis=-1, keepdims=True) * scale
    b = jnp.sum(e * normed, axis=-1, keepdims=True) * scale
    return inv * (e - a - normed * b)


def copier(sems):
    used = [0]

    def start(src, dst):
        copy = pltpu.make_async_copy(src, dst, sems.at[used[0]])
        used[0] += 1
        copy.start()
        return copy

    return start


class ForwardIn(NamedTuple):
    q: Any
    kv: Any
    kvp: Any
    h: Any
    wout: Any
    wup: Any
    wdown: Any
    wout_far: Any
    wup_far: Any
    wdown_far: Any


class ForwardOut(NamedTuple):
    out: Any
    mixed: Any
    lse: Any
    x1_low: Any
    act: Any
    slope: Any
    n1: Any
    inv1: Any
    n2: Any
    inv2: Any


class ForwardWork(NamedTuple):
    kb: Any
    v0: Any
    v1: Any
    score: Any
    weight: Any
    top: Any
    pre: Any
    x1: Any
    acc: Any


def weight_copies(start, src, x):
    c_out, c_up, c_down = [], [], []
    for j, (out, up, down) in enumerate(((src.wout, src.wup, src.wdown), (src.wout_far, src.wup_far, src.wdown_far))):
        rows, cols = out.shape[0], up.shape[1]
        c_out.append(start(out, x.wout.at[j * rows : (j + 1) * rows, :]))
        c_up.append(start(up, x.wup.at[:, j * cols : (j + 1) * cols]))
        c_down.append(start(down, x.wdown.at[j * cols : (j + 1) * cols, :]))
    return c_out, c_up, c_down


def forward_kernel(save, slot_of, tokens, counts, lengths, shift_own, shift_far, lb, ng, bup_own, bup_far, *refs):
    refs = list(refs[tokens:])
    take = lambda kind: kind(*[refs.pop(0) for _ in range(len(kind._fields))])
    src = take(ForwardIn)
    dst = take(ForwardOut) if save else ForwardOut(refs.pop(0), *[None] * 9)
    x = ForwardIn(*[refs.pop(0) for _ in range(7)], None, None, None)
    y = take(ForwardOut)
    t = take(ForwardWork)
    start = copier(refs[0])
    rows, width = x.h.shape
    hidden = x.wup.shape[1]
    half = hidden // 2
    load = ForwardIn(*[None] * 10)._replace(
        kv=start(src.kv, x.kv),
        kvp=start(src.kvp, x.kvp),
        q=start(src.q, x.q),
        h=start(src.h, x.h),
    )
    c_out, c_up, c_down = weight_copies(start, src, x)
    done = []

    def ship(a, b):
        if b is not None:
            done.append(start(a, b))

    def ship_part(a, b, part):
        if b is not None:
            done.append(start(a.at[:, part], b.at[:, part]))

    nums = mask_numbers(slot_of(lax.axis_index("section")), counts, lengths)
    core = nums[4]
    ext = key_columns(nums, t.kb.shape[1])
    for p in range(t.kb.shape[0]):
        t.kb[p, :, 128:256] = ext
    load.kv.wait()
    load.kvp.wait()
    place_rows(t.kb, slice(0, 128), x.kv, x.kvp, 0, core)
    place_values(t.v0, t.v1, x.kv, x.kvp, width, core)
    load.q.wait()
    attend(
        nums, (shift_own, shift_far), x.q, t.kb, t.v0, t.v1, t.score, t.weight, t.top, y.mixed, y.lse if save else None
    )
    ship(y.mixed, dst.mixed)
    ship(y.lse, dst.lse)
    for copy in c_out:
        copy.wait()
    t.acc[...] = dot_nn(y.mixed[...], x.wout[...])
    load.h.wait()
    for r in range(0, rows, BLOCK):
        rs = slice(r, r + BLOCK)
        normed, inv = norm_rows(x.h[rs, :].astype(F32) + t.acc[rs, :] + lb[0:1, :])
        if save:
            y.n1[rs, :] = normed.astype(BF)
            y.inv1[rs, :] = jnp.broadcast_to(inv, (BLOCK, 128))
        full = normed * ng[0:1, :] + lb[1:2, :]
        t.x1[rs, :] = full
        y.x1_low[rs, :] = full.astype(BF)
    ship(y.x1_low, dst.x1_low)
    ship(y.n1, dst.n1)
    ship(y.inv1, dst.inv1)
    chunks = hidden // CHUNK

    def up(j):
        t.pre[j % 2] = dot_nn(y.x1_low[...], x.wup[:, j * CHUNK : (j + 1) * CHUNK])

    def activate(j):
        part = slice(j * CHUNK, (j + 1) * CHUNK)
        low = (j * CHUNK) % half
        bias = (bup_own if j < chunks // 2 else bup_far)[0:1, low : low + CHUNK]
        for r in range(0, rows, BLOCK):
            rs = slice(r, r + BLOCK)
            act, slope = gelu_pair(t.pre[j % 2, rs, :] + bias)
            y.act[rs, part] = act.astype(BF)
            if save:
                y.slope[rs, part] = slope.astype(BF)

    c_up[0].wait()
    up(0)
    for j in range(chunks // 2):
        if j + 1 == chunks // 2:
            c_up[1].wait()
        up(j + 1)
        activate(j)
    ship_part(y.act, dst.act, slice(0, half))
    ship_part(y.slope, dst.slope, slice(0, half))
    c_down[0].wait()
    t.acc[...] = dot_nn(y.act[:, :half], x.wdown[:half, :])
    for j in range(chunks // 2, chunks):
        if j + 1 < chunks:
            up(j + 1)
        activate(j)
    ship_part(y.act, dst.act, slice(half, hidden))
    ship_part(y.slope, dst.slope, slice(half, hidden))
    c_down[1].wait()
    t.acc[...] += dot_nn(y.act[:, half:], x.wdown[half:, :])
    for r in range(0, rows, BLOCK):
        rs = slice(r, r + BLOCK)
        normed, inv = norm_rows(t.x1[rs, :] + t.acc[rs, :] + lb[2:3, :])
        if save:
            y.n2[rs, :] = normed.astype(BF)
            y.inv2[rs, :] = jnp.broadcast_to(inv, (BLOCK, 128))
        y.out[rs, :] = (normed * ng[1:2, :] + lb[3:4, :]).astype(BF)
    ship(y.out, dst.out)
    ship(y.n2, dst.n2)
    ship(y.inv2, dst.inv2)
    for copy in done:
        copy.wait()


def buffers(shapes):
    return [pltpu.VMEM(*s) for s in shapes]


def results(shapes):
    return tuple(jax.ShapeDtypeStruct(*s) for s in shapes)


IN_SMEM = pl.BlockSpec(memory_space=pltpu.SMEM)
IN_VMEM = pl.BlockSpec(memory_space=pltpu.VMEM)
IN_HBM = pl.BlockSpec(memory_space=pltpu.HBM)


def forward_call(save, slot_of, w, q, kv, kvp, h, tokens=()):
    rows, width = h.shape
    hidden = 2 * w.up.shape[1]
    pairs, length = width // 128, 2 * rows
    low, wide, full = ((rows, width), BF), ((rows, hidden), BF), ((rows, width), F32)
    one, twice = ((rows, 128), F32), ((rows, 2 * width), BF)
    shapes_in = (low, twice, twice, low, ((width, width), BF), ((width, hidden), BF), ((hidden, width), BF))
    shapes_out = ForwardOut(low, low, ((pairs, 2, rows), F32), low, wide, wide, low, one, low, one)
    if not save:
        gone = ((16, 128), BF)
        scratch_out = shapes_out._replace(lse=gone, slope=gone, n1=gone, inv1=gone, n2=gone, inv2=gone)
    else:
        scratch_out = shapes_out
    work = ForwardWork(
        ((pairs, length, 256), BF),
        ((pairs, length, 128), BF),
        ((pairs, length, 128), BF),
        ((2, TILE, length), F32),
        ((2, TILE, length), BF),
        ((4, TILE, 128), F32),
        ((2, rows, CHUNK), F32),
        full,
        full,
    )
    outs = shapes_out if save else shapes_out[:1]
    res = pl.pallas_call(
        functools.partial(forward_kernel, save, slot_of, len(tokens)),
        out_shape=results(outs),
        in_specs=[IN_SMEM] * 4 + [IN_VMEM] * 4 + [IN_HBM] * (10 + len(tokens)),
        out_specs=(IN_HBM,) * len(outs),
        scratch_shapes=buffers(shapes_in) + buffers(scratch_out) + buffers(work) + [pltpu.SemaphoreType.DMA((24,))],
        compiler_params=pltpu.CompilerParams(vmem_limit_bytes=VMEM_BYTES),
        cost_estimate=NO_COST,
        name="layer_forward",
    )(
        w.counts, w.lengths, w.shift_own, w.shift_far, w.lb, w.ng, w.bup_own, w.bup_far, *tokens,
        q, kv, kvp, h, w.out, w.up, w.down, w.out_far, w.up_far, w.down_far,
    )
    return ForwardOut(*res) if save else ForwardOut(res[0], *[None] * 9)


class RowsIn(NamedTuple):
    g: Any
    n2: Any
    inv2: Any
    n1: Any
    inv1: Any
    slope: Any
    wout: Any
    wup: Any
    wdown: Any
    wout_far: Any
    wup_far: Any
    wdown_far: Any


class RowsOut(NamedTuple):
    d2_low: Any
    d_pre: Any
    d1_low: Any


class HeadsIn(NamedTuple):
    mixed: Any
    lse: Any
    q: Any
    kv: Any
    kvp: Any


class HeadsOut(NamedTuple):
    dq: Any
    near: Any
    far: Any


class HeadsWork(NamedTuple):
    kb: Any
    vb: Any
    dka: Any
    dva: Any


def rows_back(start, src, dst, x, y, d_mixed, dx, ng, sums, bias_sums, behind, up_refs):
    rows, width = x.g.shape
    hidden = x.wup.shape[1]
    half = hidden // 2
    chunks = hidden // CHUNK
    soon = [start(src.g, x.g), start(src.n2, x.n2), start(src.inv2, x.inv2)]
    c_slope = [
        start(src.slope.at[:, part], x.slope.at[:, part]) for part in (slice(0, half), slice(half, hidden))
    ]
    c_out, c_up, c_down = weight_copies(start, src, x)
    late = [start(src.n1, x.n1), start(src.inv1, x.inv1)]
    if up_refs:
        x1_h, early_h, outs_h, x1, early, outs = up_refs
        up_load = [start(x1_h, x1), start(early_h, early)]
    behind()
    done = []
    zero = jnp.zeros((1, width), F32)
    s_gn, s_g, s_d2 = zero, zero, zero
    for copy in soon:
        copy.wait()
    for r in range(0, rows, BLOCK):
        rs = slice(r, r + BLOCK)
        g = x.g[rs, :].astype(F32)
        normed = x.n2[rs, :].astype(F32)
        d2 = norm_back(g, normed, x.inv2[rs, 0:1], ng[1:2, :])
        dx[rs, :] = d2
        y.d2_low[rs, :] = d2.astype(BF)
        s_gn += jnp.sum(g * normed, axis=0, keepdims=True)
        s_g += jnp.sum(g, axis=0, keepdims=True)
        s_d2 += jnp.sum(d2, axis=0, keepdims=True)
    done.append(start(y.d2_low, dst.d2_low))
    for k in range(2):
        c_down[k].wait()
        c_slope[k].wait()
        for j in range(k * chunks // 2, (k + 1) * chunks // 2):
            part = slice(j * CHUNK, (j + 1) * CHUNK)
            d_act = dot_nt(y.d2_low[...], x.wdown[part, :])
            d_pre = (d_act * x.slope[:, part].astype(F32)).astype(BF)
            y.d_pre[:, part] = d_pre
            bias_sums[0:1, part] = jnp.sum(d_pre.astype(F32), axis=0, keepdims=True)
        part = slice(k * half, (k + 1) * half)
        done.append(start(y.d_pre.at[:, part], dst.d_pre.at[:, part]))
        c_up[k].wait()
        dx[...] += dot_nt(y.d_pre[:, part], x.wup[:, part])
    def up_gradient(k):
        if up_refs:
            for j in range(2):
                to = slice(j * half // 2, (j + 1) * half // 2)
                at = slice(k * half + j * half // 2, k * half + (j + 1) * half // 2)
                outs[k][:, to] = (dot_tn(x1[...], y.d_pre[:, at]) + early[:, at].astype(F32)).astype(BF)
            done.append(start(outs[k], outs_h[k]))

    if up_refs:
        for copy in up_load:
            copy.wait()
    up_gradient(1)
    s_dn, s_dx, s_d1 = zero, zero, zero
    late[0].wait()
    late[1].wait()
    for r in range(0, rows, BLOCK):
        rs = slice(r, r + BLOCK)
        g = dx[rs, :]
        normed = x.n1[rs, :].astype(F32)
        d1 = norm_back(g, normed, x.inv1[rs, 0:1], ng[0:1, :])
        y.d1_low[rs, :] = d1.astype(BF)
        s_dn += jnp.sum(g * normed, axis=0, keepdims=True)
        s_dx += jnp.sum(g, axis=0, keepdims=True)
        s_d1 += jnp.sum(d1, axis=0, keepdims=True)
    done.append(start(y.d1_low, dst.d1_low))
    for i, s in enumerate((s_dn, s_gn, s_d1, s_dx, s_d2, s_g)):
        sums[i : i + 1, :] = s
    sums[6:8, :] = jnp.zeros((2, width), F32)
    for copy in c_out:
        copy.wait()
    d_mixed[...] = dot_nt(y.d1_low[...], x.wout[...]).astype(BF)
    up_gradient(0)
    return done


def heads_back(start, load, dst, x, y, t, d_mixed, nums, shifts):
    width = x.q.shape[1]
    core = nums[4]
    pairs = t.kb.shape[0]
    ext = key_columns(nums, t.kb.shape[1])
    for p in range(pairs):
        t.kb[p, :, 128:256] = ext
        t.vb[p, :, 128:256] = ext
    for copy in load:
        copy.wait()
    place_rows(t.kb, slice(0, 128), x.kv, x.kvp, 0, core)
    place_rows(t.vb, slice(0, 128), x.kv, x.kvp, width, core)
    t.dka[...] = jnp.zeros_like(t.dka)
    t.dva[...] = jnp.zeros_like(t.dva)
    attend_back(nums, shifts, x.q, d_mixed, x.mixed, x.lse, t.kb, t.vb, t.dka, t.dva, y.dq)
    done = [start(y.dq, dst.dq)]
    for to, side, turn in ((y.far, 1 - core, pairs // 2), (y.near, core, 0)):
        for i in range(2):
            mine = pl.ds(pl.multiple_of((2 * i + side) * TILE, TILE), TILE)
            for p in range(pairs):
                for j, total in enumerate((t.dka, t.dva)):
                    lanes = slice(j * width + p * 128, j * width + (p + 1) * 128)
                    to[i * TILE : (i + 1) * TILE, lanes] = total[(p + turn) % pairs, mine, :].astype(to.dtype)
    done += [start(y.far, dst.far), start(y.near, dst.near)]
    return done


ALL, ROWS, HEADS = 3, 1, 2


def backward_kernel(which, slot_of, tokens, counts, lengths, shift_own, shift_far, ng, *refs):
    refs = list(refs[tokens:])
    take = lambda kind: kind(*[refs.pop(0) for _ in range(len(kind._fields))])
    rows_on, heads_on = which & ROWS, which & HEADS
    if rows_on:
        r_src = take(RowsIn)
    if heads_on:
        h_src = take(HeadsIn)
    if which == HEADS:
        mixed_src = refs.pop(0)
    if which == ROWS:
        up_refs = [refs.pop(0), refs.pop(0)]
    if rows_on:
        r_dst = take(RowsOut)
        sums, bias_sums = refs.pop(0), refs.pop(0)
    if which == ROWS:
        mixed_dst = refs.pop(0)
        up_refs.append([refs.pop(0), refs.pop(0)])
    if heads_on:
        h_dst = take(HeadsOut)
    d_mixed = refs.pop(0)
    if rows_on:
        r_x = RowsIn(*[refs.pop(0) for _ in range(9)], None, None, None)
        r_y, dx = take(RowsOut), refs.pop(0)
    if which == ROWS:
        up_refs += [refs.pop(0), refs.pop(0), [refs.pop(0), refs.pop(0)]]
    if heads_on:
        h_x, h_y, h_t = take(HeadsIn), take(HeadsOut), take(HeadsWork)
    start = copier(refs[0])
    load, done = [], []

    def load_heads():
        if heads_on:
            load.extend(start(a, b) for a, b in zip(h_src, h_x))

    if rows_on:
        up_refs = up_refs if which == ROWS else None
        done += rows_back(start, r_src, r_dst, r_x, r_y, d_mixed, dx, ng, sums, bias_sums, load_heads, up_refs)
    else:
        load_heads()
        load.append(start(mixed_src, d_mixed))
    if which == ROWS:
        done.append(start(d_mixed, mixed_dst))
    if heads_on:
        nums = mask_numbers(slot_of(lax.axis_index("section")), counts, lengths)
        done += heads_back(start, load, h_dst, h_x, h_y, h_t, d_mixed, nums, (shift_own, shift_far))
    for copy in done:
        copy.wait()


def gradient_kernel(*refs):
    refs = list(refs)
    src = [refs.pop(0) for _ in range(9)]
    dst = [refs.pop(0) for _ in range(5)]
    col_sums = refs.pop(0)
    x = [refs.pop(0) for _ in range(9)]
    y = [refs.pop(0) for _ in range(5)]
    start = copier(refs[0])
    load = [start(a, b) for a, b in zip(src, x)]
    done = []
    act, d2_low, x1_low, d_pre, mixed, d1_low, h, dq, dkv = range(9)
    for k, (left, right) in enumerate(((act, d2_low), (x1_low, d_pre), (mixed, d1_low), (h, dq), (h, dkv))):
        for i in (left, right):
            if load[i] is not None:
                load[i].wait()
                load[i] = None
        tall, broad = y[k].shape
        slab = CHUNK if max(tall, broad) % CHUNK == 0 else TILE
        for j in range(max(tall, broad) // slab):
            part = slice(j * slab, (j + 1) * slab)
            if tall > broad:
                y[k][part, :] = dot_tn(x[left][:, part], x[right][...]).astype(BF)
                done.append(start(y[k].at[part, :], dst[k].at[part, :]))
            else:
                y[k][:, part] = dot_tn(x[left][...], x[right][:, part]).astype(BF)
                done.append(start(y[k].at[:, part], dst[k].at[:, part]))
    width = x[h].shape[1]
    col_sums[0:1, :] = jnp.sum(x[dq][...].astype(F32), axis=0, keepdims=True)
    col_sums[1:2, :] = jnp.sum(x[dkv][:, width:].astype(F32), axis=0, keepdims=True)
    for copy in done:
        copy.wait()


def gradient_call(s, b):
    f = s.f
    rows, width = s.h.shape
    hidden = f.act.shape[1]
    args = (f.act, b.d2_low, f.x1_low, b.d_pre, f.mixed, b.d1_low, s.h, b.dq, b.dkv)
    shapes = [
        ((hidden, width), BF), ((width, hidden), BF), ((width, width), BF), ((width, width), BF), ((width, 2 * width), BF),
    ]
    return pl.pallas_call(
        gradient_kernel,
        out_shape=results(shapes + [((2, width), F32)]),
        in_specs=[IN_HBM] * 9,
        out_specs=(IN_HBM,) * 5 + (IN_VMEM,),
        scratch_shapes=buffers([(a.shape, BF) for a in args]) + buffers(shapes) + [pltpu.SemaphoreType.DMA((40,))],
        compiler_params=pltpu.CompilerParams(vmem_limit_bytes=VMEM_BYTES),
        cost_estimate=NO_COST,
        name="layer_gradient",
    )(*args)


def half_gradient_kernel(k, by_rows, token, left_h, right_h, early_h, out_h, left, right, early, out, sems):
    start = copier(sems)
    tall, broad = out.shape
    if by_rows:
        load = [start(left_h.at[:, k * tall : (k + 1) * tall], left), start(right_h, right)]
        before = start(early_h.at[k * tall : (k + 1) * tall, :], early)
    else:
        load = [start(left_h, left), start(right_h.at[:, k * broad : (k + 1) * broad], right)]
        before = start(early_h.at[:, k * broad : (k + 1) * broad], early)
    for copy in load:
        copy.wait()
    before.wait()
    done = []
    for j in range(2):
        if by_rows:
            part = slice(j * tall // 2, (j + 1) * tall // 2)
            out[part, :] = (dot_tn(left[:, part], right[...]) + early[part, :].astype(F32)).astype(BF)
            done.append(start(out.at[part, :], out_h.at[part, :]))
        else:
            part = slice(j * broad // 2, (j + 1) * broad // 2)
            out[:, part] = (dot_tn(left[...], right[:, part]) + early[:, part].astype(F32)).astype(BF)
            done.append(start(out.at[:, part], out_h.at[:, part]))
    for copy in done:
        copy.wait()


def half_gradient_call(token, left, right, early, k, by_rows):
    rows = left.shape[0]
    tall, broad = early.shape
    tall, broad = (tall // 2, broad) if by_rows else (tall, broad // 2)
    out = ((tall, broad), BF)
    return pl.pallas_call(
        functools.partial(half_gradient_kernel, k, by_rows),
        out_shape=jax.ShapeDtypeStruct(*out),
        in_specs=[IN_HBM] * 4,
        out_specs=IN_HBM,
        scratch_shapes=buffers([((rows, tall), BF), ((rows, broad), BF), out, out]) + [pltpu.SemaphoreType.DMA((5,))],
        compiler_params=pltpu.CompilerParams(vmem_limit_bytes=VMEM_BYTES),
        cost_estimate=NO_COST,
        name="half_gradient",
    )(token, left, right, early)


def last_gradient_kernel(*refs):
    token, mixed_h, d1_h, h_h, dq_h, dkv_h, eo_h, eq_h, ekv_h, c5, s5, s6, u5, u6, *refs = refs
    outs, refs = refs[:4], refs[4:]
    small_own, small_far, mixed, d1, h, dq, dkv, eo, eq, ekv, oo, fo, oi, fi, sems = refs
    start = copier(sems)
    pairs = ((h_h, h), (dq_h, dq), (eq_h, eq), (dkv_h, dkv), (ekv_h, ekv), (mixed_h, mixed), (d1_h, d1), (eo_h, eo))
    load = [start(a, b) for a, b in pairs]
    width = h.shape[1]
    half = width // 2
    done = []
    for copy in load[:5]:
        copy.wait()
    for k, to, away in ((1, fi, outs[3]), (0, oi, outs[2])):
        for part, (right, before) in enumerate(((dq, eq), (dkv, ekv))):
            lanes = slice(k * half, (k + 1) * half)
            total = dot_tn(h[...], right[:, lanes]) + before[:, lanes].astype(F32)
            to[part * width : (part + 1) * width, :] = total.astype(BF)
        done.append(start(to, away))
    for copy in load[5:]:
        copy.wait()
    for k, to, away in ((1, fo, outs[1]), (0, oo, outs[0])):
        lanes = slice(width + k * half, width + (k + 1) * half)
        total = (dot_tn(h[...], dkv[:, lanes]) + ekv[:, lanes].astype(F32)).astype(BF)
        to[0:half, 0:half] = total[0:half]
        to[0:half, half:] = total[half:]
        lanes = slice(k * half, (k + 1) * half)
        to[half : 2 * half, :] = (dot_tn(mixed[:, lanes], d1[...]) + eo[lanes, :].astype(F32)).astype(BF)
        done.append(start(to, away))
    qb = c5[0:1, :] + jnp.sum(dq[...].astype(F32), axis=0, keepdims=True)
    vb = c5[1:2, :] + jnp.sum(dkv[:, width:].astype(F32), axis=0, keepdims=True)
    ub = u5[...] + u6[...]
    for k, to in ((0, small_own), (1, small_far)):
        to[...] = jnp.zeros_like(to)
        to[0:6, :] = s5[0:6, :] + s6[0:6, :]
        for j in range(2):
            to[6 + j : 7 + j, :] = ub[:, (2 * k + j) * width : (2 * k + j + 1) * width]
        to[8:9, :half] = qb[:, k * half : (k + 1) * half]
        to[8:9, half:] = vb[:, k * half : (k + 1) * half]
    for copy in done:
        copy.wait()


def last_gradient_call(token, s, b, early, b5):
    rows, width = s.h.shape
    half = width // 2
    args = (s.f.mixed, b.d1_low, s.h, b.dq, b.dkv, early[2], early[3], early[4])
    shapes = [((2 * half, width), BF)] * 2 + [((2 * width, half), BF)] * 2
    return pl.pallas_call(
        last_gradient_kernel,
        out_shape=results(shapes + [((16, width), F32)] * 2),
        in_specs=[IN_HBM] * 9 + [IN_VMEM] * 5,
        out_specs=(IN_HBM,) * 4 + (IN_VMEM,) * 2,
        scratch_shapes=buffers([(a.shape, BF) for a in args]) + buffers(shapes) + [pltpu.SemaphoreType.DMA((16,))],
        compiler_params=pltpu.CompilerParams(vmem_limit_bytes=VMEM_BYTES),
        cost_estimate=NO_COST,
        name="last_gradient",
    )(token, *args, early[5], b5.sums, b.sums, b5.bias_sums, b.bias_sums)


class Back(NamedTuple):
    d2_low: Any
    d_pre: Any
    d1_low: Any
    sums: Any
    bias_sums: Any
    dq: Any
    near: Any
    far: Any
    dkv: Any


def backward_call(which, slot_of, w, g, f, q, kv, kvp, d_mixed=None, tokens=(), early=None):
    rows, width = f.n1.shape
    hidden = 2 * w.up.shape[1]
    pairs, length = width // 128, 2 * rows
    low, wide, full = ((rows, width), BF), ((rows, hidden), BF), ((rows, width), F32)
    one = ((rows, 128), F32)
    twice = ((rows, 2 * width), BF)
    r_in = (low, low, one, low, one, wide, ((width, width), BF), ((width, hidden), BF), ((hidden, width), BF))
    r_out = RowsOut(low, wide, low)
    h_in = HeadsIn(low, ((pairs, 2, rows), F32), low, twice, twice)
    h_out = HeadsOut(low, twice, twice)
    h_work = HeadsWork(*[((pairs, length, 256), BF)] * 2, *[((pairs, length, 128), F32)] * 2)
    args, outs, out_specs, scratch = [], [], [], [low]
    if which & ROWS:
        args += [g, f.n2, f.inv2, f.n1, f.inv1, f.slope, w.out, w.up, w.down, w.out_far, w.up_far, w.down_far]
        outs += list(r_out) + [((8, width), F32), ((1, hidden), F32)]
        out_specs += [IN_HBM] * len(r_out) + [IN_VMEM] * 2
        scratch += list(r_in) + list(r_out) + [full]
    if which & HEADS:
        args += [f.mixed, f.lse, q, kv, kvp]
        scratch += list(h_in) + list(h_out) + list(h_work)
    if which == HEADS:
        args.append(d_mixed)
    if which == ROWS:
        half_up = ((width, hidden // 2), BF)
        args += [f.x1_low, early]
        outs += [low, half_up, half_up]
        out_specs += [IN_HBM] * 3
        scratch += [low, ((width, hidden), BF), half_up, half_up]
    if which & HEADS:
        outs += list(h_out)
        out_specs += [IN_HBM] * len(h_out)
    return pl.pallas_call(
        functools.partial(backward_kernel, which, slot_of, len(tokens)),
        out_shape=results(outs),
        in_specs=[IN_SMEM] * 4 + [IN_VMEM] + [IN_HBM] * (len(tokens) + len(args)),
        out_specs=tuple(out_specs),
        scratch_shapes=buffers(scratch) + [pltpu.SemaphoreType.DMA((32,))],
        compiler_params=pltpu.CompilerParams(vmem_limit_bytes=VMEM_BYTES),
        cost_estimate=NO_COST,
        name="layer_backward",
    )(w.counts, w.lengths, w.shift_own, w.shift_far, w.ng, *tokens, *args)


SWAP = [(0, 1), (1, 0)]


def to_peer(x):
    return lax.ppermute(x, "mp", SWAP)


def next_section(x):
    return lax.ppermute(x, "section", [(0, 1)])


def last_section(x):
    return lax.ppermute(x, "section", [(1, 0)])


def add_low(a, b):
    return (a.astype(F32) + b.astype(F32)).astype(BF)


def gate_kernel(*refs):
    pass


def tied(*xs, unread=()):
    hbm = pl.BlockSpec(memory_space=pl.ANY)
    return pl.pallas_call(
        gate_kernel,
        out_shape=tuple(jax.ShapeDtypeStruct(x.shape, x.dtype) for x in xs),
        in_specs=[hbm] * (len(xs) + len(unread)),
        out_specs=(hbm,) * len(xs),
        input_output_aliases={i: i for i in range(len(xs))},
        cost_estimate=NO_COST,
        name="gate",
    )(*xs, *unread)


class Sum:
    def __init__(self, x, size):
        self.whole = None
        if size < 4 or size % 4:
            self.whole = self.sent = lax.psum(x, "dp")
            return
        self.size = size
        self.steps = self.walk(x)
        self.got = next(self.steps)

    def walk(self, x):
        size = self.size
        line = size // 2
        half = line // 2
        me = lax.axis_index("dp")
        side = lax.rem(me, 2)
        place = me // 2
        pairs = [(i, i ^ 1) for i in range(size)]
        on_line = lambda moves: [(2 * a + s, 2 * b + s) for a, b in moves for s in range(2)]
        rows = x.shape[0] // 2
        x = x.reshape((2, rows) + x.shape[1:])
        keep = lax.dynamic_index_in_dim(x, side, 0, keepdims=False)
        send = lax.dynamic_index_in_dim(x, 1 - side, 0, keepdims=False)
        self.sent = send
        total = add_low(keep, (yield lax.ppermute(send, "dp", pairs)))
        self.sent = total
        for k in range(half - 1):
            moves = on_line([(k, k + 1), (line - 1 - k, line - 2 - k)])
            total = add_low(total, (yield lax.ppermute(total, "dp", moves)))
            self.sent = total
        moves = on_line([(half - 1, half), (half, half - 1)])
        total = add_low(total, (yield lax.ppermute(total, "dp", moves)))
        self.sent = total
        for k in reversed(range(half - 1)):
            moves = on_line([(k + 1, k), (line - 2 - k, line - 1 - k)])
            total = jnp.where((place == k) | (place == line - 1 - k), (yield lax.ppermute(total, "dp", moves)), total)
        got = yield lax.ppermute(total, "dp", pairs)
        self.whole = jnp.concatenate([jnp.where(side == 0, total, got), jnp.where(side == 0, got, total)], axis=0)
        yield None

    def take(self, got):
        self.got = self.steps.send(got)


def step_sums(sums, *others, unread=()):
    moving = [one for one in sums if one.whole is None]
    res = tied(*[one.got for one in moving], *others, unread=unread)
    for one, got in zip(moving, res):
        one.take(got)
    return res[len(moving) :]


class Layer(NamedTuple):
    q: Any
    kv: Any
    bq: Any
    bkv: Any
    out: Any
    up: Any
    down: Any
    out_far: Any
    up_far: Any
    down_far: Any
    bup_own: Any
    bup_far: Any
    ng: Any
    lb: Any
    counts: Any
    lengths: Any
    shift_own: Any
    shift_far: Any


class Saved(NamedTuple):
    h: Any
    q: Any
    kv: Any
    kvp: Any
    f: Any


def forward_tick(save, slot_of, h, w):
    kv = (dot_nn(h, w.kv) + w.bkv).astype(BF)
    kvp = to_peer(kv)
    q = (dot_nn(h, w.q) + w.bq).astype(BF)
    f = forward_call(save, slot_of, w, q, kv, kvp, h)
    return f.out, Saved(h, q, kv, kvp, f)


def rows_gradient(b, dq, dkv, w):
    return (b.d1_low.astype(F32) + dot_nt(dq, w.q) + dot_nt(dkv, w.kv)).astype(BF)


def backward_tick(slot_of, g, s, w):
    b = Back(*backward_call(ALL, slot_of, w, g, s.f, s.q, s.kv, s.kvp), None)
    b = b._replace(dkv=add_low(b.near, to_peer(b.far)))
    return rows_gradient(b, b.dq, b.dkv, w), b


def cut(x, which, size):
    return lax.slice_in_dim(x, which * size, (which + 1) * size, axis=1)


def on_device(
    tokens,
    grad_out,
    attention_in,
    attention_bias,
    attention_out,
    up_weight,
    up_bias,
    down_weight,
    norm_gains,
    layer_biases,
    block_counts,
    lengths,
    head_shifts,
):
    dp_size = lax.axis_size("dp")
    first = lax.axis_index("section") == 0
    width = tokens.shape[2]
    quarter = tokens.shape[1]
    half = attention_in.shape[3]
    hidden = up_weight.shape[2]

    crossed = lax.ppermute(jnp.where(first, grad_out[0], tokens[0]), "section", SWAP)
    from_rows = lambda x, s: jnp.concatenate([tokens[s], x], axis=0)
    cot_rows = lambda x, s: jnp.concatenate([x, grad_out[s]], axis=0)
    tok0, cot0 = from_rows(crossed, 0), cot_rows(crossed, 0)
    win, win_far = attention_in[0], to_peer(attention_in[0])
    ab, ab_far = attention_bias[0], to_peer(attention_bias)[0]
    bv = jnp.concatenate([ab[1], ab_far[1]])
    w = Layer(
        q=jnp.concatenate([win[:, 0], win_far[:, 0]], axis=1),
        kv=jnp.concatenate([win[:, 1], win_far[:, 1], win[:, 2], win_far[:, 2]], axis=1),
        bq=jnp.concatenate([ab[0], ab_far[0]]),
        bkv=jnp.concatenate([jnp.zeros_like(bv), bv]),
        out=attention_out[0],
        up=up_weight[0],
        down=down_weight[0],
        out_far=to_peer(attention_out[0]),
        up_far=to_peer(up_weight[0]),
        down_far=to_peer(down_weight[0]),
        bup_own=up_bias,
        bup_far=to_peer(up_bias),
        ng=norm_gains[0],
        lb=layer_biases[0],
        counts=block_counts,
        lengths=lengths,
        shift_own=head_shifts,
        shift_far=to_peer(head_shifts),
    )
    slot_one = lambda s: 0
    slot_a = lambda s: 1 - s
    slot_b = lambda s: s

    out1, _ = forward_tick(False, slot_one, tok0, w)
    tok1 = from_rows(last_section(tokens[1]), 1)
    out2, saved2 = forward_tick(True, slot_a, jnp.where(first, tok1, next_section(out1)), w)
    away2 = next_section(jnp.concatenate([out2, grad_out[1]], axis=0))
    g3, b3 = backward_tick(slot_a, cot0, saved2, w)
    away2, _ = tied(away2, b3.d2_low)
    away2, rows1 = away2[: 2 * quarter], away2[2 * quarter :]
    cot1 = cot_rows(rows1, 1)
    out4, saved4 = forward_tick(True, slot_b, jnp.where(first, tok0, away2), w)
    (away3,) = tied(last_section(g3), unread=(out4,))
    g5, b5 = backward_tick(slot_b, jnp.where(first, away3, cot1), saved4, w)

    early = gradient_call(saved4, b5)
    g6_in = jnp.where(first, last_section(g5), cot0)

    f6 = saved2.f
    d2_low = norm_back(g6_in.astype(F32), f6.n2.astype(F32), f6.inv2[:, :1], w.ng[1]).astype(BF)
    down_far = half_gradient_call(d2_low, f6.act, d2_low, early[0], 1, True)
    down_own = half_gradient_call(down_far, f6.act, d2_low, early[0], 0, True)
    down = Sum(add_low(down_own, to_peer(down_far)), dp_size)
    r6 = backward_call(ROWS, slot_a, w, g6_in, f6, None, None, None, None, (down.sent,), early[1])
    b6 = Back(*r6[:5], None, None, None, None)
    d_mixed, up_own, up_far = r6[5:]
    (up_far,) = step_sums([down], up_far)
    up_in = to_peer(up_far)
    up = Sum(add_low(up_own, up_in), dp_size)
    dq, near, far = backward_call(
        HEADS, slot_a, w, None, f6, saved2.q, saved2.kv, saved2.kvp, d_mixed, (down.sent, up.sent)
    )
    dq, near, far = step_sums([down, up], dq, near, far)
    b6 = b6._replace(dq=dq, dkv=add_low(near, to_peer(far)))
    out_own, out_far, in_own, in_far, small_own, small_far = last_gradient_call(up.sent, saved2, b6, early, b5)
    out_far, in_far, small_far, tick = step_sums([down, up], out_far, in_far, small_far, b6.bias_sums)
    inner = Sum(add_low(in_own, to_peer(in_far)), dp_size)
    small = small_own + to_peer(small_far)
    out_g = jnp.concatenate(
        [add_low(out_own, to_peer(out_far)), small.astype(BF), jnp.zeros((16, width), BF)], axis=0
    )
    last = Sum(out_g, dp_size)
    (tick,) = step_sums([inner], tick, unread=(last.sent,))
    (tick,) = step_sums([down, up, last], tick)
    (tick,) = step_sums([inner], tick)
    (tick,) = step_sums([last], tick)
    (tick,) = step_sums([up, inner], tick)
    (tick,) = step_sums([last], tick)
    (tick,) = step_sums([down, inner], tick)
    tick, dq, dkv = step_sums([last], tick, b6.dq, b6.dkv)
    quarters = jnp.concatenate([out2[:quarter], out4[:quarter]], axis=0)
    tick, quarters = tied(tick, quarters, unread=(last.sent,))
    layer_far = last_section(quarters)
    g6 = rows_gradient(b6, dq, dkv, w)
    tokens_far = next_section(jnp.concatenate([g5[quarter:], g6[quarter:]], axis=0))
    while up.whole is None or down.whole is None:
        (tick,) = step_sums([up, down], tick)
    pair = lambda x, y: jnp.stack([x, y])
    layer_out = jnp.where(first, layer_far.reshape(tokens.shape), pair(out2[quarter:], out4[quarter:]))
    grad_tokens = jnp.where(first, pair(g5[:quarter], g6[:quarter]), tokens_far.reshape(tokens.shape))
    down_s = down.whole.astype(F32)
    up_s = up.whole.astype(F32)
    while inner.whole is None or last.whole is None:
        tick, down_s, up_s, layer_out, grad_tokens = step_sums(
            [inner, last], tick, down_s, up_s, layer_out, grad_tokens
        )
    out_s = last.whole
    in_s = jnp.concatenate([inner.whole, out_s[:half, :half], out_s[:half, half:]], axis=0).astype(F32)
    small = out_s[2 * half : 2 * half + 16].astype(F32)
    out_s = out_s[half : 2 * half].astype(F32)

    return (
        layer_out,
        grad_tokens,
        in_s.reshape(3, width, half).transpose(1, 0, 2)[None],
        small[8].reshape(1, 2, half),
        out_s[None],
        up_s[None],
        small[6:8].reshape(1, hidden),
        down_s[None],
        small[:2][None],
        small[2:6][None],
    )


def solution(mesh):
    tokens = P("dp", ("section", "mp"), None)
    weights = (
        P("section", None, None, "mp"),
        P("section", None, "mp"),
        P("section", "mp", None),
        P("section", None, "mp"),
        P("section", "mp"),
        P("section", "mp", None),
        P("section", None, None),
        P("section", None, None),
    )
    return jax.shard_map(
        on_device,
        mesh=mesh,
        in_specs=(tokens, tokens) + weights + (P("dp"), P("dp"), P("section", "mp")),
        out_specs=(tokens, tokens) + weights,
        check_vma=False,
    )
```
